32 devices in a mesh: dp: 4 (over y, x), expert: 8 (over z, core).
Axes of the slice: x: 2, y: 2, z: 4, core: 2. Of those that a mesh axis runs over, the one named last changes fastest.
Arguments:
- tokens: bfloat16 [16, 1024, 768], P('expert', 'dp'), may hold values from -6 to 6
- cotangent: bfloat16 [16, 1024, 768], P('expert', 'dp'), may hold values from -6 to 6
- qkv_weight: bfloat16 [3, 768, 768], P(None, ('dp', 'expert')), may hold values from -0.21875 to 0.21875
- out_weight: bfloat16 [768, 768], P(('dp', 'expert')), may hold values from -1.75 to 1.75
- norm_gains: bfloat16 [2, 768], P(None, ('dp', 'expert')), may hold values from 0.5 to 1.5
- rel_bias: float32 [32, 12], replicated, may hold values from -4 to 4
- router_weight: bfloat16 [768, 16], P(('dp', 'expert')), may hold values from -0.21875 to 0.21875
- w_in: bfloat16 [16, 768, 3072], P('expert', None, 'dp'), may hold values from -0.21875 to 0.21875
- w_out: bfloat16 [16, 3072, 768], P('expert', 'dp'), may hold values from -0.109375 to 0.109375
- doc_lengths: int32 [16, 4], P('expert'), may hold values from 1 to 896, 1024 in all within a row
- bucket_ids: int32 [1024], replicated, may hold values from 0 to 31, never falling along the last dimension, each value on 1 to 256 neighbouring positions
- routes: int32 [16, 1024, 2], P('expert', 'dp'), may hold values from 0 to 15, all different within a row; in each aligned block of 256 rows (0 to 255, 256 to 511, ..., all dimensions but the last counted through in order) at most 64 rows name the same one
Outputs:
- block_out: bfloat16 [16, 1024, 768], P('expert', 'dp')
- tokens_grad: float32 [16, 1024, 768], P('expert', 'dp')
- qkv_grad: float32 [3, 768, 768], P(None, ('dp', 'expert'))
- out_proj_grad: float32 [768, 768], P(('dp', 'expert'))
- gains_grad: float32 [2, 768], P(None, ('dp', 'expert'))
- rel_bias_grad: float32 [32, 12], replicated
- router_grad: float32 [768, 16], P(('dp', 'expert'))
- w_in_grad: float32 [16, 768, 3072], P('expert', None, 'dp')
- w_out_grad: float32 [16, 3072, 768], P('expert', 'dp')
The draws below stay inside these ranges and needn't reach their ends.
Inputs may be any that keep to these rules, and one draw needn't show every extreme that they name: `doc_lengths`: the lengths of each sequence sum to 1024, and one of them is 896. `bucket_ids`: never falls as the distance grows; every bucket is used. `routes`: a token names two different experts; the 256 positions of one sequence that one index of dp holds name one expert at most 64 times, and exactly 64 times in some of these blocks.
All inputs are finite; a program needn't handle non-finite values.
Results may differ from the reference program's by a relative error of at most 0.02.
Values may be sent and summed in bfloat16 or wider, within the bound.
No kernel may reach another device: no remote copies, remote signals or barrier semaphores. Data moves between devices by JAX's collectives and lax.ppermute only.
A program may use at most 256 MiB of HBM per device.

```python
import math
import jax
import jax.numpy as jnp
import numpy as np
from jax import lax

D = 768
H = 12
DH = 64
FF = 3072
NB = 32
TOP = 2
NDOC = 4
SPAN = 256
HD = 768
E = 16
BATCH = 16
L = 1024
M = 64
N_DP = 4


def level_of(key, shape, shards, smallest, high):
    level, own = 1.0, jax.random.fold_in(key, 6)
    for position, blocks in shards:
        steps = jnp.exp(jax.random.uniform(jax.random.fold_in(own, position), (blocks,), jnp.float32, smallest / len(shards), high / len(shards)))
        level = level * jnp.repeat(steps, shape[position] // blocks).reshape([-1 if axis == position else 1 for axis in range(len(shape))])
    return level


def split_up(count, total, limit, slope):
    portions = [(1 << 20) // math.isqrt(grade ** slope) + 1 for grade in range(2, count + 1)]
    spare, given = total - limit - (count - 1), [1] * (count - 1)
    while spare > 0:
        movable = [i for i in range(count - 1) if given[i] < limit]
        mass, left = sum([portions[i] for i in movable]), spare
        for i in movable:
            addition = min(limit - given[i], max(1, left * portions[i] // mass), spare)
            given[i] = given[i] + addition
            spare = spare - addition
    return np.array([limit] + given)


def uneven_parts(key, number_of, total, bound, lean):
    if number_of == 2:
        one = jax.random.randint(key, (), max(1, total - bound), min(bound, total - 1) + 1)
        return jnp.stack([one, total - one])
    tallies = jnp.asarray(split_up(number_of, total, bound, lean), jnp.int32)
    couples = (number_of - 1) // 2
    source_of, taker = tallies[1:1 + 2 * couples:2], tallies[2:2 + 2 * couples:2]
    margin = jnp.minimum(source_of - 1, bound - taker)
    moved = jax.random.randint(jax.random.fold_in(key, 1), (couples,), 0, 1 << 20) % (margin + 1)
    tallies = tallies.at[1:1 + 2 * couples:2].set(source_of - moved).at[2:2 + 2 * couples:2].set(taker + moved)
    return tallies[jax.random.permutation(jax.random.fold_in(key, 2), number_of)]


def shared_out(key, own, number, rows, number_of, top, bound, lean):
    order = jax.random.permutation(key, number_of)
    heavy_load, ordinary = load_shares(number_of, rows * top, bound, lean, True), load_shares(number_of, rows * top, bound, lean, False)
    places = jnp.arange(number_of)

    def named(sizes, offset_by):
        used = int((sizes > 0).sum())
        fixed = max(1, used // 4)
        moved = fixed + (places - fixed + offset_by * (used - fixed)) % max(1, number_of - fixed)
        return jnp.zeros((number_of,), jnp.int32).at[order[jnp.where(places < fixed, places, moved)]].set(jnp.asarray(sizes, jnp.int32))

    sizes = jnp.where(number % 4 == 0, named(heavy_load, number // 4), named(ordinary, number - number // 4 - 1))
    mixed = jax.random.permutation(jax.random.fold_in(own, 3), number_of)
    giver, receiver = mixed[0:number_of // 2 * 2:2], mixed[1:number_of // 2 * 2:2]
    slack = jnp.minimum(sizes[giver] - 1, bound - sizes[receiver]) // 2
    slack = jnp.where((giver == order[0]) | (receiver == order[0]) | (sizes[receiver] == 0), 0, jnp.maximum(slack, 0))
    moved = jax.random.randint(jax.random.fold_in(own, 4), (number_of // 2,), 0, 1 << 20) % (slack + 1)
    sizes = sizes.at[giver].add(-moved).at[receiver].add(moved)
    members = jnp.searchsorted(jnp.cumsum(sizes), jnp.arange(rows * top), side="right").astype(jnp.int32)
    grid = members.reshape(top, rows).T
    grid = grid[jax.random.permutation(jax.random.fold_in(own, 1), rows)]
    offset_by = jax.random.randint(jax.random.fold_in(own, 2), (rows, 1), 0, top)
    return jnp.take_along_axis(grid, (jnp.arange(top)[None, :] + offset_by) % top, axis=1)


def load_shares(count, total, limit, slope, full):
    loads = [(1 << 20) // math.isqrt(standing ** slope) + 1 for standing in range(1, count + 1)]
    largest = limit if full else min(limit, max(-(-total // count), total * loads[0] // sum(loads)))
    least = 1 if total - largest >= count - 1 else 0
    holding, rest = [largest] + [least] * (count - 1), total - largest - least * (count - 1)
    while rest > 0:
        movable = [i for i in range(1, count) if holding[i] < largest] or [i for i in range(1, count) if holding[i] < limit]
        pool, budget = sum([loads[i] for i in movable]), rest
        for i in movable:
            extra = min(limit - holding[i], max(1, budget * loads[i] // pool), rest)
            holding[i] = holding[i] + extra
            rest = rest - extra
    return np.array(holding)


def bell_draw(key, extent, width, most, split=(), kind=jnp.bfloat16):
    values = jax.random.normal(key, extent, jnp.float32) * width
    if len(split) > 0:
        values = level_of(key, extent, split, -0.22, 0.18) * values
    return jnp.clip(values, min=-most, max=most).astype(kind)


def setup_inputs(seed: int = 0) -> dict:
    seeds = jax.random.split(jax.random.key(seed), 13)
    tokens = bell_draw(seeds[0], (BATCH, L, D), 1.0, 6.0, ((0, 8), (1, 4)))
    cotangent = bell_draw(seeds[1], (BATCH, L, D), 1.0, 6.0, ((0, 8), (1, 4)))
    qkv_weight = bell_draw(seeds[2], (3, D, HD), D ** -0.5, 0.21875, ((1, 32),))
    out_weight = bell_draw(seeds[3], (HD, D), (D // 64) ** -0.5, 1.75, ((0, 32),))
    norm_gains = jnp.clip(1.0 + 0.1 * jax.random.normal(seeds[4], (2, D), jnp.float32), 0.5, 1.5).astype(jnp.bfloat16)
    rel_bias = bell_draw(seeds[5], (NB, H), 1.0, 4.0, (), jnp.float32)
    router_weight = bell_draw(seeds[6], (D, E), D ** -0.5, 0.21875, ((0, 32),))
    w_in = bell_draw(seeds[7], (E, D, FF), D ** -0.5, 0.21875, ((0, 8), (2, 4)))
    w_out = bell_draw(seeds[8], (E, FF, D), FF ** -0.5, 0.109375, ((0, 8), (1, 4)))
    doc_lengths = jax.vmap(lambda own: uneven_parts(own, NDOC, L, L - SPAN // 2, 2))(jax.random.split(seeds[9], BATCH)).reshape((BATCH, NDOC)).astype(jnp.int32)
    bucket_ids = jnp.searchsorted(jnp.cumsum(uneven_parts(seeds[10], NB, L, L // 4, 0)), jnp.arange(L), side="right").astype(jnp.int32)
    routes_keys = jax.random.split(jax.random.fold_in(seeds[11], 1), BATCH * L // SPAN)
    routes_turns = jax.random.permutation(jax.random.fold_in(seeds[11], 3), BATCH * L // SPAN)
    routes = jax.vmap(lambda own, number: shared_out(jax.random.fold_in(seeds[11], 2), own, number, SPAN, E, TOP, M, 1))(routes_keys, routes_turns).reshape((BATCH, L, TOP))
    return dict(tokens=tokens, cotangent=cotangent, qkv_weight=qkv_weight, out_weight=out_weight, norm_gains=norm_gains, rel_bias=rel_bias, router_weight=router_weight, w_in=w_in, w_out=w_out, doc_lengths=doc_lengths, bucket_ids=bucket_ids, routes=routes)


@jax.custom_vjp
def low(v):
    return lax.optimization_barrier(v.astype(jnp.bfloat16)).astype(jnp.float32)

@jax.custom_vjp
def low_back(v):
    return v

def low_keep(v):
    return (low(v), None)

def low_pass(kept, grad):
    return (grad,)

def back_keep(v):
    return (v, None)

def back_low(kept, grad):
    return (low(grad),)
low.defvjp(low_keep, low_pass)
low_back.defvjp(back_keep, back_low)
EPS = 1e-06
SCALE = 0.125
NEG = -1e+30
HIGHEST = lax.Precision.HIGHEST

def rms_scale(values, gain):
    inverse = lax.rsqrt(lax.optimization_barrier(jnp.mean(values * values, axis=-1, keepdims=True)) + EPS)
    return values * inverse * gain

def softmax_last(scores):
    highest = lax.optimization_barrier(jnp.max(scores, axis=-1, keepdims=True))
    raised = jnp.exp(scores - highest)
    return raised / lax.optimization_barrier(jnp.sum(raised, axis=-1, keepdims=True))

def route_tables(routes):
    n_pairs = BATCH * L * TOP
    pair_expert = routes.reshape(n_pairs).astype(jnp.int32)
    ordering = jnp.argsort(pair_expert, stable=True).astype(jnp.int32)
    sorted_expert = pair_expert[ordering]
    matches = (pair_expert[:, None] == jnp.arange(E, dtype=jnp.int32)[None, :]).astype(jnp.int32)
    counts = lax.optimization_barrier(jnp.sum(matches, axis=0)).astype(jnp.int32)
    starts = (jnp.cumsum(counts).astype(jnp.int32) - counts).astype(jnp.int32)
    ranking = jnp.arange(n_pairs, dtype=jnp.int32) - starts[sorted_expert]
    capacity = BATCH * N_DP * M
    placed = (sorted_expert * capacity + ranking).astype(jnp.int32)
    slot_table = jnp.full((E * capacity,), n_pairs, jnp.int32).at[placed].set(ordering).reshape(E, capacity)
    slot_of_pair = jnp.zeros((n_pairs,), jnp.int32).at[ordering].set(placed)
    return (slot_table, slot_of_pair)

def layer_forward(tokens, qkv_weight, out_weight, norm_gains, rel_bias, router_weight, w_in, w_out, doc_lengths, bucket_ids, routes, slot_table, slot_of_pair):
    n_rows = BATCH * L
    inputs = tokens.reshape(n_rows, D)
    normed1 = low(rms_scale(inputs, norm_gains[0]))
    projected = jnp.einsum('td,cde->cte', normed1, qkv_weight, precision=HIGHEST)
    projected = low(low_back(projected)).reshape(3, BATCH, L, H, DH)
    bucket_hits = (bucket_ids[:, None] == jnp.arange(NB, dtype=jnp.int32)[None, :]).astype(jnp.float32)
    dist_bias = jnp.dot(rel_bias.T, bucket_hits.T, precision=HIGHEST)
    places = jnp.arange(L, dtype=jnp.int32)
    spacing = places[:, None] - places[None, :]
    biases = jnp.take(dist_bias, jnp.clip(spacing, 0, L - 1), axis=1)
    doc_ends = jnp.cumsum(doc_lengths, axis=-1).astype(jnp.int32)
    documents = lax.optimization_barrier(jnp.sum((places[None, :, None] >= doc_ends[:, None, :]).astype(jnp.int32), axis=-1)).astype(jnp.int32)

    def one_sequence(operands):
        queries, key_rows, values, document = operands
        scores = jnp.einsum('qhd,khd->hqk', queries, key_rows, precision=HIGHEST) * SCALE + biases
        scores = low_back(scores)
        allowed = jnp.logical_and(spacing >= 0, document[:, None] == document[None, :])
        scores = jnp.where(allowed[None], scores, NEG)
        probs = softmax_last(scores)
        return jnp.einsum('hqk,khd->qhd', low(probs), values, precision=HIGHEST)
    attended = lax.map(jax.checkpoint(one_sequence), (projected[0], projected[1], projected[2], documents))
    attended = low(low_back(attended.reshape(n_rows, HD)))
    branch = low_back(jnp.dot(attended, out_weight, precision=HIGHEST))
    resid = inputs + branch
    normed2 = low(rms_scale(resid, norm_gains[1]))
    logits = low_back(jnp.dot(normed2, router_weight, precision=HIGHEST))
    route_pairs = routes.reshape(n_rows, TOP)
    gates = softmax_last(jnp.take_along_axis(logits, route_pairs, axis=1))
    pair_rows = low_back(jnp.repeat(normed2, TOP, axis=0))
    padded = jnp.concatenate([pair_rows, jnp.zeros((1, D), jnp.float32)], axis=0)

    def one_expert(operands):
        indices, weight_in, weight_out = operands
        chosen = padded[indices]
        pre_act = low_back(jnp.dot(chosen, weight_in, precision=HIGHEST))
        hidden = low(jax.nn.gelu(pre_act))
        return low(low_back(jnp.dot(hidden, weight_out, precision=HIGHEST)))
    expert_rows = lax.map(jax.checkpoint(one_expert), (slot_table, w_in, w_out))
    capacity = slot_table.shape[1]
    pair_out = expert_rows.reshape(E * capacity, D)[slot_of_pair].reshape(n_rows, TOP, D)
    mixed = lax.optimization_barrier(jnp.sum(gates[:, :, None] * pair_out, axis=1))
    return (resid + mixed).reshape(BATCH, L, D)

def reference(tokens, cotangent, qkv_weight, out_weight, norm_gains, rel_bias, router_weight, w_in, w_out, doc_lengths, bucket_ids, routes):
    slot_table, slot_of_pair = route_tables(routes)

    def forward(tok_values, qkv_values, out_values, gain_values, bias_values, router_values, in_values, down_values):
        return layer_forward(tok_values, qkv_values, out_values, gain_values, bias_values, router_values, in_values, down_values, doc_lengths, bucket_ids, routes, slot_table, slot_of_pair)
    floats = tuple((array.astype(jnp.float32) for array in (tokens, qkv_weight, out_weight, norm_gains, rel_bias, router_weight, w_in, w_out)))
    block_out, pullback = jax.vjp(forward, *floats)
    grads = pullback(cotangent.astype(jnp.float32))
    return (block_out.astype(jnp.bfloat16), grads[0], grads[1], grads[2], grads[3], grads[4], grads[5], grads[6], grads[7])
```

```python
import functools

import jax
import jax.numpy as jnp
from jax import lax
from jax.experimental import pallas as pl
from jax.experimental.pallas import tpu as pltpu
from jax.sharding import PartitionSpec as P

EPS = 1e-06
SCALE = 0.125
NEG = -1e30
VMEM_LIMIT = 48 * 1024 * 1024


def norm_forward(values, gain):
    inverse = lax.rsqrt(jnp.mean(values * values, axis=-1, keepdims=True) + EPS)
    return (values * inverse * gain, inverse)


def norm_backward(values, inverse, gain, grad_in):
    scaled = grad_in * gain
    gain_grad = jnp.sum(grad_in * values * inverse, axis=0)
    cubed = inverse * inverse * inverse
    value_grad = inverse * scaled - values * cubed * jnp.mean(
        scaled * values, axis=-1, keepdims=True
    )
    return (value_grad, gain_grad)


def spread_rows(base, span):
    grown = base
    while grown.shape[0] < span:
        grown = jnp.concatenate([grown, pltpu.roll(grown, grown.shape[0], 1)], axis=0)
    return grown[:, span:]


def fold_rows(block, span):
    wide = jnp.concatenate([jnp.zeros_like(block), block], axis=1)
    while wide.shape[0] > 8:
        half = wide.shape[0] // 2
        wide = wide[:half] + pltpu.roll(wide[half:], 2 * span - half, 1)
    return wide


def attention_forward_kernel(
    n_piece, span, head_dim, q_ref, k_ref, v_ref, base_ref, start_ref, out_ref, lse_ref, bias_ref
):
    @pl.when(pl.program_id(1) == 0)
    def fill_bias():
        for head in range(2):
            for piece in range(n_piece):
                bias_ref[head, piece] = spread_rows(base_ref[0, head, piece], span)

    start = start_ref[0]
    queries = q_ref[0]
    lane_head = lax.broadcasted_iota(jnp.int32, queries.shape, 1) // head_dim
    key_row = lax.broadcasted_iota(jnp.int32, (span, span), 0)
    values_t = [v_ref[0, pl.ds(piece * span, span), :].T for piece in range(n_piece)]
    outs = []
    for head in range(2):
        masked = jnp.where(lane_head == head, queries, jnp.zeros_like(queries))
        scores = []
        highest = None
        for piece in range(n_piece):
            keys = k_ref[0, pl.ds(piece * span, span), :]
            block = lax.dot_general(
                keys, masked, (((1,), (1,)), ((), ())), preferred_element_type=jnp.float32
            )
            block = block + bias_ref[head, piece]
            block = jnp.where(key_row + piece * span >= start, block, NEG)
            scores.append(block)
            top = jnp.max(block, axis=0, keepdims=True)
            highest = top if highest is None else jnp.maximum(highest, top)
        total = jnp.zeros_like(highest)
        result = jnp.zeros((head_dim, span), jnp.float32)
        for piece in range(n_piece):
            weights = jnp.exp(scores[piece] - highest)
            total = total + jnp.sum(weights, axis=0, keepdims=True)
            result = result + jnp.dot(
                values_t[piece][head * head_dim : (head + 1) * head_dim],
                weights.astype(jnp.bfloat16),
                preferred_element_type=jnp.float32,
            )
        outs.append(result / total)
        lse_ref[0, 0, head : head + 1, :] = highest + jnp.log(total)
    out_ref[0] = jnp.concatenate(outs, axis=0).T.astype(out_ref.dtype)


def attention_backward_kernel(
    n_piece,
    span,
    head_dim,
    q_ref,
    k_ref,
    v_ref,
    out_ref,
    grad_ref,
    base_ref,
    start_ref,
    lse_ref,
    dq_ref,
    dk_ref,
    dv_ref,
    dist_ref,
    bias_ref,
    sum_ref,
):
    batch = pl.program_id(1)

    @pl.when(batch == 0)
    def fill_bias():
        for head in range(2):
            for piece in range(n_piece):
                bias_ref[head, piece] = spread_rows(base_ref[0, head, piece], span)
                sum_ref[head, piece] = jnp.zeros((span, span), jnp.float32)

    start = start_ref[0]
    queries = q_ref[0]
    grads = grad_ref[0]
    product = grads.astype(jnp.float32) * out_ref[0].astype(jnp.float32)
    product_hi = product.astype(jnp.bfloat16)
    product_lo = (product - product_hi.astype(jnp.float32)).astype(jnp.bfloat16)
    lane_head = lax.broadcasted_iota(jnp.int32, queries.shape, 1) // head_dim
    key_row = lax.broadcasted_iota(jnp.int32, (span, span), 0)
    picker = (
        lax.broadcasted_iota(jnp.int32, (8, 2 * head_dim), 1) // head_dim
        == lax.broadcasted_iota(jnp.int32, (8, 2 * head_dim), 0)
    ).astype(jnp.bfloat16)
    rows_by_rows = (((1,), (1,)), ((), ()))
    correction = lax.dot_general(
        picker, product_hi, rows_by_rows, preferred_element_type=jnp.float32
    ) + lax.dot_general(picker, product_lo, rows_by_rows, preferred_element_type=jnp.float32)
    zero = jnp.zeros_like(queries)
    head_queries = [jnp.where(lane_head == head, queries, zero) for head in range(2)]
    head_grads = [jnp.where(lane_head == head, grads, zero) for head in range(2)]
    query_grads = [jnp.zeros((head_dim, span), jnp.float32) for _ in range(2)]
    for piece in range(n_piece):
        rows = pl.ds(piece * span, span)
        keys = k_ref[0, rows, :]
        values = v_ref[0, rows, :]
        keys_t = keys.T
        allowed = key_row + piece * span >= start
        key_grad = jnp.zeros((span, 2 * head_dim), jnp.float32)
        value_grad = jnp.zeros((span, 2 * head_dim), jnp.float32)
        for head in range(2):
            scores = lax.dot_general(
                keys, head_queries[head], rows_by_rows, preferred_element_type=jnp.float32
            )
            scores = jnp.where(allowed, scores + bias_ref[head, piece], NEG)
            probs = jnp.exp(scores - lse_ref[0, 0, head : head + 1, :])
            prob_grad = lax.dot_general(
                values, head_grads[head], rows_by_rows, preferred_element_type=jnp.float32
            )
            score_grad = (probs * (prob_grad - correction[head : head + 1, :])).astype(jnp.bfloat16)
            sum_ref[head, piece] += score_grad.astype(jnp.float32)
            value_grad = value_grad + jnp.dot(
                probs.astype(jnp.bfloat16), head_grads[head], preferred_element_type=jnp.float32
            )
            key_grad = key_grad + jnp.dot(
                score_grad, head_queries[head], preferred_element_type=jnp.float32
            )
            query_grads[head] = query_grads[head] + jnp.dot(
                keys_t[head * head_dim : (head + 1) * head_dim],
                score_grad,
                preferred_element_type=jnp.float32,
            )
        dk_ref[0, rows, :] = key_grad.astype(jnp.bfloat16)
        dv_ref[0, rows, :] = value_grad.astype(jnp.bfloat16)
    dq_ref[0] = (jnp.concatenate(query_grads, axis=0) * SCALE).T.astype(jnp.bfloat16)

    @pl.when(batch == pl.num_programs(1) - 1)
    def fold_distances():
        for head in range(2):
            for piece in range(n_piece):
                dist_ref[0, head, piece] = fold_rows(sum_ref[head, piece], span)


def attention_specs(n_piece, span, pair):
    n_keys = n_piece * span
    rows = pl.BlockSpec((1, span, pair), lambda h, b: (b, 0, h))
    keys = pl.BlockSpec((1, n_keys, pair), lambda h, b: (b, 0, h))
    base = pl.BlockSpec((1, 2, n_piece, 8, 2 * span), lambda h, b: (h, 0, 0, 0, 0))
    start = pl.BlockSpec((1, 1, span), lambda h, b: (b, 0, 0))
    lse = pl.BlockSpec((1, 1, 2, span), lambda h, b: (h, b, 0, 0))
    return rows, keys, base, start, lse


def attention_forward(queries, keys, values, base, start, n_heads):
    n_batch, span, inner = queries.shape
    n_piece = keys.shape[1] // span
    head_dim = inner // n_heads
    n_pairs = n_heads // 2
    rows, key_rows, base_spec, start_spec, lse_spec = attention_specs(n_piece, span, 2 * head_dim)
    flops = 4 * n_batch * n_heads * span * n_piece * span * head_dim
    return pl.pallas_call(
        functools.partial(attention_forward_kernel, n_piece, span, head_dim),
        grid=(n_pairs, n_batch),
        in_specs=[rows, key_rows, key_rows, base_spec, start_spec],
        out_specs=[rows, lse_spec],
        out_shape=[
            jax.ShapeDtypeStruct(queries.shape, jnp.bfloat16),
            jax.ShapeDtypeStruct((n_pairs, n_batch, 2, span), jnp.float32),
        ],
        scratch_shapes=[pltpu.VMEM((2, n_piece, span, span), jnp.float32)],
        compiler_params=pltpu.CompilerParams(vmem_limit_bytes=VMEM_LIMIT),
        cost_estimate=pl.CostEstimate(
            flops=4 * flops, bytes_accessed=8 * keys.size, transcendentals=0
        ),
        name="attention_forward",
    )(queries, keys, values, base, start)


def attention_backward(queries, keys, values, attended, grads, base, start, lse, n_heads):
    n_batch, span, inner = queries.shape
    n_piece = keys.shape[1] // span
    head_dim = inner // n_heads
    n_pairs = n_heads // 2
    rows, key_rows, base_spec, start_spec, lse_spec = attention_specs(n_piece, span, 2 * head_dim)
    flops = 10 * n_batch * n_heads * span * n_piece * span * head_dim
    return pl.pallas_call(
        functools.partial(attention_backward_kernel, n_piece, span, head_dim),
        grid=(n_pairs, n_batch),
        in_specs=[rows, key_rows, key_rows, rows, rows, base_spec, start_spec, lse_spec],
        out_specs=[rows, key_rows, key_rows, base_spec],
        out_shape=[
            jax.ShapeDtypeStruct(queries.shape, jnp.bfloat16),
            jax.ShapeDtypeStruct(keys.shape, jnp.bfloat16),
            jax.ShapeDtypeStruct(keys.shape, jnp.bfloat16),
            jax.ShapeDtypeStruct((n_pairs, 2, n_piece, 8, 2 * span), jnp.float32),
        ],
        scratch_shapes=[
            pltpu.VMEM((2, n_piece, span, span), jnp.float32),
            pltpu.VMEM((2, n_piece, span, span), jnp.float32),
        ],
        compiler_params=pltpu.CompilerParams(vmem_limit_bytes=VMEM_LIMIT),
        cost_estimate=pl.CostEstimate(
            flops=4 * flops, bytes_accessed=12 * keys.size, transcendentals=0
        ),
        name="attention_backward",
    )(queries, keys, values, attended, grads, base, start, lse)


def bias_base(rel_bias, bucket_ids, offset, span):
    length = bucket_ids.shape[0]
    n_piece = length // span
    hits = (bucket_ids[None, :] == jnp.arange(rel_bias.shape[0], dtype=jnp.int32)[:, None]).astype(
        jnp.float32
    )
    table = jnp.dot(rel_bias.T, hits, precision=lax.Precision.HIGHEST)
    padded = jnp.pad(table, ((0, 0), (length + span + 8, span)), constant_values=NEG)
    rows = []
    for s in range(8):
        window = lax.dynamic_slice_in_dim(padded, offset + 8 - s + span, length + span, 1)
        rows.append(
            jnp.stack(
                [window[:, length - (p + 1) * span : length - (p + 1) * span + 2 * span] for p in range(n_piece)],
                axis=1,
            )
        )
    base = jnp.stack(rows, axis=2)
    return base.reshape(base.shape[0] // 2, 2, n_piece, 8, 2 * span)


def bias_fold(dist, bucket_ids, offset, n_buckets):
    n_heads = dist.shape[0] * 2
    n_piece, span = dist.shape[2], dist.shape[4] // 2
    length = n_piece * span
    parts = dist.reshape(n_heads, n_piece, 8, 2 * span)
    sums = sum(
        jnp.concatenate([parts[:, :, s, s:], jnp.zeros((n_heads, n_piece, s), jnp.float32)], axis=-1)
        for s in range(8)
    )
    total = jnp.zeros((n_heads, length + span), jnp.float32)
    for p in range(n_piece):
        at = length - (p + 1) * span
        total = total.at[:, at : at + 2 * span].add(sums[:, p])
    padded = jnp.pad(total, ((0, 0), (0, length)))
    by_distance = lax.dynamic_slice_in_dim(padded, length - offset, length, 1)
    hits = (bucket_ids[:, None] == jnp.arange(n_buckets, dtype=jnp.int32)[None, :]).astype(jnp.float32)
    return jnp.dot(by_distance, hits, precision=lax.Precision.HIGHEST).T


def document_starts(doc_lengths, offset, span):
    ends = jnp.cumsum(doc_lengths, axis=-1)
    places = offset + jnp.arange(span, dtype=jnp.int32)
    begun = ends[:, None, :] <= places[None, :, None]
    return jnp.max(jnp.where(begun, ends[:, None, :], 0), axis=-1)[:, None, :]


def body(
    tokens,
    cotangent,
    qkv_weight,
    out_weight,
    norm_gains,
    rel_bias,
    router_weight,
    w_in,
    w_out,
    doc_lengths,
    bucket_ids,
    routes,
):
    n_batch, n_span, n_width = tokens.shape
    n_rows = n_batch * n_span
    n_buckets, n_heads = rel_bias.shape
    n_inner = qkv_weight.shape[2]
    head_dim = n_inner // n_heads
    length = n_span * lax.axis_size("dp")
    offset = lax.axis_index("dp") * n_span
    groups = lax.axis_size("expert")
    local_experts = w_in.shape[0]
    experts_all = local_experts * groups
    slot_bound = max(2, 2 * n_span * 2 // experts_all)
    n_slots = n_batch * slot_bound
    qkv_full, out_full, router_full, gains_full = (
        lax.all_gather(qkv_weight, ("dp", "expert"), axis=1, tiled=True),
        lax.all_gather(out_weight, ("dp", "expert"), axis=0, tiled=True),
        lax.all_gather(router_weight, ("dp", "expert"), axis=0, tiled=True),
        lax.all_gather(norm_gains, ("dp", "expert"), axis=1, tiled=True),
    )
    in_full, down_full = (
        lax.all_gather(w_in, "dp", axis=2, tiled=True),
        lax.all_gather(w_out, "dp", axis=1, tiled=True),
    )
    inputs = tokens.reshape(n_rows, n_width).astype(jnp.float32)
    normed1, inverse1 = norm_forward(inputs, gains_full[0].astype(jnp.float32))
    normed1_low = normed1.astype(jnp.bfloat16)
    projected = jnp.einsum(
        "td,cde->cte", normed1_low, qkv_full, preferred_element_type=jnp.float32
    ).astype(jnp.bfloat16)
    queries = (projected[0] * SCALE).reshape(n_batch, n_span, n_inner)
    key_rows = projected[1].reshape(n_batch, n_span, n_inner)
    value_rows = projected[2].reshape(n_batch, n_span, n_inner)
    base = bias_base(rel_bias, bucket_ids, offset, n_span)
    starts = document_starts(doc_lengths, offset, n_span)
    key_piece = lax.all_gather(key_rows, "dp", axis=1, tiled=True)
    value_piece = lax.all_gather(value_rows, "dp", axis=1, tiled=True)
    attended_rows, log_total = attention_forward(
        queries, key_piece, value_piece, base, starts, n_heads
    )
    attended = attended_rows.reshape(n_rows, n_inner)
    branch = jnp.dot(attended, out_full, preferred_element_type=jnp.float32)
    resid = inputs + branch
    normed2, inverse2 = norm_forward(resid, gains_full[1].astype(jnp.float32))
    normed2_low = normed2.astype(jnp.bfloat16)
    logits = jnp.dot(normed2_low, router_full, preferred_element_type=jnp.float32)
    route_pairs = routes.reshape(n_rows, 2)
    chosen = jnp.take_along_axis(logits, route_pairs, axis=1)
    chosen_exp = jnp.exp(chosen - jnp.max(chosen, axis=-1, keepdims=True))
    gates = chosen_exp / jnp.sum(chosen_exp, axis=-1, keepdims=True)
    pair_expert = routes.reshape(n_batch, n_span * 2)
    expert_range = jnp.arange(experts_all, dtype=jnp.int32)
    matches = (pair_expert[..., None] == expert_range).astype(jnp.int32)
    earlier = jnp.cumsum(matches, axis=1) - matches
    pair_rank = jnp.sum(earlier * matches, axis=-1)
    destination = (
        pair_expert * n_slots
        + jnp.arange(n_batch, dtype=jnp.int32)[:, None] * slot_bound
        + pair_rank
    ).reshape(-1)
    pair_source = jnp.repeat(normed2_low, 2, axis=0)
    outgoing = (
        jnp.zeros((experts_all * n_slots, n_width), jnp.bfloat16).at[destination].set(pair_source)
    )
    arrived = lax.all_to_all(outgoing, "expert", split_axis=0, concat_axis=0, tiled=True).reshape(
        groups, local_experts, n_slots, n_width
    )
    hidden_pre = jnp.einsum("sepd,edf->sepf", arrived, in_full, preferred_element_type=jnp.float32)
    hidden_low = jax.nn.gelu(hidden_pre).astype(jnp.bfloat16)
    produced = jnp.einsum(
        "sepf,efd->sepd", hidden_low, down_full, preferred_element_type=jnp.float32
    ).astype(jnp.bfloat16)
    returned = lax.all_to_all(
        produced.reshape(-1, n_width), "expert", split_axis=0, concat_axis=0, tiled=True
    )
    pair_out = returned[destination].astype(jnp.float32).reshape(n_rows, 2, n_width)
    mixed = jnp.sum(gates[:, :, None] * pair_out, axis=1)
    block_out = (resid + mixed).astype(jnp.bfloat16).reshape(n_batch, n_span, n_width)
    qkv_back, out_back, router_back, gains_back = (
        lax.all_gather(qkv_weight, ("dp", "expert"), axis=1, tiled=True),
        lax.all_gather(out_weight, ("dp", "expert"), axis=0, tiled=True),
        lax.all_gather(router_weight, ("dp", "expert"), axis=0, tiled=True),
        lax.all_gather(norm_gains, ("dp", "expert"), axis=1, tiled=True),
    )
    in_back, down_back = (
        lax.all_gather(w_in, "dp", axis=2, tiled=True),
        lax.all_gather(w_out, "dp", axis=1, tiled=True),
    )
    grad_out = cotangent.reshape(n_rows, n_width).astype(jnp.float32)
    gate_grad = jnp.sum(grad_out[:, None, :] * pair_out, axis=-1)
    chosen_grad = gates * (gate_grad - jnp.sum(gates * gate_grad, axis=-1, keepdims=True))
    route_hits = (route_pairs[:, :, None] == expert_range).astype(jnp.float32)
    logit_low = jnp.sum(route_hits * chosen_grad[:, :, None], axis=1).astype(jnp.bfloat16)
    pair_grad = (
        (gates[:, :, None] * grad_out[:, None, :]).astype(jnp.bfloat16).reshape(n_rows * 2, n_width)
    )
    outgoing_grad = (
        jnp.zeros((experts_all * n_slots, n_width), jnp.bfloat16).at[destination].set(pair_grad)
    )
    arrived_grad = lax.all_to_all(
        outgoing_grad, "expert", split_axis=0, concat_axis=0, tiled=True
    ).reshape(groups, local_experts, n_slots, n_width)
    hidden_grad = jnp.einsum(
        "sepd,efd->sepf", arrived_grad, down_back, preferred_element_type=jnp.float32
    )
    gelu_value, gelu_pull = jax.vjp(jax.nn.gelu, hidden_pre)
    pre_grad = gelu_pull(hidden_grad)[0].astype(jnp.bfloat16)
    down_grad = jnp.einsum(
        "sepf,sepd->efd", hidden_low, arrived_grad, preferred_element_type=jnp.float32
    )
    in_grad = jnp.einsum("sepd,sepf->edf", arrived, pre_grad, preferred_element_type=jnp.float32)
    input_grad = jnp.einsum(
        "sepf,edf->sepd", pre_grad, in_back, preferred_element_type=jnp.float32
    ).astype(jnp.bfloat16)
    sent_back = lax.all_to_all(
        input_grad.reshape(-1, n_width), "expert", split_axis=0, concat_axis=0, tiled=True
    )
    pair_input_grad = jnp.sum(
        sent_back[destination].astype(jnp.float32).reshape(n_rows, 2, n_width), axis=1
    )
    normed2_grad = pair_input_grad + jnp.dot(
        logit_low, router_back.T, preferred_element_type=jnp.float32
    )
    router_grad = jnp.dot(normed2_low.T, logit_low, preferred_element_type=jnp.float32)
    resid_norm_grad, gain2_grad = norm_backward(
        resid, inverse2, gains_back[1].astype(jnp.float32), normed2_grad
    )
    resid_grad = grad_out + resid_norm_grad
    branch_low = resid_grad.astype(jnp.bfloat16)
    out_proj_grad = jnp.dot(attended.T, branch_low, preferred_element_type=jnp.float32)
    attended_grad = jnp.dot(branch_low, out_back.T, preferred_element_type=jnp.float32).astype(
        jnp.bfloat16
    )
    query_grad, key_grad_all, value_grad_all, dist_grad = attention_backward(
        queries,
        key_piece,
        value_piece,
        attended_rows,
        attended_grad.reshape(n_batch, n_span, n_inner),
        base,
        starts,
        log_total,
        n_heads,
    )
    bias_grad = bias_fold(dist_grad, bucket_ids, offset, n_buckets)
    key_grad, value_grad = (
        lax.psum_scatter(
            key_grad_all, "dp", scatter_dimension=1, tiled=True
        ).astype(jnp.float32),
        lax.psum_scatter(
            value_grad_all, "dp", scatter_dimension=1, tiled=True
        ).astype(jnp.float32),
    )
    query_low = query_grad.reshape(n_rows, n_inner)
    projected_grad = jnp.stack(
        [
            query_low,
            key_grad.reshape(n_rows, n_inner).astype(jnp.bfloat16),
            value_grad.reshape(n_rows, n_inner).astype(jnp.bfloat16),
        ]
    )
    qkv_grad = jnp.einsum(
        "td,cte->cde", normed1_low, projected_grad, preferred_element_type=jnp.float32
    )
    normed1_grad = jnp.einsum(
        "cte,cde->td", projected_grad, qkv_back, preferred_element_type=jnp.float32
    )
    input_norm_grad, gain1_grad = norm_backward(
        inputs, inverse1, gains_back[0].astype(jnp.float32), normed1_grad
    )
    tokens_grad = (resid_grad + input_norm_grad).reshape(n_batch, n_span, n_width)
    gains_grad = jnp.stack([gain1_grad, gain2_grad])
    qkv_share, out_share, router_share, gains_share = (
        lax.psum_scatter(qkv_grad, ("dp", "expert"), scatter_dimension=1, tiled=True),
        lax.psum_scatter(out_proj_grad, ("dp", "expert"), scatter_dimension=0, tiled=True),
        lax.psum_scatter(router_grad, ("dp", "expert"), scatter_dimension=0, tiled=True),
        lax.psum_scatter(gains_grad, ("dp", "expert"), scatter_dimension=1, tiled=True),
    )
    in_share, down_share = (
        lax.psum_scatter(
            in_grad.astype(jnp.bfloat16), "dp", scatter_dimension=2, tiled=True
        ).astype(jnp.float32),
        lax.psum_scatter(
            down_grad.astype(jnp.bfloat16), "dp", scatter_dimension=1, tiled=True
        ).astype(jnp.float32),
    )
    rel_bias_grad = lax.psum(bias_grad, ("dp", "expert"))
    return (
        block_out,
        tokens_grad,
        qkv_share,
        out_share,
        gains_share,
        rel_bias_grad,
        router_share,
        in_share,
        down_share,
    )


def solution(mesh):
    return jax.shard_map(
        body,
        mesh=mesh,
        in_specs=(
            P("expert", "dp", None),
            P("expert", "dp", None),
            P(None, ("dp", "expert"), None),
            P(("dp", "expert"), None),
            P(None, ("dp", "expert")),
            P(),
            P(("dp", "expert"), None),
            P("expert", None, "dp"),
            P("expert", "dp", None),
            P("expert", None),
            P(),
            P("expert", "dp", None),
        ),
        out_specs=(
            P("expert", "dp", None),
            P("expert", "dp", None),
            P(None, ("dp", "expert"), None),
            P(("dp", "expert"), None),
            P(None, ("dp", "expert")),
            P(),
            P(("dp", "expert"), None),
            P("expert", None, "dp"),
            P("expert", "dp", None),
        ),
        check_vma=False,
    )
```

```python
import functools

import jax
import jax.numpy as jnp
from jax import lax
from jax.experimental import pallas as pl
from jax.experimental.pallas import tpu as pltpu
from jax.sharding import PartitionSpec as P

EPS = 1e-06
SCALE = 0.125
NEG = -1e30
VMEM_LIMIT = 48 * 1024 * 1024
SHORT = pl.CostEstimate(flops=1, bytes_accessed=1, transcendentals=0)
ROWS_BY_ROWS = (((1,), (1,)), ((), ()))
COLS_BY_COLS = (((0,), (0,)), ((), ()))
FIRST_BIT = ((0, 1), (1, 0), (2, 3), (3, 2))
SECOND_BIT = ((0, 2), (2, 0), (1, 3), (3, 1))
PARTNER = tuple((i, i ^ 1) for i in range(8))
NEXT_CHIP = tuple((i, i ^ 2) for i in range(8))
SECOND_CHIP = tuple((i, i ^ 4) for i in range(8))


def norm_forward(values, gain):
    inverse = lax.rsqrt(jnp.mean(values * values, axis=-1, keepdims=True) + EPS)
    return (values * inverse * gain, inverse)


def norm_backward(values, inverse, gain, grad_in):
    scaled = grad_in * gain
    cubed = inverse * inverse * inverse
    return inverse * scaled - values * cubed * jnp.mean(scaled * values, axis=-1, keepdims=True)


def low(values):
    return values.astype(jnp.bfloat16)


def wide(values):
    return values.astype(jnp.float32)


def pass_kernel(*refs):
    pass


def after(value, *others):
    if not others:
        return value
    return pl.pallas_call(
        pass_kernel,
        in_specs=[pl.BlockSpec(memory_space=pl.ANY)] * (1 + len(others)),
        out_specs=pl.BlockSpec(memory_space=pl.ANY),
        out_shape=jax.ShapeDtypeStruct(value.shape, value.dtype),
        input_output_aliases={0: 0},
        cost_estimate=SHORT,
        name="after",
    )(value, *others)


def by_steps():
    return lax.axis_size("dp") == 4 and lax.axis_size("expert") == 8


def dp_order():
    n_dp = lax.axis_size("dp")
    if by_steps():
        me = lax.axis_index("dp")
        return [jnp.bitwise_xor(me, r) for r in range(n_dp)]
    return [jnp.int32(r) for r in range(n_dp)]


def expert_order():
    groups = lax.axis_size("expert")
    if by_steps():
        me = lax.axis_index("expert")
        return [jnp.bitwise_xor(me, 2 * r + p) for p in range(2) for r in range(4)]
    return [jnp.int32(r) for r in range(groups)]


def dp_gather(block):
    if not by_steps():
        full = lax.all_gather(block, "dp")
        return [full[r] for r in range(full.shape[0])]
    half = block.shape[0] // 2
    along = lax.ppermute(block, "dp", FIRST_BIT)
    across = lax.ppermute(block, "dp", SECOND_BIT)
    far_low = lax.ppermute(across[:half], "dp", FIRST_BIT)
    far_high = lax.ppermute(along[half:], "dp", SECOND_BIT)
    return [block, along, across, jnp.concatenate([far_low, far_high], axis=0)]


def dp_gather_pair(first, second):
    if not by_steps():
        return dp_gather(first), dp_gather(second), (), ()
    along = [lax.ppermute(block, "dp", FIRST_BIT) for block in (first, second)]
    across = [lax.ppermute(block, "dp", SECOND_BIT) for block in (first, second)]
    far_first = lax.ppermute(across[0], "dp", FIRST_BIT)
    far_second = lax.ppermute(along[1], "dp", SECOND_BIT)
    return (
        [first, along[0], across[0], far_first],
        [second, along[1], across[1], far_second],
        (along[0], across[0]),
        (along[1], across[1]),
    )


def dp_scatter_pair(first, second):
    if not by_steps():
        return [
            wide(lax.psum_scatter(jnp.stack(parts), "dp", scatter_dimension=0))
            for parts in (first, second)
        ]
    first_far = lax.ppermute(first[3], "dp", FIRST_BIT)
    second_far = lax.ppermute(second[3], "dp", SECOND_BIT)
    first_along = lax.ppermute(first[1], "dp", FIRST_BIT)
    second_across = lax.ppermute(second[2], "dp", SECOND_BIT)
    return first_far, second_far, first_along, second_across


def dp_scatter_pair_end(first, second, received):
    if not by_steps():
        return (*received, ())
    first_far, second_far, first_along, second_across = received
    first_last = lax.ppermute(low(wide(first[2]) + wide(first_far)), "dp", SECOND_BIT)
    second_last = lax.ppermute(low(wide(second[1]) + wide(second_far)), "dp", FIRST_BIT)
    return (
        wide(first[0]) + wide(first_along) + wide(first_last),
        wide(second[0]) + wide(second_across) + wide(second_last),
        (first_last, second_last),
    )


def dp_scatter(parts):
    if not by_steps():
        return wide(lax.psum_scatter(jnp.stack(parts), "dp", scatter_dimension=0))
    half = parts[0].shape[0] // 2
    low_half, high_half = ([part[rows] for part in parts] for rows in (slice(0, half), slice(half, None)))
    received = dp_scatter_pair(low_half, high_half)
    return jnp.concatenate(dp_scatter_pair_end(low_half, high_half, received)[:2], axis=0)


def line_gather(block, gates=()):
    near = lax.ppermute(block, "expert", NEXT_CHIP)
    far = lax.ppermute(block, "expert", SECOND_CHIP)
    corner = lax.ppermute(after(far, *gates), "expert", NEXT_CHIP)
    return [block, near, far, corner]


def line_scatter(parts, first_gate=(), second_gate=(), near_gate=()):
    corner = lax.ppermute(after(parts[3], *first_gate), "expert", NEXT_CHIP)
    passed = after(low(wide(parts[2]) + wide(corner)), *second_gate)
    near = lax.ppermute(after(parts[1], *near_gate), "expert", NEXT_CHIP)
    far = lax.ppermute(passed, "expert", SECOND_CHIP)
    return wide(parts[0]) + wide(near) + wide(far), corner, (near, far)


def expert_gather(block, gates=()):
    if not by_steps():
        return lax.all_gather(block, "expert"), ()
    mine = line_gather(block, gates)
    return jnp.stack(mine + [lax.ppermute(piece, "expert", PARTNER) for piece in mine]), mine


def expert_scatter(parts, first_gate=(), second_gate=(), near_gate=()):
    if not by_steps():
        total = wide(lax.psum_scatter(parts, "expert", scatter_dimension=0))
        return total, total, ()
    other = lax.ppermute(after(parts[4:], *first_gate), "expert", PARTNER)
    merged = [low(wide(parts[r]) + wide(other[r])) for r in range(4)]
    return line_scatter(merged, (), second_gate, near_gate)


def gather_all(shard, gates=()):
    rows, columns = shard.shape
    if not by_steps():
        return lax.all_gather(shard, ("dp", "expert"), axis=0, tiled=True), ()
    place = lax.axis_index("dp")
    odd_first, odd_second = place % 2 == 1, place // 2 == 1
    along = lax.ppermute(shard, "dp", FIRST_BIT)
    near = jnp.where(odd_first, jnp.stack([along, shard]), jnp.stack([shard, along]))
    far = lax.ppermute(near, "dp", SECOND_BIT)
    plane = jnp.where(odd_second, jnp.concatenate([far, near]), jnp.concatenate([near, far]))
    mine = line_gather(plane)
    pieces = mine + [lax.ppermute(piece, "expert", PARTNER) for piece in mine]
    owners = expert_order()
    full = jnp.zeros((4, 8, rows, columns), shard.dtype)
    pieces[0] = after(pieces[0], *gates)
    for index, piece in enumerate(pieces):
        full = lax.dynamic_update_slice_in_dim(full, piece[:, None], owners[index], 1)
    return full.reshape(32 * rows, columns), mine[3:]


def scatter_all(parts, gates=()):
    if not by_steps():
        return wide(lax.psum_scatter(parts, ("dp", "expert"), scatter_dimension=1, tiled=True))
    count, rows, columns = parts.shape
    blocks = parts.reshape(count, 4, 4, 2, rows // 32, columns)
    me = lax.axis_index("expert")
    chip, core = me // 2, me % 2
    kept, given = (
        lax.dynamic_index_in_dim(blocks, index, 3, keepdims=False) for index in (core, 1 - core)
    )
    merged = low(wide(kept) + wide(lax.ppermute(given, "expert", PARTNER)))
    plane = low(
        dp_scatter(
            [lax.dynamic_index_in_dim(merged, place, 1, keepdims=False) for place in dp_order()]
        )
    )
    pieces = [
        lax.dynamic_index_in_dim(plane, jnp.bitwise_xor(chip, r), 1, keepdims=False)
        for r in range(4)
    ]
    return line_scatter(pieces, gates)[0]


def sum_all(values):
    if not by_steps():
        return lax.psum(values, ("dp", "expert"))
    for bit in (1, 2, 4):
        values = values + lax.ppermute(values, "expert", [(i, i ^ bit) for i in range(8)])
    for pairs in (FIRST_BIT, SECOND_BIT):
        values = values + lax.ppermute(values, "dp", pairs)
    return values


def spread_rows(base, span):
    grown = base
    while grown.shape[0] < span:
        grown = jnp.concatenate([grown, pltpu.roll(grown, grown.shape[0], 1)], axis=0)
    return grown[:, span:]


def fold_rows(block, span):
    wide = jnp.concatenate([jnp.zeros_like(block), block], axis=1)
    while wide.shape[0] > 1:
        half = wide.shape[0] // 2
        wide = wide[:half] + pltpu.roll(wide[half:], 2 * span - half, 1)
    return wide


def attention_forward_kernel(
    n_piece, span, head_dim, n_gate, q_ref, k_ref, v_ref, base_ref, start_ref, *refs
):
    out_ref, lse_ref, bias_ref = refs[n_gate:]

    @pl.when(pl.program_id(1) == 0)
    def fill_bias():
        for head in range(2):
            for piece in range(n_piece):
                bias_ref[head, piece] = spread_rows(
                    base_ref[0, head, piece : piece + 1, :], span
                )

    queries = q_ref[0]
    lane_head = lax.broadcasted_iota(jnp.int32, queries.shape, 1) // head_dim
    key_row = lax.broadcasted_iota(jnp.int32, (span, span), 0)
    values_t = [v_ref[0, pl.ds(piece * span, span), :].T for piece in range(n_piece)]
    outs = []
    for head in range(2):
        masked = jnp.where(lane_head == head, queries, jnp.zeros_like(queries))
        scores = []
        highest = None
        for piece in range(n_piece):
            keys = k_ref[0, pl.ds(piece * span, span), :]
            block = lax.dot_general(
                keys, masked, (((1,), (1,)), ((), ())), preferred_element_type=jnp.float32
            )
            block = block + bias_ref[head, piece]
            block = jnp.where(key_row >= start_ref[0, piece : piece + 1, :], block, NEG)
            scores.append(block)
            top = jnp.max(block, axis=0, keepdims=True)
            highest = top if highest is None else jnp.maximum(highest, top)
        total = jnp.zeros_like(highest)
        result = jnp.zeros((head_dim, span), jnp.float32)
        for piece in range(n_piece):
            weights = jnp.exp(scores[piece] - highest)
            total = total + jnp.sum(weights, axis=0, keepdims=True)
            result = result + jnp.dot(
                values_t[piece][head * head_dim : (head + 1) * head_dim],
                weights.astype(jnp.bfloat16),
                preferred_element_type=jnp.float32,
            )
        outs.append(result / total)
        lse_ref[0, 0, head : head + 1, :] = highest + jnp.log(total)
    out_ref[0] = jnp.concatenate(outs, axis=0).T.astype(out_ref.dtype)


def attention_backward_kernel(
    n_piece,
    span,
    head_dim,
    n_gate,
    q_ref,
    k_ref,
    v_ref,
    out_ref,
    grad_ref,
    base_ref,
    start_ref,
    lse_ref,
    *refs,
):
    dq_ref, dk_ref, dv_ref, dist_ref, bias_ref, sum_ref = refs[n_gate:]
    batch = pl.program_id(1)

    @pl.when(batch == 0)
    def fill_bias():
        for head in range(2):
            for piece in range(n_piece):
                bias_ref[head, piece] = spread_rows(
                    base_ref[0, head, piece : piece + 1, :], span
                )
                sum_ref[head, piece] = jnp.zeros((span, span), jnp.float32)

    queries = q_ref[0]
    grads = grad_ref[0]
    product = grads.astype(jnp.float32) * out_ref[0].astype(jnp.float32)
    product_hi = product.astype(jnp.bfloat16)
    product_lo = (product - product_hi.astype(jnp.float32)).astype(jnp.bfloat16)
    lane_head = lax.broadcasted_iota(jnp.int32, queries.shape, 1) // head_dim
    key_row = lax.broadcasted_iota(jnp.int32, (span, span), 0)
    picker = (
        lax.broadcasted_iota(jnp.int32, (8, 2 * head_dim), 1) // head_dim
        == lax.broadcasted_iota(jnp.int32, (8, 2 * head_dim), 0)
    ).astype(jnp.bfloat16)
    rows_by_rows = (((1,), (1,)), ((), ()))
    correction = lax.dot_general(
        picker, product_hi, rows_by_rows, preferred_element_type=jnp.float32
    ) + lax.dot_general(picker, product_lo, rows_by_rows, preferred_element_type=jnp.float32)
    zero = jnp.zeros_like(queries)
    head_queries = [jnp.where(lane_head == head, queries, zero) for head in range(2)]
    head_grads = [jnp.where(lane_head == head, grads, zero) for head in range(2)]
    query_grads = [jnp.zeros((head_dim, span), jnp.float32) for _ in range(2)]
    for piece in range(n_piece):
        rows = pl.ds(piece * span, span)
        keys = k_ref[0, rows, :]
        values = v_ref[0, rows, :]
        keys_t = keys.T
        allowed = key_row >= start_ref[0, piece : piece + 1, :]
        key_grad = jnp.zeros((span, 2 * head_dim), jnp.float32)
        value_grad = jnp.zeros((span, 2 * head_dim), jnp.float32)
        for head in range(2):
            scores = lax.dot_general(
                keys, head_queries[head], rows_by_rows, preferred_element_type=jnp.float32
            )
            scores = jnp.where(allowed, scores + bias_ref[head, piece], NEG)
            probs = jnp.exp(scores - lse_ref[0, 0, head : head + 1, :])
            prob_grad = lax.dot_general(
                values, head_grads[head], rows_by_rows, preferred_element_type=jnp.float32
            )
            score_grad = (probs * (prob_grad - correction[head : head + 1, :])).astype(jnp.bfloat16)
            sum_ref[head, piece] += score_grad.astype(jnp.float32)
            value_grad = value_grad + jnp.dot(
                probs.astype(jnp.bfloat16), head_grads[head], preferred_element_type=jnp.float32
            )
            key_grad = key_grad + jnp.dot(
                score_grad, head_queries[head], preferred_element_type=jnp.float32
            )
            query_grads[head] = query_grads[head] + jnp.dot(
                keys_t[head * head_dim : (head + 1) * head_dim],
                score_grad,
                preferred_element_type=jnp.float32,
            )
        dk_ref[0, rows, :] = key_grad.astype(jnp.bfloat16)
        dv_ref[0, rows, :] = value_grad.astype(jnp.bfloat16)
    dq_ref[0] = (jnp.concatenate(query_grads, axis=0) * SCALE).T.astype(jnp.bfloat16)

    @pl.when(batch == pl.num_programs(1) - 1)
    def fold_distances():
        for head in range(2):
            for piece in range(n_piece):
                dist_ref[0, head, piece : piece + 1, :] = fold_rows(sum_ref[head, piece], span)


def gate_specs(gate):
    return [pl.BlockSpec(memory_space=pl.ANY) for _ in gate]


def attention_specs(n_piece, span, pair):
    n_keys = n_piece * span
    rows = pl.BlockSpec((1, span, pair), lambda h, b: (b, 0, h))
    keys = pl.BlockSpec((1, n_keys, pair), lambda h, b: (b, 0, h))
    base = pl.BlockSpec((1, 2, n_piece, 2 * span), lambda h, b: (h, 0, 0, 0))
    start = pl.BlockSpec((1, n_piece, span), lambda h, b: (b, 0, 0))
    lse = pl.BlockSpec((1, 1, 2, span), lambda h, b: (h, b, 0, 0))
    return rows, keys, base, start, lse


def attention_forward(queries, keys, values, base, start, n_heads, gate=()):
    n_batch, span, inner = queries.shape
    n_piece = keys.shape[1] // span
    head_dim = inner // n_heads
    n_pairs = n_heads // 2
    rows, key_rows, base_spec, start_spec, lse_spec = attention_specs(n_piece, span, 2 * head_dim)
    return pl.pallas_call(
        functools.partial(attention_forward_kernel, n_piece, span, head_dim, len(gate)),
        grid=(n_pairs, n_batch),
        in_specs=[rows, key_rows, key_rows, base_spec, start_spec] + gate_specs(gate),
        out_specs=[rows, lse_spec],
        out_shape=[
            jax.ShapeDtypeStruct(queries.shape, jnp.bfloat16),
            jax.ShapeDtypeStruct((n_pairs, n_batch, 2, span), jnp.float32),
        ],
        scratch_shapes=[pltpu.VMEM((2, n_piece, span, span), jnp.float32)],
        compiler_params=pltpu.CompilerParams(vmem_limit_bytes=VMEM_LIMIT),
        cost_estimate=SHORT,
        name="attention_forward",
    )(queries, keys, values, base, start, *gate)


def attention_backward(
    queries, keys, values, attended, grads, base, start, lse, n_heads, gate=()
):
    n_batch, span, inner = queries.shape
    n_piece = keys.shape[1] // span
    head_dim = inner // n_heads
    n_pairs = n_heads // 2
    rows, key_rows, base_spec, start_spec, lse_spec = attention_specs(n_piece, span, 2 * head_dim)
    return pl.pallas_call(
        functools.partial(attention_backward_kernel, n_piece, span, head_dim, len(gate)),
        grid=(n_pairs, n_batch),
        in_specs=[rows, key_rows, key_rows, rows, rows, base_spec, start_spec, lse_spec]
        + gate_specs(gate),
        out_specs=[rows, key_rows, key_rows, base_spec],
        out_shape=[
            jax.ShapeDtypeStruct(queries.shape, jnp.bfloat16),
            jax.ShapeDtypeStruct(keys.shape, jnp.bfloat16),
            jax.ShapeDtypeStruct(keys.shape, jnp.bfloat16),
            jax.ShapeDtypeStruct((n_pairs, 2, n_piece, 2 * span), jnp.float32),
        ],
        scratch_shapes=[
            pltpu.VMEM((2, n_piece, span, span), jnp.float32),
            pltpu.VMEM((2, n_piece, span, span), jnp.float32),
        ],
        compiler_params=pltpu.CompilerParams(vmem_limit_bytes=VMEM_LIMIT),
        cost_estimate=pl.CostEstimate(
            flops=40 * n_batch * n_heads * span * n_piece * span * head_dim,
            bytes_accessed=12 * keys.size,
            transcendentals=0,
        ),
        name="attention_backward",
    )(queries, keys, values, attended, grads, base, start, lse, *gate)


def bias_base(rel_bias, bucket_ids, offsets, span):
    length = bucket_ids.shape[0]
    hits = wide(bucket_ids[None, :] == jnp.arange(rel_bias.shape[0], dtype=jnp.int32)[:, None])
    table = jnp.dot(rel_bias.T, hits, precision=lax.Precision.HIGHEST)
    padded = jnp.pad(table, ((0, 0), (length, 0)), constant_values=NEG)
    windows = [
        lax.dynamic_slice_in_dim(padded, offset + length - span, 2 * span, 1) for offset in offsets
    ]
    base = jnp.stack(windows, axis=1)
    return base.reshape(base.shape[0] // 2, 2, len(offsets), 2 * span)


def bias_fold(dist, bucket_ids, offsets, n_buckets):
    n_heads, n_piece, span = dist.shape[0] * 2, dist.shape[2], dist.shape[3] // 2
    length = bucket_ids.shape[0]
    sums = dist.reshape(n_heads, n_piece, 2 * span)
    hits = wide(bucket_ids[:, None] == jnp.arange(n_buckets, dtype=jnp.int32)[None, :])
    padded = jnp.pad(hits, ((length, 0), (0, 0)))
    windows = jnp.stack(
        [lax.dynamic_slice_in_dim(padded, offset + length - span, 2 * span, 0) for offset in offsets]
    )
    return jnp.einsum("hpu,pun->nh", sums, windows, precision=lax.Precision.HIGHEST)


def document_starts(doc_lengths, offset, span):
    ends = jnp.cumsum(doc_lengths, axis=-1)
    places = offset + jnp.arange(span, dtype=jnp.int32)
    begun = ends[:, None, :] <= places[None, :, None]
    return jnp.max(jnp.where(begun, ends[:, None, :], 0), axis=-1)


def token_gates(router_t, tokens, routes):
    logits = lax.dot_general(
        router_t, tokens, ROWS_BY_ROWS, preferred_element_type=jnp.float32
    )
    expert = lax.broadcasted_iota(jnp.int32, logits.shape, 0)
    hits = [expert == routes[k : k + 1, :] for k in range(2)]
    chosen = [jnp.sum(jnp.where(hit, logits, 0.0), axis=0, keepdims=True) for hit in hits]
    highest = jnp.maximum(chosen[0], chosen[1])
    raised = [jnp.exp(value - highest) for value in chosen]
    total = raised[0] + raised[1]
    return [value / total for value in raised], hits


def slot_table(slots, n_slots):
    index = lax.broadcasted_iota(jnp.int32, (n_slots, slots.shape[1]), 0)
    return jnp.concatenate(
        [wide(index == slots[e : e + 1, :]) for e in range(slots.shape[0])], axis=0
    )


def dispatch_kernel(
    n_slots, n_gate, token_ref, grad_ref, router_ref, route_ref, slot_ref, first_ref, *refs
):
    in_ref, up_ref, kept_ref, gate_ref = refs[n_gate:]
    tokens = token_ref[0]
    gates, _ = token_gates(router_ref[...], tokens, route_ref[0])
    slots = slot_ref[0]
    table = slot_table(slots, n_slots)
    table_low = low(table)
    local = slots.shape[0]
    picked = jnp.dot(table_low, tokens, preferred_element_type=jnp.float32)
    grads = jnp.dot(table_low, grad_ref[0], preferred_element_type=jnp.float32)
    first = first_ref[0]
    gate_ref[0] = jnp.concatenate(gates, axis=0)
    for e in range(local):
        rows = slice(e * n_slots, (e + 1) * n_slots)
        gate = jnp.where(
            route_ref[0, 0:1, :] == first + e,
            gates[0],
            jnp.where(route_ref[0, 1:2, :] == first + e, gates[1], 0.0),
        )
        slot_gate = jnp.sum(table[rows] * gate, axis=1, keepdims=True)
        in_ref[e] = low(picked[rows])
        kept_ref[e] = low(grads[rows])
        up_ref[e] = low(grads[rows] * slot_gate)


def dispatch(tokens, grads, router_t, routes, slots, first, n_slots, gate=()):
    n_block, span, width = tokens.shape
    local = slots.shape[1]
    block = pl.BlockSpec((1, span, width), lambda b: (b, 0, 0))
    per_device = n_block // grads.shape[0]
    grad_block = pl.BlockSpec((1, span, width), lambda b: (b // per_device, b % per_device, 0))
    rows = pl.BlockSpec((local, n_slots, width), lambda b: (0, b, 0))
    return pl.pallas_call(
        functools.partial(dispatch_kernel, n_slots, len(gate)),
        grid=(n_block,),
        in_specs=[
            block,
            grad_block,
            pl.BlockSpec(router_t.shape, lambda b: (0, 0)),
            pl.BlockSpec((1, 2, span), lambda b: (b, 0, 0)),
            pl.BlockSpec((1, local, span), lambda b: (b, 0, 0)),
            pl.BlockSpec(memory_space=pltpu.SMEM),
        ]
        + gate_specs(gate),
        out_specs=[rows, rows, rows, pl.BlockSpec((1, 2, span), lambda b: (b, 0, 0))],
        out_shape=[jax.ShapeDtypeStruct((local, n_block * n_slots, width), jnp.bfloat16)] * 3
        + [jax.ShapeDtypeStruct((n_block, 2, span), jnp.float32)],
        compiler_params=pltpu.CompilerParams(vmem_limit_bytes=VMEM_LIMIT),
        cost_estimate=SHORT,
        name="dispatch",
    )(tokens, grads, router_t, routes, slots, first, *gate)


def combine_kernel(
    n_slots,
    n_gate,
    in_ref,
    kept_ref,
    gate_ref,
    router_ref,
    route_ref,
    slot_ref,
    first_ref,
    out_ref,
    back_ref,
    *refs,
):
    mixed_ref, sum_ref, router_grad_ref = refs[n_gate:]

    @pl.when(pl.program_id(0) == 0)
    def clear():
        router_grad_ref[...] = jnp.zeros_like(router_grad_ref)

    slots = slot_ref[0]
    local, span = slots.shape
    gates = [gate_ref[0, k : k + 1, :] for k in range(2)]
    expert = lax.broadcasted_iota(jnp.int32, (router_ref.shape[1], span), 0)
    hits = [expert == route_ref[0, k : k + 1, :] for k in range(2)]
    table = slot_table(slots, n_slots)
    table_low = low(table)
    first = first_ref[0]

    def rows_of(ref):
        return jnp.concatenate([ref[e] for e in range(local)], axis=0)

    produced = wide(rows_of(out_ref))
    gate_grad = jnp.sum(wide(rows_of(kept_ref)) * produced, axis=1, keepdims=True)
    spread = (wide(hits[0]) - wide(hits[1])) * (gates[0] * gates[1])
    spread_hi = low(spread)
    spread_lo = low(spread - wide(spread_hi))
    factor = lax.dot_general(
        table_low, spread_hi, ROWS_BY_ROWS, preferred_element_type=jnp.float32
    ) + lax.dot_general(table_low, spread_lo, ROWS_BY_ROWS, preferred_element_type=jnp.float32)
    signs, slot_gates = [], []
    for e in range(local):
        rows = slice(e * n_slots, (e + 1) * n_slots)
        is_first = route_ref[0, 0:1, :] == first + e
        is_second = route_ref[0, 1:2, :] == first + e
        sign = jnp.where(is_first, 1.0, jnp.where(is_second, -1.0, 0.0))
        gate = jnp.where(is_first, gates[0], jnp.where(is_second, gates[1], 0.0))
        signs.append(jnp.sum(table[rows] * sign, axis=1, keepdims=True))
        slot_gates.append(jnp.sum(table[rows] * gate, axis=1, keepdims=True))
    sign, slot_gate = jnp.concatenate(signs, axis=0), jnp.concatenate(slot_gates, axis=0)
    logit_grad = factor * (sign * gate_grad)
    logit_hi = low(logit_grad)
    logit_lo = low(logit_grad - wide(logit_hi))
    back = wide(rows_of(back_ref))
    for part in (logit_hi, logit_lo):
        back = back + lax.dot_general(
            part, router_ref[...], ROWS_BY_ROWS, preferred_element_type=jnp.float32
        )
    mixed_ref[0] = low(
        lax.dot_general(
            table_low,
            low(produced * slot_gate),
            COLS_BY_COLS,
            preferred_element_type=jnp.float32,
        )
    )
    sum_ref[0] = low(
        lax.dot_general(table_low, low(back), COLS_BY_COLS, preferred_element_type=jnp.float32)
    )
    picked = rows_of(in_ref)
    for part in (logit_hi, logit_lo):
        router_grad_ref[...] += lax.dot_general(
            part, picked, COLS_BY_COLS, preferred_element_type=jnp.float32
        )


def combine(inputs, kept, gates, router, routes, slots, first, out, back, n_slots, gate=()):
    n_block, local, span = slots.shape
    width, experts = router.shape
    rows = pl.BlockSpec((local, n_slots, width), lambda b: (0, b, 0))
    block = pl.BlockSpec((1, span, width), lambda b: (b, 0, 0))
    return pl.pallas_call(
        functools.partial(combine_kernel, n_slots, len(gate)),
        grid=(n_block,),
        in_specs=[
            rows,
            rows,
            pl.BlockSpec((1, 2, span), lambda b: (b, 0, 0)),
            pl.BlockSpec(router.shape, lambda b: (0, 0)),
            pl.BlockSpec((1, 2, span), lambda b: (b, 0, 0)),
            pl.BlockSpec((1, local, span), lambda b: (b, 0, 0)),
            pl.BlockSpec(memory_space=pltpu.SMEM),
            rows,
            rows,
        ]
        + gate_specs(gate),
        out_specs=[block, block, pl.BlockSpec((experts, width), lambda b: (0, 0))],
        out_shape=[
            jax.ShapeDtypeStruct((n_block, span, width), jnp.bfloat16),
            jax.ShapeDtypeStruct((n_block, span, width), jnp.bfloat16),
            jax.ShapeDtypeStruct((experts, width), jnp.float32),
        ],
        compiler_params=pltpu.CompilerParams(vmem_limit_bytes=VMEM_LIMIT),
        cost_estimate=SHORT,
        name="combine",
    )(inputs, kept, gates, router, routes, slots, first, out, back, *gate)


def expert_kernel(tile, started, *refs):
    if started:
        x_ref, g_ref, in_ref, down_ref, out_so_far, back_so_far = refs[:6]
        refs = refs[6:]
    else:
        x_ref, g_ref, in_ref, down_ref = refs[:4]
        refs = refs[4:]
    out_ref, back_ref, in_grad_ref, down_grad_ref, x_t, hidden_t, pre_grads = refs
    step = pl.program_id(1)
    rows = pl.ds(pl.multiple_of(step * tile, tile), tile)
    x = x_ref[0, rows, :]
    g = g_ref[0, rows, :]
    pre = jnp.dot(x, in_ref[0], preferred_element_type=jnp.float32)
    hidden_grad = lax.dot_general(
        g, down_ref[0], ROWS_BY_ROWS, preferred_element_type=jnp.float32
    )
    root = 0.7978845608028654
    square = pre * pre
    bent = jnp.tanh(pre * (root + root * 0.044715 * square))
    half = 0.5 + 0.5 * bent
    hidden = low(pre * half)
    slope = half + pre * (half * (1.0 - bent)) * (root + 3.0 * root * 0.044715 * square)
    pre_grad = low(hidden_grad * slope)
    out = jnp.dot(hidden, down_ref[0], preferred_element_type=jnp.float32)
    back = lax.dot_general(
        pre_grad, in_ref[0], ROWS_BY_ROWS, preferred_element_type=jnp.float32
    )
    if started:
        out = out + out_so_far[0]
        back = back + back_so_far[0]
    out_ref[0] = out.astype(out_ref.dtype)
    back_ref[0] = back.astype(back_ref.dtype)
    x_t[:, rows] = x.T
    hidden_t[:, rows] = hidden.T
    pre_grads[rows, :] = pre_grad

    @pl.when(step == pl.num_programs(1) - 1)
    def weight_grads():
        part = 256
        for at in range(0, hidden_t.shape[0], part):
            some = slice(at, min(at + part, hidden_t.shape[0]))
            down_grad_ref[0, some, :] = low(
                jnp.dot(hidden_t[some, :], g_ref[0], preferred_element_type=jnp.float32)
            )
        for at in range(0, x_t.shape[0], part):
            some = slice(at, min(at + part, x_t.shape[0]))
            in_grad_ref[0, some, :] = low(
                jnp.dot(x_t[some, :], pre_grads[...], preferred_element_type=jnp.float32)
            )


def expert_slice(x, g, w_in, w_out, so_far, is_last):
    local, n_rows, width = x.shape
    inner = w_in.shape[2]
    tile = 256
    whole = pl.BlockSpec((1, n_rows, width), lambda e, i: (e, 0, 0))
    up = pl.BlockSpec((1, width, inner), lambda e, i: (e, 0, 0))
    down = pl.BlockSpec((1, inner, width), lambda e, i: (e, 0, 0))
    some = pl.BlockSpec((1, tile, width), lambda e, i: (e, i, 0))
    started = so_far is not None
    kind = jnp.bfloat16 if is_last else jnp.float32
    totals = tuple(so_far) if started else ()
    return pl.pallas_call(
        functools.partial(expert_kernel, tile, started),
        grid=(local, n_rows // tile),
        in_specs=[whole, whole, up, down] + [some] * len(totals),
        out_specs=[some, some, up, down],
        out_shape=[
            jax.ShapeDtypeStruct(x.shape, kind),
            jax.ShapeDtypeStruct(x.shape, kind),
            jax.ShapeDtypeStruct(w_in.shape, jnp.bfloat16),
            jax.ShapeDtypeStruct(w_out.shape, jnp.bfloat16),
        ],
        input_output_aliases={4: 0, 5: 1} if started and not is_last else {},
        scratch_shapes=[
            pltpu.VMEM((width, n_rows), jnp.bfloat16),
            pltpu.VMEM((inner, n_rows), jnp.bfloat16),
            pltpu.VMEM((n_rows, inner), jnp.bfloat16),
        ],
        compiler_params=pltpu.CompilerParams(vmem_limit_bytes=VMEM_LIMIT),
        cost_estimate=SHORT,
        name="expert_slice",
    )(x, g, w_in, w_out, *totals)


def body(
    tokens,
    cotangent,
    qkv_weight,
    out_weight,
    norm_gains,
    rel_bias,
    router_weight,
    w_in,
    w_out,
    doc_lengths,
    bucket_ids,
    routes,
):
    n_batch, n_span, n_width = tokens.shape
    n_rows = n_batch * n_span
    n_buckets, n_heads = rel_bias.shape
    n_inner = qkv_weight.shape[2]
    groups = lax.axis_size("expert")
    local_experts = w_in.shape[0]
    experts_all = local_experts * groups
    n_slots = max(2, 2 * n_span * 2 // experts_all)
    dp_places = dp_order()
    place = lax.axis_index("dp")
    n_dp = len(dp_places)
    offsets = [(place - piece) * n_span for piece in dp_places]
    extra = experts_all + 2
    lanes = -(-extra // 128) * 128
    route_rows = -(-2 * n_rows // n_width // 16) * 16
    packed = jnp.concatenate(
        [qkv_weight[0], qkv_weight[1], qkv_weight[2], out_weight]
        + [router_weight, norm_gains.T, jnp.zeros((out_weight.shape[0], lanes - extra), jnp.bfloat16)],
        axis=1,
    )
    token_pieces = dp_gather(tokens)
    ahead = token_pieces[1:3] if by_steps() else ()
    in_pieces, down_pieces, near_in, near_down = dp_gather_pair(after(w_in, *ahead), w_out)
    full, full_last = gather_all(packed, near_in)
    weights = [full[:, c * n_inner : (c + 1) * n_inner] for c in range(4)]
    router = full[:, 4 * n_inner : 4 * n_inner + experts_all]
    router_t = router.T
    gains = wide(full[:, 4 * n_inner + experts_all : 4 * n_inner + extra].T)
    route_values = low(routes.reshape(n_batch, n_span, 2).transpose(0, 2, 1)).reshape(-1)
    route_values = jnp.pad(route_values, (0, route_rows * n_width - 2 * n_rows))
    grad_rows = jnp.concatenate(
        [cotangent.reshape(n_rows, n_width), route_values.reshape(route_rows, n_width)]
    )
    grad_all, grad_steps = expert_gather(after(grad_rows, *full_last))
    routes_all = grad_all[:, n_rows:].reshape(groups, -1)[:, : 2 * n_rows]
    routes_all = routes_all.astype(jnp.int32).reshape(groups * n_batch, 2, n_span)
    first = lax.axis_index("expert").astype(jnp.int32) * local_experts
    mine = first + jnp.arange(local_experts, dtype=jnp.int32)
    member = jnp.any(routes_all[:, None] == mine[None, :, None, None], axis=2)
    before = wide(jnp.arange(n_span)[:, None] < jnp.arange(n_span)[None, :])
    ranks = jnp.einsum(
        "bet,tu->beu", low(member), low(before), preferred_element_type=jnp.float32
    ).astype(jnp.int32)
    slots = jnp.where(member, ranks, -1)
    first = first[None]

    base = bias_base(rel_bias, bucket_ids, offsets, n_span)
    begin = document_starts(doc_lengths, place * n_span, n_span)
    starts = jnp.stack([begin - piece * n_span for piece in dp_places], axis=1)

    normed1_all = jnp.stack(
        [low(norm_forward(wide(piece), gains[0])[0]) for piece in token_pieces], axis=1
    )
    normed1_all = normed1_all.reshape(n_batch, n_dp * n_span, n_width)
    flat_normed1 = normed1_all.reshape(-1, n_width)
    normed1 = normed1_all[:, :n_span] if by_steps() else lax.dynamic_slice_in_dim(
        normed1_all, place * n_span, n_span, 1
    )
    normed1 = normed1.reshape(n_rows, n_width)
    queries = low(low(jnp.dot(normed1, weights[0], preferred_element_type=jnp.float32)) * SCALE)
    queries = queries.reshape(n_batch, n_span, n_inner)
    keys, values = (
        low(jnp.dot(flat_normed1, weights[c], preferred_element_type=jnp.float32)).reshape(
            n_batch, -1, n_inner
        )
        for c in (1, 2)
    )
    attended_rows, log_total = attention_forward(
        queries, keys, values, base, starts, n_heads, tuple(grad_steps[1:])
    )
    attended = attended_rows.reshape(n_rows, n_inner)
    inputs = wide(tokens.reshape(n_rows, n_width))
    resid = inputs + jnp.dot(attended, weights[3], preferred_element_type=jnp.float32)
    normed2, inverse2 = norm_forward(resid, gains[1])
    normed2_low = low(normed2).reshape(n_batch, n_span, n_width)
    token_all = expert_gather(normed2_low, near_down)[0]
    token_all = token_all.reshape(groups * n_batch, n_span, n_width)
    expert_in, expert_up, expert_kept, gates = dispatch(
        token_all,
        grad_all,
        router_t,
        routes_all,
        slots,
        first,
        n_slots,
        (*in_pieces[1:], *down_pieces[1:]),
    )
    so_far = None
    in_grads, down_grads = {}, {}
    for r in (*range(n_dp - 1, 3, -1), 3, 1, 2, 0):
        *so_far, in_grads[r], down_grads[r] = expert_slice(
            expert_in, expert_up, in_pieces[r], down_pieces[r], so_far, r == 0
        )
    in_grads, down_grads = ([grads[r] for r in range(n_dp)] for grads in (in_grads, down_grads))
    piece_shape = (groups, n_batch, n_span, n_width)
    received = dp_scatter_pair(in_grads, down_grads)
    in_share, down_share, last = dp_scatter_pair_end(in_grads, down_grads, received)
    mixed_all, back_all, router_grad = combine(
        expert_in,
        expert_kept,
        gates,
        router,
        routes_all,
        slots,
        first,
        *so_far,
        n_slots,
        received[:2] if last else (),
    )
    normed2_grad, _, back_last = expert_scatter(
        back_all.reshape(piece_shape), received[2:] if last else ()
    )
    normed2_grad = normed2_grad.reshape(n_rows, n_width)
    gain2_grad = jnp.sum(normed2_grad * resid * inverse2, axis=0)
    grad_out = wide(cotangent.reshape(n_rows, n_width))
    resid_grad = grad_out + norm_backward(resid, inverse2, gains[1], normed2_grad)
    branch_low = low(resid_grad)
    attended_grad = low(
        lax.dot_general(branch_low, weights[3], ROWS_BY_ROWS, preferred_element_type=jnp.float32)
    )
    query_grad, key_grad, value_grad, dist_grad = attention_backward(
        queries,
        keys,
        values,
        attended_rows,
        attended_grad.reshape(n_batch, n_span, n_inner),
        base,
        starts,
        log_total,
        n_heads,
        last,
    )
    bias_grad = bias_fold(dist_grad, bucket_ids, offsets, n_buckets)
    mixed_all = after(mixed_all.reshape(piece_shape), *back_last)
    mixed, mixed_corner, mixed_last = expert_scatter(mixed_all, (), (dist_grad,), (dist_grad,))
    block_out = low(resid + mixed.reshape(n_rows, n_width)).reshape(n_batch, n_span, n_width)
    query_grad = query_grad.reshape(n_rows, n_inner)
    key_grad = after(key_grad, mixed_corner).reshape(-1, n_inner)
    value_grad = value_grad.reshape(-1, n_inner)
    own_part = lax.dot_general(
        query_grad, weights[0], ROWS_BY_ROWS, preferred_element_type=jnp.float32
    )
    all_part = lax.dot_general(
        key_grad, weights[1], ROWS_BY_ROWS, preferred_element_type=jnp.float32
    ) + lax.dot_general(value_grad, weights[2], ROWS_BY_ROWS, preferred_element_type=jnp.float32)
    all_part = all_part.reshape(n_batch, n_dp, n_span, n_width)
    sent = low(all_part)
    shared = dp_scatter([sent[:, r] for r in range(n_dp)])
    normed1_grad = own_part + shared.reshape(n_rows, n_width)
    inverse1 = lax.rsqrt(jnp.mean(inputs * inputs, axis=-1, keepdims=True) + EPS)
    tokens_grad = resid_grad + norm_backward(inputs, inverse1, gains[0], normed1_grad)
    def rows_grad(rows, grads):
        return low(
            lax.dot_general(rows, grads, COLS_BY_COLS, preferred_element_type=jnp.float32)
        )

    weight_grads = jnp.stack(
        [
            rows_grad(normed1, query_grad),
            rows_grad(flat_normed1, key_grad),
            rows_grad(flat_normed1, value_grad),
            rows_grad(attended, branch_low),
        ]
    )
    gain1_grad = (
        sum(jnp.sum(wide(weight_grads[c]) * wide(weights[c]), axis=1) for c in range(3)) / gains[0]
    )
    shares = scatter_all(weight_grads, mixed_last)
    small_rows = experts_all + 2
    bias_flat = jnp.pad(bias_grad.reshape(1, -1), ((0, 0), (0, n_width - bias_grad.size)))
    small = sum_all(
        jnp.concatenate([router_grad, gain1_grad[None], gain2_grad[None], bias_flat])
    )
    rel_bias_grad = small[small_rows, : bias_grad.size].reshape(bias_grad.shape)
    n_own = router_weight.shape[0]
    own = lax.dynamic_slice_in_dim(
        small, (place * groups + lax.axis_index("expert")) * n_own, n_own, 1
    )
    router_share = own[:experts_all].T
    gains_share = own[experts_all:small_rows]
    qkv_share, out_share = shares[:3], shares[3]
    return (
        block_out,
        tokens_grad.reshape(n_batch, n_span, n_width),
        qkv_share,
        out_share,
        gains_share,
        rel_bias_grad,
        router_share,
        in_share,
        down_share,
    )


def solution(mesh):
    return jax.shard_map(
        body,
        mesh=mesh,
        in_specs=(
            P("expert", "dp", None),
            P("expert", "dp", None),
            P(None, ("dp", "expert"), None),
            P(("dp", "expert"), None),
            P(None, ("dp", "expert")),
            P(),
            P(("dp", "expert"), None),
            P("expert", None, "dp"),
            P("expert", "dp", None),
            P("expert", None),
            P(),
            P("expert", "dp", None),
        ),
        out_specs=(
            P("expert", "dp", None),
            P("expert", "dp", None),
            P(None, ("dp", "expert"), None),
            P(("dp", "expert"), None),
            P(None, ("dp", "expert")),
            P(),
            P(("dp", "expert"), None),
            P("expert", None, "dp"),
            P("expert", "dp", None),
        ),
        check_vma=False,
    )
```

```python
import functools

import jax
import jax.numpy as jnp
from jax import lax
from jax.experimental import pallas as pl
from jax.experimental.pallas import tpu as pltpu
from jax.sharding import PartitionSpec as P

EPS = 1e-06
SCALE = 0.125
NEG = -1e30
VMEM_LIMIT = 48 * 1024 * 1024
SHORT = pl.CostEstimate(flops=1, bytes_accessed=1, transcendentals=0)
ROWS_BY_ROWS = (((1,), (1,)), ((), ()))
COLS_BY_COLS = (((0,), (0,)), ((), ()))
FIRST_BIT = ((0, 1), (1, 0), (2, 3), (3, 2))
SECOND_BIT = ((0, 2), (2, 0), (1, 3), (3, 1))
PARTNER = tuple((i, i ^ 1) for i in range(8))
NEXT_CHIP = tuple((i, i ^ 2) for i in range(8))
SECOND_CHIP = tuple((i, i ^ 4) for i in range(8))


def norm_forward(values, gain):
    inverse = lax.rsqrt(jnp.mean(values * values, axis=-1, keepdims=True) + EPS)
    return (values * inverse * gain, inverse)


def norm_backward(values, inverse, gain, grad_in):
    scaled = grad_in * gain
    cubed = inverse * inverse * inverse
    return inverse * scaled - values * cubed * jnp.mean(scaled * values, axis=-1, keepdims=True)


def low(values):
    return values.astype(jnp.bfloat16)


def wide(values):
    return values.astype(jnp.float32)


def pass_kernel(*refs):
    pass


def after(value, *others):
    if not others:
        return value
    return pl.pallas_call(
        pass_kernel,
        in_specs=[pl.BlockSpec(memory_space=pl.ANY)] * (1 + len(others)),
        out_specs=pl.BlockSpec(memory_space=pl.ANY),
        out_shape=jax.ShapeDtypeStruct(value.shape, value.dtype),
        input_output_aliases={0: 0},
        cost_estimate=SHORT,
        name="after",
    )(value, *others)


def by_steps():
    return lax.axis_size("dp") == 4 and lax.axis_size("expert") == 8


def dp_order():
    n_dp = lax.axis_size("dp")
    if by_steps():
        me = lax.axis_index("dp")
        return [jnp.bitwise_xor(me, r) for r in range(n_dp)]
    return [jnp.int32(r) for r in range(n_dp)]


def expert_order():
    groups = lax.axis_size("expert")
    if by_steps():
        me = lax.axis_index("expert")
        return [jnp.bitwise_xor(me, 2 * r + p) for p in range(2) for r in range(4)]
    return [jnp.int32(r) for r in range(groups)]


def dp_gather(block):
    if not by_steps():
        full = lax.all_gather(block, "dp")
        return [full[r] for r in range(full.shape[0])]
    half = block.shape[0] // 2
    along = lax.ppermute(block, "dp", FIRST_BIT)
    across = lax.ppermute(block, "dp", SECOND_BIT)
    far_low = lax.ppermute(across[:half], "dp", FIRST_BIT)
    far_high = lax.ppermute(along[half:], "dp", SECOND_BIT)
    return [block, along, across, jnp.concatenate([far_low, far_high], axis=0)]


def dp_gather_pair(first, second, gate=()):
    if not by_steps():
        return dp_gather(first), dp_gather(second), (), ()
    sent = (after(first, *gate), second)
    along = [lax.ppermute(block, "dp", FIRST_BIT) for block in sent]
    across = [lax.ppermute(block, "dp", SECOND_BIT) for block in sent]
    far_first = lax.ppermute(across[0], "dp", FIRST_BIT)
    far_second = lax.ppermute(along[1], "dp", SECOND_BIT)
    return (
        [first, along[0], across[0], far_first],
        [second, along[1], across[1], far_second],
        (along[0], across[0]),
        (along[1], across[1]),
    )


def dp_scatter_pair(first, second):
    if not by_steps():
        return [
            wide(lax.psum_scatter(jnp.stack(parts), "dp", scatter_dimension=0))
            for parts in (first, second)
        ]
    first_far = lax.ppermute(first[3], "dp", FIRST_BIT)
    second_far = lax.ppermute(second[3], "dp", SECOND_BIT)
    first_along = lax.ppermute(first[1], "dp", FIRST_BIT)
    second_across = lax.ppermute(second[2], "dp", SECOND_BIT)
    return first_far, second_far, first_along, second_across


def dp_scatter_pair_end(first, second, received, gate=()):
    if not by_steps():
        return (*received, ())
    first_far, second_far, first_along, second_across = received
    first_sum = after(low(wide(first[2]) + wide(first_far)), *gate)
    first_last = lax.ppermute(first_sum, "dp", SECOND_BIT)
    second_last = lax.ppermute(low(wide(second[1]) + wide(second_far)), "dp", FIRST_BIT)
    return (
        wide(first[0]) + wide(first_along) + wide(first_last),
        wide(second[0]) + wide(second_across) + wide(second_last),
        (first_last, second_last),
    )


def dp_scatter(parts, gate=()):
    if not by_steps():
        return wide(lax.psum_scatter(jnp.stack(parts), "dp", scatter_dimension=0))
    half = parts[0].shape[0] // 2
    low_half, high_half = ([part[rows] for part in parts] for rows in (slice(0, half), slice(half, None)))
    received = dp_scatter_pair(low_half, high_half)
    ends = dp_scatter_pair_end(low_half, high_half, received, gate)
    return jnp.concatenate(ends[:2], axis=0)


def line_gather(block, gates=()):
    near = lax.ppermute(block, "expert", NEXT_CHIP)
    far = lax.ppermute(block, "expert", SECOND_CHIP)
    corner = lax.ppermute(after(far, *gates), "expert", NEXT_CHIP)
    return [block, near, far, corner]


def line_scatter(parts, first_gate=(), second_gate=(), near_gate=()):
    corner = lax.ppermute(after(parts[3], *first_gate), "expert", NEXT_CHIP)
    passed = after(low(wide(parts[2]) + wide(corner)), *second_gate)
    near = lax.ppermute(after(parts[1], *near_gate), "expert", NEXT_CHIP)
    far = lax.ppermute(passed, "expert", SECOND_CHIP)
    return wide(parts[0]) + wide(near) + wide(far), corner, (near, far)


def expert_gather(block, gates=()):
    if not by_steps():
        return lax.all_gather(block, "expert"), ()
    mine = line_gather(block, gates)
    return jnp.stack(mine + [lax.ppermute(piece, "expert", PARTNER) for piece in mine]), mine


def swap_cores(parts, gate=()):
    if not by_steps():
        return parts
    return lax.ppermute(after(parts[4:], *gate), "expert", PARTNER)


def expert_scatter(parts, other, second_gate=(), near_gate=()):
    if not by_steps():
        total = wide(lax.psum_scatter(parts, "expert", scatter_dimension=0))
        return total, total, ()
    merged = [low(wide(parts[r]) + wide(other[r])) for r in range(4)]
    return line_scatter(merged, (), second_gate, near_gate)


def gather_all(shard):
    rows, columns = shard.shape
    if not by_steps():
        return lax.all_gather(shard, ("dp", "expert"), axis=0, tiled=True), (), ()
    place = lax.axis_index("dp")
    odd_first, odd_second = place % 2 == 1, place // 2 == 1
    along = lax.ppermute(shard, "dp", FIRST_BIT)
    near = jnp.where(odd_first, jnp.stack([along, shard]), jnp.stack([shard, along]))
    far = lax.ppermute(near, "dp", SECOND_BIT)
    plane = jnp.where(odd_second, jnp.concatenate([far, near]), jnp.concatenate([near, far]))
    mine = line_gather(plane)
    pieces = mine + [lax.ppermute(piece, "expert", PARTNER) for piece in mine]
    owners = expert_order()
    full = jnp.zeros((4, 8, rows, columns), shard.dtype)
    for index, piece in enumerate(pieces):
        full = lax.dynamic_update_slice_in_dim(full, piece[:, None], owners[index], 1)
    return full.reshape(32 * rows, columns), (far,), mine[3:]


def scatter_all(parts, gates=()):
    if not by_steps():
        return wide(lax.psum_scatter(parts, ("dp", "expert"), scatter_dimension=1, tiled=True))
    count, rows, columns = parts.shape
    blocks = parts.reshape(count, 4, 4, 2, rows // 32, columns)
    me = lax.axis_index("expert")
    chip, core = me // 2, me % 2
    kept, given = (
        lax.dynamic_index_in_dim(blocks, index, 3, keepdims=False) for index in (core, 1 - core)
    )
    merged = low(wide(kept) + wide(lax.ppermute(given, "expert", PARTNER)))
    plane = low(
        dp_scatter(
            [lax.dynamic_index_in_dim(merged, place, 1, keepdims=False) for place in dp_order()],
            gates,
        )
    )
    pieces = [
        lax.dynamic_index_in_dim(plane, jnp.bitwise_xor(chip, r), 1, keepdims=False)
        for r in range(4)
    ]
    return line_scatter(pieces)[0]


def sum_all(values):
    if not by_steps():
        return lax.psum(values, ("dp", "expert"))
    for bit in (1, 2, 4):
        values = values + lax.ppermute(values, "expert", [(i, i ^ bit) for i in range(8)])
    for pairs in (FIRST_BIT, SECOND_BIT):
        values = values + lax.ppermute(values, "dp", pairs)
    return values


def spread_rows(base, span):
    grown = base
    while grown.shape[0] < span:
        grown = jnp.concatenate([grown, pltpu.roll(grown, grown.shape[0], 1)], axis=0)
    return grown[:, span:]


def fold_rows(block, span):
    wide = jnp.concatenate([jnp.zeros_like(block), block], axis=1)
    while wide.shape[0] > 1:
        half = wide.shape[0] // 2
        wide = wide[:half] + pltpu.roll(wide[half:], 2 * span - half, 1)
    return wide


def attention_forward_kernel(
    n_piece, span, head_dim, n_gate, q_ref, k_ref, v_ref, base_ref, start_ref, *refs
):
    out_ref, lse_ref, bias_ref = refs[n_gate:]

    @pl.when(pl.program_id(1) == 0)
    def fill_bias():
        for head in range(2):
            for piece in range(n_piece):
                bias_ref[head, piece] = spread_rows(
                    base_ref[0, head, piece : piece + 1, :], span
                )

    queries = q_ref[0]
    lane_head = lax.broadcasted_iota(jnp.int32, queries.shape, 1) // head_dim
    key_row = lax.broadcasted_iota(jnp.int32, (span, span), 0)
    values_t = [v_ref[0, pl.ds(piece * span, span), :].T for piece in range(n_piece)]
    outs = []
    for head in range(2):
        masked = jnp.where(lane_head == head, queries, jnp.zeros_like(queries))
        scores = []
        highest = None
        for piece in range(n_piece):
            keys = k_ref[0, pl.ds(piece * span, span), :]
            block = lax.dot_general(
                keys, masked, (((1,), (1,)), ((), ())), preferred_element_type=jnp.float32
            )
            block = block + bias_ref[head, piece]
            block = jnp.where(key_row >= start_ref[0, piece : piece + 1, :], block, NEG)
            scores.append(block)
            top = jnp.max(block, axis=0, keepdims=True)
            highest = top if highest is None else jnp.maximum(highest, top)
        total = jnp.zeros_like(highest)
        result = jnp.zeros((head_dim, span), jnp.float32)
        for piece in range(n_piece):
            weights = jnp.exp(scores[piece] - highest)
            total = total + jnp.sum(weights, axis=0, keepdims=True)
            result = result + jnp.dot(
                values_t[piece][head * head_dim : (head + 1) * head_dim],
                weights.astype(jnp.bfloat16),
                preferred_element_type=jnp.float32,
            )
        outs.append(result / total)
        lse_ref[0, 0, head : head + 1, :] = highest + jnp.log(total)
    out_ref[0] = jnp.concatenate(outs, axis=0).T.astype(out_ref.dtype)


def attention_backward_kernel(
    n_piece,
    span,
    head_dim,
    n_gate,
    q_ref,
    k_ref,
    v_ref,
    out_ref,
    grad_ref,
    base_ref,
    start_ref,
    lse_ref,
    *refs,
):
    dq_ref, dk_ref, dv_ref, dist_ref, bias_ref, sum_ref = refs[n_gate:]
    batch = pl.program_id(1)

    @pl.when(batch == 0)
    def fill_bias():
        for head in range(2):
            for piece in range(n_piece):
                bias_ref[head, piece] = spread_rows(
                    base_ref[0, head, piece : piece + 1, :], span
                )
                sum_ref[head, piece] = jnp.zeros((span, span), jnp.float32)

    queries = q_ref[0]
    grads = grad_ref[0]
    product = grads.astype(jnp.float32) * out_ref[0].astype(jnp.float32)
    product_hi = product.astype(jnp.bfloat16)
    product_lo = (product - product_hi.astype(jnp.float32)).astype(jnp.bfloat16)
    lane_head = lax.broadcasted_iota(jnp.int32, queries.shape, 1) // head_dim
    key_row = lax.broadcasted_iota(jnp.int32, (span, span), 0)
    picker = (
        lax.broadcasted_iota(jnp.int32, (8, 2 * head_dim), 1) // head_dim
        == lax.broadcasted_iota(jnp.int32, (8, 2 * head_dim), 0)
    ).astype(jnp.bfloat16)
    rows_by_rows = (((1,), (1,)), ((), ()))
    correction = lax.dot_general(
        picker, product_hi, rows_by_rows, preferred_element_type=jnp.float32
    ) + lax.dot_general(picker, product_lo, rows_by_rows, preferred_element_type=jnp.float32)
    zero = jnp.zeros_like(queries)
    head_queries = [jnp.where(lane_head == head, queries, zero) for head in range(2)]
    head_grads = [jnp.where(lane_head == head, grads, zero) for head in range(2)]
    query_grads = [jnp.zeros((head_dim, span), jnp.float32) for _ in range(2)]
    for piece in range(n_piece):
        rows = pl.ds(piece * span, span)
        keys = k_ref[0, rows, :]
        values = v_ref[0, rows, :]
        keys_t = keys.T
        allowed = key_row >= start_ref[0, piece : piece + 1, :]
        key_grad = jnp.zeros((span, 2 * head_dim), jnp.float32)
        value_grad = jnp.zeros((span, 2 * head_dim), jnp.float32)
        for head in range(2):
            scores = lax.dot_general(
                keys, head_queries[head], rows_by_rows, preferred_element_type=jnp.float32
            )
            scores = jnp.where(allowed, scores + bias_ref[head, piece], NEG)
            probs = jnp.exp(scores - lse_ref[0, 0, head : head + 1, :])
            prob_grad = lax.dot_general(
                values, head_grads[head], rows_by_rows, preferred_element_type=jnp.float32
            )
            score_grad = (probs * (prob_grad - correction[head : head + 1, :])).astype(jnp.bfloat16)
            sum_ref[head, piece] += score_grad.astype(jnp.float32)
            value_grad = value_grad + jnp.dot(
                probs.astype(jnp.bfloat16), head_grads[head], preferred_element_type=jnp.float32
            )
            key_grad = key_grad + jnp.dot(
                score_grad, head_queries[head], preferred_element_type=jnp.float32
            )
            query_grads[head] = query_grads[head] + jnp.dot(
                keys_t[head * head_dim : (head + 1) * head_dim],
                score_grad,
                preferred_element_type=jnp.float32,
            )
        dk_ref[0, rows, :] = key_grad.astype(jnp.bfloat16)
        dv_ref[0, rows, :] = value_grad.astype(jnp.bfloat16)
    dq_ref[0] = (jnp.concatenate(query_grads, axis=0) * SCALE).T.astype(jnp.bfloat16)

    @pl.when(batch == pl.num_programs(1) - 1)
    def fold_distances():
        for head in range(2):
            for piece in range(n_piece):
                dist_ref[0, head, piece : piece + 1, :] = fold_rows(sum_ref[head, piece], span)


def gate_specs(gate):
    return [pl.BlockSpec(memory_space=pl.ANY) for _ in gate]


def attention_specs(n_piece, span, pair):
    n_keys = n_piece * span
    rows = pl.BlockSpec((1, span, pair), lambda h, b: (b, 0, h))
    keys = pl.BlockSpec((1, n_keys, pair), lambda h, b: (b, 0, h))
    base = pl.BlockSpec((1, 2, n_piece, 2 * span), lambda h, b: (h, 0, 0, 0))
    start = pl.BlockSpec((1, n_piece, span), lambda h, b: (b, 0, 0))
    lse = pl.BlockSpec((1, 1, 2, span), lambda h, b: (h, b, 0, 0))
    return rows, keys, base, start, lse


def attention_forward(queries, keys, values, base, start, n_heads, gate=()):
    n_batch, span, inner = queries.shape
    n_piece = keys.shape[1] // span
    head_dim = inner // n_heads
    n_pairs = n_heads // 2
    rows, key_rows, base_spec, start_spec, lse_spec = attention_specs(n_piece, span, 2 * head_dim)
    return pl.pallas_call(
        functools.partial(attention_forward_kernel, n_piece, span, head_dim, len(gate)),
        grid=(n_pairs, n_batch),
        in_specs=[rows, key_rows, key_rows, base_spec, start_spec] + gate_specs(gate),
        out_specs=[rows, lse_spec],
        out_shape=[
            jax.ShapeDtypeStruct(queries.shape, jnp.bfloat16),
            jax.ShapeDtypeStruct((n_pairs, n_batch, 2, span), jnp.float32),
        ],
        scratch_shapes=[pltpu.VMEM((2, n_piece, span, span), jnp.float32)],
        compiler_params=pltpu.CompilerParams(vmem_limit_bytes=VMEM_LIMIT),
        cost_estimate=SHORT,
        name="attention_forward",
    )(queries, keys, values, base, start, *gate)


def attention_backward(
    queries, keys, values, attended, grads, base, start, lse, n_heads, gate=()
):
    n_batch, span, inner = queries.shape
    n_piece = keys.shape[1] // span
    head_dim = inner // n_heads
    n_pairs = n_heads // 2
    rows, key_rows, base_spec, start_spec, lse_spec = attention_specs(n_piece, span, 2 * head_dim)
    return pl.pallas_call(
        functools.partial(attention_backward_kernel, n_piece, span, head_dim, len(gate)),
        grid=(n_pairs, n_batch),
        in_specs=[rows, key_rows, key_rows, rows, rows, base_spec, start_spec, lse_spec]
        + gate_specs(gate),
        out_specs=[rows, key_rows, key_rows, base_spec],
        out_shape=[
            jax.ShapeDtypeStruct(queries.shape, jnp.bfloat16),
            jax.ShapeDtypeStruct(keys.shape, jnp.bfloat16),
            jax.ShapeDtypeStruct(keys.shape, jnp.bfloat16),
            jax.ShapeDtypeStruct((n_pairs, 2, n_piece, 2 * span), jnp.float32),
        ],
        scratch_shapes=[
            pltpu.VMEM((2, n_piece, span, span), jnp.float32),
            pltpu.VMEM((2, n_piece, span, span), jnp.float32),
        ],
        compiler_params=pltpu.CompilerParams(vmem_limit_bytes=VMEM_LIMIT),
        cost_estimate=pl.CostEstimate(
            flops=40 * n_batch * n_heads * span * n_piece * span * head_dim,
            bytes_accessed=12 * keys.size,
            transcendentals=0,
        ),
        name="attention_backward",
    )(queries, keys, values, attended, grads, base, start, lse, *gate)


def bias_base(rel_bias, bucket_ids, offsets, span):
    length = bucket_ids.shape[0]
    hits = wide(bucket_ids[None, :] == jnp.arange(rel_bias.shape[0], dtype=jnp.int32)[:, None])
    table = jnp.dot(rel_bias.T, hits, precision=lax.Precision.HIGHEST)
    padded = jnp.pad(table, ((0, 0), (length, 0)), constant_values=NEG)
    windows = [
        lax.dynamic_slice_in_dim(padded, offset + length - span, 2 * span, 1) for offset in offsets
    ]
    base = jnp.stack(windows, axis=1)
    return base.reshape(base.shape[0] // 2, 2, len(offsets), 2 * span)


def bias_fold(dist, bucket_ids, offsets, n_buckets):
    n_heads, n_piece, span = dist.shape[0] * 2, dist.shape[2], dist.shape[3] // 2
    length = bucket_ids.shape[0]
    sums = dist.reshape(n_heads, n_piece, 2 * span)
    hits = wide(bucket_ids[:, None] == jnp.arange(n_buckets, dtype=jnp.int32)[None, :])
    padded = jnp.pad(hits, ((length, 0), (0, 0)))
    windows = jnp.stack(
        [lax.dynamic_slice_in_dim(padded, offset + length - span, 2 * span, 0) for offset in offsets]
    )
    return jnp.einsum("hpu,pun->nh", sums, windows, precision=lax.Precision.HIGHEST)


def document_starts(doc_lengths, offset, span):
    ends = jnp.cumsum(doc_lengths, axis=-1)
    places = offset + jnp.arange(span, dtype=jnp.int32)
    begun = ends[:, None, :] <= places[None, :, None]
    return jnp.max(jnp.where(begun, ends[:, None, :], 0), axis=-1)


def token_gates(router_t, tokens, routes):
    logits = lax.dot_general(
        router_t, tokens, ROWS_BY_ROWS, preferred_element_type=jnp.float32
    )
    expert = lax.broadcasted_iota(jnp.int32, logits.shape, 0)
    hits = [expert == routes[k : k + 1, :] for k in range(2)]
    chosen = [jnp.sum(jnp.where(hit, logits, 0.0), axis=0, keepdims=True) for hit in hits]
    highest = jnp.maximum(chosen[0], chosen[1])
    raised = [jnp.exp(value - highest) for value in chosen]
    total = raised[0] + raised[1]
    return [value / total for value in raised], hits


def slot_table(slots, n_slots):
    index = lax.broadcasted_iota(jnp.int32, (n_slots, slots.shape[1]), 0)
    return jnp.concatenate(
        [wide(index == slots[e : e + 1, :]) for e in range(slots.shape[0])], axis=0
    )


def dispatch_kernel(
    n_slots, n_gate, token_ref, grad_ref, router_ref, route_ref, slot_ref, first_ref, *refs
):
    in_ref, up_ref, kept_ref, gate_ref = refs[n_gate:]
    tokens = token_ref[0]
    gates, _ = token_gates(router_ref[...], tokens, route_ref[0])
    slots = slot_ref[0]
    table = slot_table(slots, n_slots)
    table_low = low(table)
    local = slots.shape[0]
    picked = jnp.dot(table_low, tokens, preferred_element_type=jnp.float32)
    grads = jnp.dot(table_low, grad_ref[0], preferred_element_type=jnp.float32)
    first = first_ref[0]
    gate_ref[0] = jnp.concatenate(gates, axis=0)
    for e in range(local):
        rows = slice(e * n_slots, (e + 1) * n_slots)
        gate = jnp.where(
            route_ref[0, 0:1, :] == first + e,
            gates[0],
            jnp.where(route_ref[0, 1:2, :] == first + e, gates[1], 0.0),
        )
        slot_gate = jnp.sum(table[rows] * gate, axis=1, keepdims=True)
        in_ref[e] = low(picked[rows])
        kept_ref[e] = low(grads[rows])
        up_ref[e] = low(grads[rows] * slot_gate)


def dispatch(tokens, grads, router_t, routes, slots, first, n_slots, gate=()):
    n_block, span, width = tokens.shape
    local = slots.shape[1]
    block = pl.BlockSpec((1, span, width), lambda b: (b, 0, 0))
    per_device = n_block // grads.shape[0]
    grad_block = pl.BlockSpec((1, span, width), lambda b: (b // per_device, b % per_device, 0))
    rows = pl.BlockSpec((local, n_slots, width), lambda b: (0, b, 0))
    return pl.pallas_call(
        functools.partial(dispatch_kernel, n_slots, len(gate)),
        grid=(n_block,),
        in_specs=[
            block,
            grad_block,
            pl.BlockSpec(router_t.shape, lambda b: (0, 0)),
            pl.BlockSpec((1, 2, span), lambda b: (b, 0, 0)),
            pl.BlockSpec((1, local, span), lambda b: (b, 0, 0)),
            pl.BlockSpec(memory_space=pltpu.SMEM),
        ]
        + gate_specs(gate),
        out_specs=[rows, rows, rows, pl.BlockSpec((1, 2, span), lambda b: (b, 0, 0))],
        out_shape=[jax.ShapeDtypeStruct((local, n_block * n_slots, width), jnp.bfloat16)] * 3
        + [jax.ShapeDtypeStruct((n_block, 2, span), jnp.float32)],
        compiler_params=pltpu.CompilerParams(vmem_limit_bytes=VMEM_LIMIT),
        cost_estimate=SHORT,
        name="dispatch",
    )(tokens, grads, router_t, routes, slots, first, *gate)


def combine_kernel(
    n_slots,
    n_gate,
    in_ref,
    kept_ref,
    gate_ref,
    router_ref,
    route_ref,
    slot_ref,
    first_ref,
    out_ref,
    back_ref,
    *refs,
):
    mixed_ref, sum_ref, router_grad_ref = refs[n_gate:]

    @pl.when(pl.program_id(0) == 0)
    def clear():
        router_grad_ref[...] = jnp.zeros_like(router_grad_ref)

    slots = slot_ref[0]
    local, span = slots.shape
    gates = [gate_ref[0, k : k + 1, :] for k in range(2)]
    expert = lax.broadcasted_iota(jnp.int32, (router_ref.shape[1], span), 0)
    hits = [expert == route_ref[0, k : k + 1, :] for k in range(2)]
    table = slot_table(slots, n_slots)
    table_low = low(table)
    first = first_ref[0]

    def rows_of(ref):
        return jnp.concatenate([ref[e] for e in range(local)], axis=0)

    produced = wide(rows_of(out_ref))
    gate_grad = jnp.sum(wide(rows_of(kept_ref)) * produced, axis=1, keepdims=True)
    spread = (wide(hits[0]) - wide(hits[1])) * (gates[0] * gates[1])
    spread_hi = low(spread)
    spread_lo = low(spread - wide(spread_hi))
    factor = lax.dot_general(
        table_low, spread_hi, ROWS_BY_ROWS, preferred_element_type=jnp.float32
    ) + lax.dot_general(table_low, spread_lo, ROWS_BY_ROWS, preferred_element_type=jnp.float32)
    signs, slot_gates = [], []
    for e in range(local):
        rows = slice(e * n_slots, (e + 1) * n_slots)
        is_first = route_ref[0, 0:1, :] == first + e
        is_second = route_ref[0, 1:2, :] == first + e
        sign = jnp.where(is_first, 1.0, jnp.where(is_second, -1.0, 0.0))
        gate = jnp.where(is_first, gates[0], jnp.where(is_second, gates[1], 0.0))
        signs.append(jnp.sum(table[rows] * sign, axis=1, keepdims=True))
        slot_gates.append(jnp.sum(table[rows] * gate, axis=1, keepdims=True))
    sign, slot_gate = jnp.concatenate(signs, axis=0), jnp.concatenate(slot_gates, axis=0)
    logit_grad = factor * (sign * gate_grad)
    logit_hi = low(logit_grad)
    logit_lo = low(logit_grad - wide(logit_hi))
    back = wide(rows_of(back_ref))
    for part in (logit_hi, logit_lo):
        back = back + lax.dot_general(
            part, router_ref[...], ROWS_BY_ROWS, preferred_element_type=jnp.float32
        )
    mixed_ref[0] = low(
        lax.dot_general(
            table_low,
            low(produced * slot_gate),
            COLS_BY_COLS,
            preferred_element_type=jnp.float32,
        )
    )
    sum_ref[0] = low(
        lax.dot_general(table_low, low(back), COLS_BY_COLS, preferred_element_type=jnp.float32)
    )
    picked = rows_of(in_ref)
    for part in (logit_hi, logit_lo):
        router_grad_ref[...] += lax.dot_general(
            part, picked, COLS_BY_COLS, preferred_element_type=jnp.float32
        )


def combine(inputs, kept, gates, router, routes, slots, first, out, back, n_slots, gate=()):
    n_block, local, span = slots.shape
    width, experts = router.shape
    rows = pl.BlockSpec((local, n_slots, width), lambda b: (0, b, 0))
    block = pl.BlockSpec((1, span, width), lambda b: (b, 0, 0))
    return pl.pallas_call(
        functools.partial(combine_kernel, n_slots, len(gate)),
        grid=(n_block,),
        in_specs=[
            rows,
            rows,
            pl.BlockSpec((1, 2, span), lambda b: (b, 0, 0)),
            pl.BlockSpec(router.shape, lambda b: (0, 0)),
            pl.BlockSpec((1, 2, span), lambda b: (b, 0, 0)),
            pl.BlockSpec((1, local, span), lambda b: (b, 0, 0)),
            pl.BlockSpec(memory_space=pltpu.SMEM),
            rows,
            rows,
        ]
        + gate_specs(gate),
        out_specs=[block, block, pl.BlockSpec((experts, width), lambda b: (0, 0))],
        out_shape=[
            jax.ShapeDtypeStruct((n_block, span, width), jnp.bfloat16),
            jax.ShapeDtypeStruct((n_block, span, width), jnp.bfloat16),
            jax.ShapeDtypeStruct((experts, width), jnp.float32),
        ],
        compiler_params=pltpu.CompilerParams(vmem_limit_bytes=VMEM_LIMIT),
        cost_estimate=SHORT,
        name="combine",
    )(inputs, kept, gates, router, routes, slots, first, out, back, *gate)


def expert_kernel(tile, started, *refs):
    if started:
        x_ref, g_ref, in_ref, down_ref, out_so_far, back_so_far = refs[:6]
        refs = refs[6:]
    else:
        x_ref, g_ref, in_ref, down_ref = refs[:4]
        refs = refs[4:]
    out_ref, back_ref, in_grad_ref, down_grad_ref, x_t, hidden_t, pre_grads = refs
    step = pl.program_id(1)
    rows = pl.ds(pl.multiple_of(step * tile, tile), tile)
    x = x_ref[0, rows, :]
    g = g_ref[0, rows, :]
    pre = jnp.dot(x, in_ref[0], preferred_element_type=jnp.float32)
    hidden_grad = lax.dot_general(
        g, down_ref[0], ROWS_BY_ROWS, preferred_element_type=jnp.float32
    )
    root = 0.7978845608028654
    square = pre * pre
    bent = jnp.tanh(pre * (root + root * 0.044715 * square))
    half = 0.5 + 0.5 * bent
    hidden = low(pre * half)
    slope = half + pre * (half * (1.0 - bent)) * (root + 3.0 * root * 0.044715 * square)
    pre_grad = low(hidden_grad * slope)
    out = jnp.dot(hidden, down_ref[0], preferred_element_type=jnp.float32)
    back = lax.dot_general(
        pre_grad, in_ref[0], ROWS_BY_ROWS, preferred_element_type=jnp.float32
    )
    if started:
        out = out + out_so_far[0]
        back = back + back_so_far[0]
    out_ref[0] = out.astype(out_ref.dtype)
    back_ref[0] = back.astype(back_ref.dtype)
    x_t[:, rows] = x.T
    hidden_t[:, rows] = hidden.T
    pre_grads[rows, :] = pre_grad

    @pl.when(step == pl.num_programs(1) - 1)
    def weight_grads():
        part = 256
        for at in range(0, hidden_t.shape[0], part):
            some = slice(at, min(at + part, hidden_t.shape[0]))
            down_grad_ref[0, some, :] = low(
                jnp.dot(hidden_t[some, :], g_ref[0], preferred_element_type=jnp.float32)
            )
        for at in range(0, x_t.shape[0], part):
            some = slice(at, min(at + part, x_t.shape[0]))
            in_grad_ref[0, some, :] = low(
                jnp.dot(x_t[some, :], pre_grads[...], preferred_element_type=jnp.float32)
            )


def expert_slice(x, g, w_in, w_out, so_far, is_last):
    local, n_rows, width = x.shape
    inner = w_in.shape[2]
    tile = min(n_rows, 1024)
    whole = pl.BlockSpec((1, n_rows, width), lambda e, i: (e, 0, 0))
    up = pl.BlockSpec((1, width, inner), lambda e, i: (e, 0, 0))
    down = pl.BlockSpec((1, inner, width), lambda e, i: (e, 0, 0))
    some = pl.BlockSpec((1, tile, width), lambda e, i: (e, i, 0))
    started = so_far is not None
    kind = jnp.bfloat16 if is_last else jnp.float32
    totals = tuple(so_far) if started else ()
    return pl.pallas_call(
        functools.partial(expert_kernel, tile, started),
        grid=(local, n_rows // tile),
        in_specs=[whole, whole, up, down] + [some] * len(totals),
        out_specs=[some, some, up, down],
        out_shape=[
            jax.ShapeDtypeStruct(x.shape, kind),
            jax.ShapeDtypeStruct(x.shape, kind),
            jax.ShapeDtypeStruct(w_in.shape, jnp.bfloat16),
            jax.ShapeDtypeStruct(w_out.shape, jnp.bfloat16),
        ],
        input_output_aliases={4: 0, 5: 1} if started and not is_last else {},
        scratch_shapes=[
            pltpu.VMEM((width, n_rows), jnp.bfloat16),
            pltpu.VMEM((inner, n_rows), jnp.bfloat16),
            pltpu.VMEM((n_rows, inner), jnp.bfloat16),
        ],
        compiler_params=pltpu.CompilerParams(vmem_limit_bytes=VMEM_LIMIT),
        cost_estimate=SHORT,
        name="expert_slice",
    )(x, g, w_in, w_out, *totals)


def body(
    tokens,
    cotangent,
    qkv_weight,
    out_weight,
    norm_gains,
    rel_bias,
    router_weight,
    w_in,
    w_out,
    doc_lengths,
    bucket_ids,
    routes,
):
    n_batch, n_span, n_width = tokens.shape
    n_rows = n_batch * n_span
    n_buckets, n_heads = rel_bias.shape
    n_inner = qkv_weight.shape[2]
    groups = lax.axis_size("expert")
    local_experts = w_in.shape[0]
    experts_all = local_experts * groups
    n_slots = max(2, 2 * n_span * 2 // experts_all)
    dp_places = dp_order()
    place = lax.axis_index("dp")
    n_dp = len(dp_places)
    offsets = [(place - piece) * n_span for piece in dp_places]
    extra = experts_all + 2
    lanes = -(-extra // 128) * 128
    route_rows = -(-2 * n_rows // n_width // 16) * 16
    packed = jnp.concatenate(
        [qkv_weight[0], qkv_weight[1], qkv_weight[2], out_weight]
        + [router_weight, norm_gains.T, jnp.zeros((out_weight.shape[0], lanes - extra), jnp.bfloat16)],
        axis=1,
    )
    token_pieces = dp_gather(tokens)
    full, full_plane, full_last = gather_all(packed)
    ahead = (*token_pieces[1:3], *full_plane) if by_steps() else ()
    in_pieces, down_pieces, near_in, near_down = dp_gather_pair(w_in, w_out, ahead)
    weights = [full[:, c * n_inner : (c + 1) * n_inner] for c in range(4)]
    router = full[:, 4 * n_inner : 4 * n_inner + experts_all]
    router_t = router.T
    gains = wide(full[:, 4 * n_inner + experts_all : 4 * n_inner + extra].T)
    route_values = low(routes.reshape(n_batch, n_span, 2).transpose(0, 2, 1)).reshape(-1)
    route_values = jnp.pad(route_values, (0, route_rows * n_width - 2 * n_rows))
    grad_rows = jnp.concatenate(
        [cotangent.reshape(n_rows, n_width), route_values.reshape(route_rows, n_width)]
    )
    grad_all, grad_steps = expert_gather(after(grad_rows, *full_last))
    routes_all = grad_all[:, n_rows:].reshape(groups, -1)[:, : 2 * n_rows]
    routes_all = routes_all.astype(jnp.int32).reshape(groups * n_batch, 2, n_span)
    first = lax.axis_index("expert").astype(jnp.int32) * local_experts
    mine = first + jnp.arange(local_experts, dtype=jnp.int32)
    member = jnp.any(routes_all[:, None] == mine[None, :, None, None], axis=2)
    before = wide(jnp.arange(n_span)[:, None] < jnp.arange(n_span)[None, :])
    ranks = jnp.einsum(
        "bet,tu->beu", low(member), low(before), preferred_element_type=jnp.float32
    ).astype(jnp.int32)
    slots = jnp.where(member, ranks, -1)
    first = first[None]

    base = bias_base(rel_bias, bucket_ids, offsets, n_span)
    begin = document_starts(doc_lengths, place * n_span, n_span)
    starts = jnp.stack([begin - piece * n_span for piece in dp_places], axis=1)

    normed1_all = jnp.stack(
        [low(norm_forward(wide(piece), gains[0])[0]) for piece in token_pieces], axis=1
    )
    normed1_all = normed1_all.reshape(n_batch, n_dp * n_span, n_width)
    flat_normed1 = normed1_all.reshape(-1, n_width)
    normed1 = normed1_all[:, :n_span] if by_steps() else lax.dynamic_slice_in_dim(
        normed1_all, place * n_span, n_span, 1
    )
    normed1 = normed1.reshape(n_rows, n_width)
    queries = low(low(jnp.dot(normed1, weights[0], preferred_element_type=jnp.float32)) * SCALE)
    queries = queries.reshape(n_batch, n_span, n_inner)
    keys, values = (
        low(jnp.dot(flat_normed1, weights[c], preferred_element_type=jnp.float32)).reshape(
            n_batch, -1, n_inner
        )
        for c in (1, 2)
    )
    attended_rows, log_total = attention_forward(
        queries, keys, values, base, starts, n_heads, (*near_in, *grad_steps[1:3])
    )
    attended = attended_rows.reshape(n_rows, n_inner)
    inputs = wide(tokens.reshape(n_rows, n_width))
    resid = inputs + jnp.dot(attended, weights[3], preferred_element_type=jnp.float32)
    normed2, inverse2 = norm_forward(resid, gains[1])
    normed2_low = low(normed2).reshape(n_batch, n_span, n_width)
    normed2_low = after(normed2_low, *grad_steps[3:])
    token_all = expert_gather(normed2_low, near_down)[0]
    token_all = token_all.reshape(groups * n_batch, n_span, n_width)
    expert_in, expert_up, expert_kept, gates = dispatch(
        token_all,
        grad_all,
        router_t,
        routes_all,
        slots,
        first,
        n_slots,
        (*in_pieces[1:], *down_pieces[1:]),
    )
    so_far = None
    in_grads, down_grads = {}, {}
    for r in (*range(n_dp - 1, 3, -1), 3, 1, 2, 0):
        *so_far, in_grads[r], down_grads[r] = expert_slice(
            expert_in, expert_up, in_pieces[r], down_pieces[r], so_far, r == 0
        )
    in_grads, down_grads = ([grads[r] for r in range(n_dp)] for grads in (in_grads, down_grads))
    piece_shape = (groups, n_batch, n_span, n_width)
    received = dp_scatter_pair(in_grads, down_grads)
    in_share, down_share, last = dp_scatter_pair_end(in_grads, down_grads, received)
    mixed_all, back_all, router_grad = combine(
        expert_in,
        expert_kept,
        gates,
        router,
        routes_all,
        slots,
        first,
        *so_far,
        n_slots,
        received[:2] if last else (),
    )
    back_all = back_all.reshape(piece_shape)
    back_other = swap_cores(back_all, received[2:] if last else ())
    normed2_grad, back_corner, _ = expert_scatter(back_all, back_other)
    normed2_grad = normed2_grad.reshape(n_rows, n_width)
    mixed_all = after(mixed_all.reshape(piece_shape), back_corner)
    mixed_other = swap_cores(mixed_all)
    gain2_grad = jnp.sum(normed2_grad * resid * inverse2, axis=0)
    grad_out = wide(cotangent.reshape(n_rows, n_width))
    resid_grad = grad_out + norm_backward(resid, inverse2, gains[1], normed2_grad)
    branch_low = low(resid_grad)
    attended_grad = low(
        lax.dot_general(branch_low, weights[3], ROWS_BY_ROWS, preferred_element_type=jnp.float32)
    )
    query_grad, key_grad, value_grad, dist_grad = attention_backward(
        queries,
        keys,
        values,
        attended_rows,
        attended_grad.reshape(n_batch, n_span, n_inner),
        base,
        starts,
        log_total,
        n_heads,
        (*last, mixed_other),
    )
    bias_grad = bias_fold(dist_grad, bucket_ids, offsets, n_buckets)
    mixed, mixed_corner, mixed_last = expert_scatter(
        mixed_all, mixed_other, (dist_grad,), (dist_grad,)
    )
    block_out = low(resid + mixed.reshape(n_rows, n_width)).reshape(n_batch, n_span, n_width)
    query_grad = query_grad.reshape(n_rows, n_inner)
    key_grad = key_grad.reshape(-1, n_inner)
    value_grad = value_grad.reshape(-1, n_inner)
    own_part = lax.dot_general(
        query_grad, weights[0], ROWS_BY_ROWS, preferred_element_type=jnp.float32
    )
    all_part = lax.dot_general(
        key_grad, weights[1], ROWS_BY_ROWS, preferred_element_type=jnp.float32
    ) + lax.dot_general(value_grad, weights[2], ROWS_BY_ROWS, preferred_element_type=jnp.float32)
    all_part = all_part.reshape(n_batch, n_dp, n_span, n_width)
    sent = low(all_part)
    shared = dp_scatter([sent[:, r] for r in range(n_dp)])
    normed1_grad = own_part + shared.reshape(n_rows, n_width)
    inverse1 = lax.rsqrt(jnp.mean(inputs * inputs, axis=-1, keepdims=True) + EPS)
    tokens_grad = resid_grad + norm_backward(inputs, inverse1, gains[0], normed1_grad)
    def rows_grad(rows, grads):
        return low(
            lax.dot_general(rows, grads, COLS_BY_COLS, preferred_element_type=jnp.float32)
        )

    weight_grads = jnp.stack(
        [
            rows_grad(normed1, query_grad),
            rows_grad(flat_normed1, key_grad),
            rows_grad(flat_normed1, value_grad),
            rows_grad(attended, branch_low),
        ]
    )
    weight_grads = after(weight_grads, mixed_corner)
    gain1_grad = (
        sum(jnp.sum(wide(weight_grads[c]) * wide(weights[c]), axis=1) for c in range(3)) / gains[0]
    )
    shares = scatter_all(weight_grads, mixed_last)
    small_rows = experts_all + 2
    bias_flat = jnp.pad(bias_grad.reshape(1, -1), ((0, 0), (0, n_width - bias_grad.size)))
    small = sum_all(
        jnp.concatenate([router_grad, gain1_grad[None], gain2_grad[None], bias_flat])
    )
    rel_bias_grad = small[small_rows, : bias_grad.size].reshape(bias_grad.shape)
    n_own = router_weight.shape[0]
    own = lax.dynamic_slice_in_dim(
        small, (place * groups + lax.axis_index("expert")) * n_own, n_own, 1
    )
    router_share = own[:experts_all].T
    gains_share = own[experts_all:small_rows]
    qkv_share, out_share = shares[:3], shares[3]
    return (
        block_out,
        tokens_grad.reshape(n_batch, n_span, n_width),
        qkv_share,
        out_share,
        gains_share,
        rel_bias_grad,
        router_share,
        in_share,
        down_share,
    )


def solution(mesh):
    return jax.shard_map(
        body,
        mesh=mesh,
        in_specs=(
            P("expert", "dp", None),
            P("expert", "dp", None),
            P(None, ("dp", "expert"), None),
            P(("dp", "expert"), None),
            P(None, ("dp", "expert")),
            P(),
            P(("dp", "expert"), None),
            P("expert", None, "dp"),
            P("expert", "dp", None),
            P("expert", None),
            P(),
            P("expert", "dp", None),
        ),
        out_specs=(
            P("expert", "dp", None),
            P("expert", "dp", None),
            P(None, ("dp", "expert"), None),
            P(("dp", "expert"), None),
            P(None, ("dp", "expert")),
            P(),
            P(("dp", "expert"), None),
            P("expert", None, "dp"),
            P("expert", "dp", None),
        ),
        check_vma=False,
    )
```

```python
import functools

import jax
import jax.numpy as jnp
from jax import lax
from jax.experimental import pallas as pl
from jax.experimental.pallas import tpu as pltpu
from jax.sharding import PartitionSpec as P

EPS = 1e-06
SCALE = 0.125
NEG = -1e30
VMEM_LIMIT = 48 * 1024 * 1024
SHORT = pl.CostEstimate(flops=1, bytes_accessed=1, transcendentals=0)
ROWS_BY_ROWS = (((1,), (1,)), ((), ()))
COLS_BY_COLS = (((0,), (0,)), ((), ()))
FIRST_BIT = ((0, 1), (1, 0), (2, 3), (3, 2))
SECOND_BIT = ((0, 2), (2, 0), (1, 3), (3, 1))
PARTNER = tuple((i, i ^ 1) for i in range(8))
NEXT_CHIP = tuple((i, i ^ 2) for i in range(8))
SECOND_CHIP = tuple((i, i ^ 4) for i in range(8))


def norm_forward(values, gain):
    inverse = lax.rsqrt(jnp.mean(values * values, axis=-1, keepdims=True) + EPS)
    return (values * inverse * gain, inverse)


def norm_backward(values, inverse, gain, grad_in):
    scaled = grad_in * gain
    cubed = inverse * inverse * inverse
    return inverse * scaled - values * cubed * jnp.mean(scaled * values, axis=-1, keepdims=True)


def low(values):
    return values.astype(jnp.bfloat16)


def wide(values):
    return values.astype(jnp.float32)


def pass_kernel(*refs):
    pass


def after(value, *others):
    if not others:
        return value
    return pl.pallas_call(
        pass_kernel,
        in_specs=[pl.BlockSpec(memory_space=pl.ANY)] * (1 + len(others)),
        out_specs=pl.BlockSpec(memory_space=pl.ANY),
        out_shape=jax.ShapeDtypeStruct(value.shape, value.dtype),
        input_output_aliases={0: 0},
        cost_estimate=SHORT,
        name="after",
    )(value, *others)


def by_steps():
    return lax.axis_size("dp") == 4 and lax.axis_size("expert") == 8


def dp_order():
    n_dp = lax.axis_size("dp")
    if by_steps():
        me = lax.axis_index("dp")
        return [jnp.bitwise_xor(me, r) for r in range(n_dp)]
    return [jnp.int32(r) for r in range(n_dp)]


def expert_order():
    groups = lax.axis_size("expert")
    if by_steps():
        me = lax.axis_index("expert")
        return [jnp.bitwise_xor(me, 2 * r + p) for p in range(2) for r in range(4)]
    return [jnp.int32(r) for r in range(groups)]


def dp_gather(block):
    if not by_steps():
        full = lax.all_gather(block, "dp")
        return [full[r] for r in range(full.shape[0])]
    half = block.shape[0] // 2
    along = lax.ppermute(block, "dp", FIRST_BIT)
    across = lax.ppermute(block, "dp", SECOND_BIT)
    far_low = lax.ppermute(across[:half], "dp", FIRST_BIT)
    far_high = lax.ppermute(along[half:], "dp", SECOND_BIT)
    return [block, along, across, jnp.concatenate([far_low, far_high], axis=0)]


def dp_gather_pair(first, second, gate=()):
    if not by_steps():
        return dp_gather(first), dp_gather(second), (), ()
    sent = (after(first, *gate), second)
    along = [lax.ppermute(block, "dp", FIRST_BIT) for block in sent]
    across = [lax.ppermute(block, "dp", SECOND_BIT) for block in sent]
    far_first = lax.ppermute(across[0], "dp", FIRST_BIT)
    far_second = lax.ppermute(along[1], "dp", SECOND_BIT)
    return (
        [first, along[0], across[0], far_first],
        [second, along[1], across[1], far_second],
        (along[0], across[0]),
        (along[1], across[1]),
    )


def dp_scatter_pair(first, second):
    if not by_steps():
        return [
            wide(lax.psum_scatter(jnp.stack(parts), "dp", scatter_dimension=0))
            for parts in (first, second)
        ]
    first_far = lax.ppermute(first[3], "dp", FIRST_BIT)
    second_far = lax.ppermute(second[3], "dp", SECOND_BIT)
    first_along = lax.ppermute(first[1], "dp", FIRST_BIT)
    second_across = lax.ppermute(second[2], "dp", SECOND_BIT)
    return first_far, second_far, first_along, second_across


def dp_scatter_pair_end(first, second, received, gate=()):
    if not by_steps():
        return (*received, ())
    first_far, second_far, first_along, second_across = received
    first_sum = after(low(wide(first[2]) + wide(first_far)), *gate)
    first_last = lax.ppermute(first_sum, "dp", SECOND_BIT)
    second_last = lax.ppermute(low(wide(second[1]) + wide(second_far)), "dp", FIRST_BIT)
    return (
        wide(first[0]) + wide(first_along) + wide(first_last),
        wide(second[0]) + wide(second_across) + wide(second_last),
        (first_last, second_last),
    )


def dp_scatter(parts, gate=()):
    if not by_steps():
        return wide(lax.psum_scatter(jnp.stack(parts), "dp", scatter_dimension=0))
    half = parts[0].shape[0] // 2
    low_half, high_half = ([part[rows] for part in parts] for rows in (slice(0, half), slice(half, None)))
    received = dp_scatter_pair(low_half, high_half)
    ends = dp_scatter_pair_end(low_half, high_half, received, gate)
    return jnp.concatenate(ends[:2], axis=0)


def line_gather(block, gates=()):
    near = lax.ppermute(block, "expert", NEXT_CHIP)
    far = lax.ppermute(block, "expert", SECOND_CHIP)
    corner = lax.ppermute(after(far, *gates), "expert", NEXT_CHIP)
    return [block, near, far, corner]


def line_scatter(parts, first_gate=(), second_gate=(), near_gate=()):
    corner = lax.ppermute(after(parts[3], *first_gate), "expert", NEXT_CHIP)
    passed = after(low(wide(parts[2]) + wide(corner)), *second_gate)
    near = lax.ppermute(after(parts[1], *near_gate), "expert", NEXT_CHIP)
    far = lax.ppermute(passed, "expert", SECOND_CHIP)
    return wide(parts[0]) + wide(near) + wide(far), corner, (near, far)


def expert_gather(block, gates=(), last_gates=()):
    if not by_steps():
        return lax.all_gather(block, "expert"), ()
    mine = line_gather(block, gates)
    mine[3] = after(mine[3], *last_gates)
    return jnp.stack(mine + [lax.ppermute(piece, "expert", PARTNER) for piece in mine]), mine


def swap_cores(given, gate=()):
    if not by_steps():
        return given
    return lax.ppermute(after(given, *gate), "expert", PARTNER)


def expert_scatter(kept, other, second_gate=(), near_gate=()):
    if not by_steps():
        parts = jnp.concatenate([kept, other])
        total = wide(lax.psum_scatter(parts, "expert", scatter_dimension=0))
        return total, total, ()
    merged = [low(wide(kept[r]) + wide(other[r])) for r in range(4)]
    return line_scatter(merged, (), second_gate, near_gate)


def gather_all(shard):
    rows, columns = shard.shape
    if not by_steps():
        return lax.all_gather(shard, ("dp", "expert"), axis=0, tiled=True), (), ()
    place = lax.axis_index("dp")
    odd_first, odd_second = place % 2 == 1, place // 2 == 1
    along = lax.ppermute(shard, "dp", FIRST_BIT)
    near = jnp.where(odd_first, jnp.stack([along, shard]), jnp.stack([shard, along]))
    far = lax.ppermute(near, "dp", SECOND_BIT)
    plane = jnp.where(odd_second, jnp.concatenate([far, near]), jnp.concatenate([near, far]))
    mine = line_gather(plane)
    pieces = mine + [lax.ppermute(piece, "expert", PARTNER) for piece in mine]
    owners = expert_order()
    full = jnp.zeros((4, 8, rows, columns), shard.dtype)
    for index, piece in enumerate(pieces):
        full = lax.dynamic_update_slice_in_dim(full, piece[:, None], owners[index], 1)
    return full.reshape(32 * rows, columns), (far,), mine[3:]


def scatter_all(parts, gates=()):
    if not by_steps():
        return wide(lax.psum_scatter(parts, ("dp", "expert"), scatter_dimension=1, tiled=True))
    count, rows, columns = parts.shape
    blocks = parts.reshape(count, 4, 4, 2, rows // 32, columns)
    me = lax.axis_index("expert")
    chip, core = me // 2, me % 2
    kept, given = (
        lax.dynamic_index_in_dim(blocks, index, 3, keepdims=False) for index in (core, 1 - core)
    )
    merged = low(wide(kept) + wide(lax.ppermute(given, "expert", PARTNER)))
    plane = low(
        dp_scatter(
            [lax.dynamic_index_in_dim(merged, place, 1, keepdims=False) for place in dp_order()],
            gates,
        )
    )
    pieces = [
        lax.dynamic_index_in_dim(plane, jnp.bitwise_xor(chip, r), 1, keepdims=False)
        for r in range(4)
    ]
    return line_scatter(pieces)[0]


def sum_all(values):
    if not by_steps():
        return lax.psum(values, ("dp", "expert"))
    for bit in (1, 2, 4):
        values = values + lax.ppermute(values, "expert", [(i, i ^ bit) for i in range(8)])
    for pairs in (FIRST_BIT, SECOND_BIT):
        values = values + lax.ppermute(values, "dp", pairs)
    return values


def spread_rows(base, span):
    grown = base
    while grown.shape[0] < span:
        grown = jnp.concatenate([grown, pltpu.roll(grown, grown.shape[0], 1)], axis=0)
    return grown[:, span:]


def fold_rows(block, span):
    wide = jnp.concatenate([jnp.zeros_like(block), block], axis=1)
    while wide.shape[0] > 1:
        half = wide.shape[0] // 2
        wide = wide[:half] + pltpu.roll(wide[half:], 2 * span - half, 1)
    return wide


def attention_forward_kernel(
    n_piece, span, head_dim, n_gate, q_ref, k_ref, v_ref, base_ref, start_ref, *refs
):
    out_ref, lse_ref, bias_ref = refs[n_gate:]

    @pl.when(pl.program_id(1) == 0)
    def fill_bias():
        for head in range(2):
            for piece in range(n_piece):
                bias_ref[head, piece] = spread_rows(
                    base_ref[0, head, piece : piece + 1, :], span
                )

    queries = q_ref[0]
    lane_head = lax.broadcasted_iota(jnp.int32, queries.shape, 1) // head_dim
    key_row = lax.broadcasted_iota(jnp.int32, (span, span), 0)
    values_t = [v_ref[0, pl.ds(piece * span, span), :].T for piece in range(n_piece)]
    outs = []
    for head in range(2):
        masked = jnp.where(lane_head == head, queries, jnp.zeros_like(queries))
        scores = []
        highest = None
        for piece in range(n_piece):
            keys = k_ref[0, pl.ds(piece * span, span), :]
            block = lax.dot_general(
                keys, masked, (((1,), (1,)), ((), ())), preferred_element_type=jnp.float32
            )
            block = block + bias_ref[head, piece]
            block = jnp.where(key_row >= start_ref[0, piece : piece + 1, :], block, NEG)
            scores.append(block)
            top = jnp.max(block, axis=0, keepdims=True)
            highest = top if highest is None else jnp.maximum(highest, top)
        total = jnp.zeros_like(highest)
        result = jnp.zeros((head_dim, span), jnp.float32)
        for piece in range(n_piece):
            weights = jnp.exp(scores[piece] - highest)
            total = total + jnp.sum(weights, axis=0, keepdims=True)
            result = result + jnp.dot(
                values_t[piece][head * head_dim : (head + 1) * head_dim],
                weights.astype(jnp.bfloat16),
                preferred_element_type=jnp.float32,
            )
        outs.append(result / total)
        lse_ref[0, 0, head : head + 1, :] = highest + jnp.log(total)
    out_ref[0] = jnp.concatenate(outs, axis=0).T.astype(out_ref.dtype)


def attention_backward_kernel(
    n_piece,
    span,
    head_dim,
    n_gate,
    q_ref,
    k_ref,
    v_ref,
    out_ref,
    grad_ref,
    base_ref,
    start_ref,
    lse_ref,
    *refs,
):
    dq_ref, dk_ref, dv_ref, dist_ref, bias_ref, sum_ref = refs[n_gate:]
    batch = pl.program_id(1)

    @pl.when(batch == 0)
    def fill_bias():
        for head in range(2):
            for piece in range(n_piece):
                bias_ref[head, piece] = spread_rows(
                    base_ref[0, head, piece : piece + 1, :], span
                )
                sum_ref[head, piece] = jnp.zeros((span, span), jnp.float32)

    queries = q_ref[0]
    grads = grad_ref[0]
    product = grads.astype(jnp.float32) * out_ref[0].astype(jnp.float32)
    product_hi = product.astype(jnp.bfloat16)
    product_lo = (product - product_hi.astype(jnp.float32)).astype(jnp.bfloat16)
    lane_head = lax.broadcasted_iota(jnp.int32, queries.shape, 1) // head_dim
    key_row = lax.broadcasted_iota(jnp.int32, (span, span), 0)
    picker = (
        lax.broadcasted_iota(jnp.int32, (8, 2 * head_dim), 1) // head_dim
        == lax.broadcasted_iota(jnp.int32, (8, 2 * head_dim), 0)
    ).astype(jnp.bfloat16)
    rows_by_rows = (((1,), (1,)), ((), ()))
    correction = lax.dot_general(
        picker, product_hi, rows_by_rows, preferred_element_type=jnp.float32
    ) + lax.dot_general(picker, product_lo, rows_by_rows, preferred_element_type=jnp.float32)
    zero = jnp.zeros_like(queries)
    head_queries = [jnp.where(lane_head == head, queries, zero) for head in range(2)]
    head_grads = [jnp.where(lane_head == head, grads, zero) for head in range(2)]
    query_grads = [jnp.zeros((head_dim, span), jnp.float32) for _ in range(2)]
    for piece in range(n_piece):
        rows = pl.ds(piece * span, span)
        keys = k_ref[0, rows, :]
        values = v_ref[0, rows, :]
        keys_t = keys.T
        allowed = key_row >= start_ref[0, piece : piece + 1, :]
        key_grad = jnp.zeros((span, 2 * head_dim), jnp.float32)
        value_grad = jnp.zeros((span, 2 * head_dim), jnp.float32)
        for head in range(2):
            scores = lax.dot_general(
                keys, head_queries[head], rows_by_rows, preferred_element_type=jnp.float32
            )
            scores = jnp.where(allowed, scores + bias_ref[head, piece], NEG)
            probs = jnp.exp(scores - lse_ref[0, 0, head : head + 1, :])
            prob_grad = lax.dot_general(
                values, head_grads[head], rows_by_rows, preferred_element_type=jnp.float32
            )
            score_grad = (probs * (prob_grad - correction[head : head + 1, :])).astype(jnp.bfloat16)
            sum_ref[head, piece] += score_grad.astype(jnp.float32)
            value_grad = value_grad + jnp.dot(
                probs.astype(jnp.bfloat16), head_grads[head], preferred_element_type=jnp.float32
            )
            key_grad = key_grad + jnp.dot(
                score_grad, head_queries[head], preferred_element_type=jnp.float32
            )
            query_grads[head] = query_grads[head] + jnp.dot(
                keys_t[head * head_dim : (head + 1) * head_dim],
                score_grad,
                preferred_element_type=jnp.float32,
            )
        dk_ref[0, rows, :] = key_grad.astype(jnp.bfloat16)
        dv_ref[0, rows, :] = value_grad.astype(jnp.bfloat16)
    dq_ref[0] = (jnp.concatenate(query_grads, axis=0) * SCALE).T.astype(jnp.bfloat16)

    @pl.when(batch == pl.num_programs(1) - 1)
    def fold_distances():
        for head in range(2):
            for piece in range(n_piece):
                dist_ref[0, head, piece : piece + 1, :] = fold_rows(sum_ref[head, piece], span)


def gate_specs(gate):
    return [pl.BlockSpec(memory_space=pl.ANY) for _ in gate]


def attention_specs(n_piece, span, pair):
    n_keys = n_piece * span
    rows = pl.BlockSpec((1, span, pair), lambda h, b: (b, 0, h))
    keys = pl.BlockSpec((1, n_keys, pair), lambda h, b: (b, 0, h))
    base = pl.BlockSpec((1, 2, n_piece, 2 * span), lambda h, b: (h, 0, 0, 0))
    start = pl.BlockSpec((1, n_piece, span), lambda h, b: (b, 0, 0))
    lse = pl.BlockSpec((1, 1, 2, span), lambda h, b: (h, b, 0, 0))
    return rows, keys, base, start, lse


def attention_forward(queries, keys, values, base, start, n_heads, gate=()):
    n_batch, span, inner = queries.shape
    n_piece = keys.shape[1] // span
    head_dim = inner // n_heads
    n_pairs = n_heads // 2
    rows, key_rows, base_spec, start_spec, lse_spec = attention_specs(n_piece, span, 2 * head_dim)
    return pl.pallas_call(
        functools.partial(attention_forward_kernel, n_piece, span, head_dim, len(gate)),
        grid=(n_pairs, n_batch),
        in_specs=[rows, key_rows, key_rows, base_spec, start_spec] + gate_specs(gate),
        out_specs=[rows, lse_spec],
        out_shape=[
            jax.ShapeDtypeStruct(queries.shape, jnp.bfloat16),
            jax.ShapeDtypeStruct((n_pairs, n_batch, 2, span), jnp.float32),
        ],
        scratch_shapes=[pltpu.VMEM((2, n_piece, span, span), jnp.float32)],
        compiler_params=pltpu.CompilerParams(vmem_limit_bytes=VMEM_LIMIT),
        cost_estimate=SHORT,
        name="attention_forward",
    )(queries, keys, values, base, start, *gate)


def attention_backward(
    queries, keys, values, attended, grads, base, start, lse, n_heads, gate=()
):
    n_batch, span, inner = queries.shape
    n_piece = keys.shape[1] // span
    head_dim = inner // n_heads
    n_pairs = n_heads // 2
    rows, key_rows, base_spec, start_spec, lse_spec = attention_specs(n_piece, span, 2 * head_dim)
    return pl.pallas_call(
        functools.partial(attention_backward_kernel, n_piece, span, head_dim, len(gate)),
        grid=(n_pairs, n_batch),
        in_specs=[rows, key_rows, key_rows, rows, rows, base_spec, start_spec, lse_spec]
        + gate_specs(gate),
        out_specs=[rows, key_rows, key_rows, base_spec],
        out_shape=[
            jax.ShapeDtypeStruct(queries.shape, jnp.bfloat16),
            jax.ShapeDtypeStruct(keys.shape, jnp.bfloat16),
            jax.ShapeDtypeStruct(keys.shape, jnp.bfloat16),
            jax.ShapeDtypeStruct((n_pairs, 2, n_piece, 2 * span), jnp.float32),
        ],
        scratch_shapes=[
            pltpu.VMEM((2, n_piece, span, span), jnp.float32),
            pltpu.VMEM((2, n_piece, span, span), jnp.float32),
        ],
        compiler_params=pltpu.CompilerParams(vmem_limit_bytes=VMEM_LIMIT),
        cost_estimate=pl.CostEstimate(
            flops=40 * n_batch * n_heads * span * n_piece * span * head_dim,
            bytes_accessed=12 * keys.size,
            transcendentals=0,
        ),
        name="attention_backward",
    )(queries, keys, values, attended, grads, base, start, lse, *gate)


def bias_base(rel_bias, bucket_ids, offsets, span):
    length = bucket_ids.shape[0]
    hits = wide(bucket_ids[None, :] == jnp.arange(rel_bias.shape[0], dtype=jnp.int32)[:, None])
    table = jnp.dot(rel_bias.T, hits, precision=lax.Precision.HIGHEST)
    padded = jnp.pad(table, ((0, 0), (length, 0)), constant_values=NEG)
    windows = [
        lax.dynamic_slice_in_dim(padded, offset + length - span, 2 * span, 1) for offset in offsets
    ]
    base = jnp.stack(windows, axis=1)
    return base.reshape(base.shape[0] // 2, 2, len(offsets), 2 * span)


def bias_fold(dist, bucket_ids, offsets, n_buckets):
    n_heads, n_piece, span = dist.shape[0] * 2, dist.shape[2], dist.shape[3] // 2
    length = bucket_ids.shape[0]
    sums = dist.reshape(n_heads, n_piece, 2 * span)
    hits = wide(bucket_ids[:, None] == jnp.arange(n_buckets, dtype=jnp.int32)[None, :])
    padded = jnp.pad(hits, ((length, 0), (0, 0)))
    windows = jnp.stack(
        [lax.dynamic_slice_in_dim(padded, offset + length - span, 2 * span, 0) for offset in offsets]
    )
    return jnp.einsum("hpu,pun->nh", sums, windows, precision=lax.Precision.HIGHEST)


def document_starts(doc_lengths, offset, span):
    ends = jnp.cumsum(doc_lengths, axis=-1)
    places = offset + jnp.arange(span, dtype=jnp.int32)
    begun = ends[:, None, :] <= places[None, :, None]
    return jnp.max(jnp.where(begun, ends[:, None, :], 0), axis=-1)


def token_gates(router_t, tokens, routes):
    logits = lax.dot_general(
        router_t, tokens, ROWS_BY_ROWS, preferred_element_type=jnp.float32
    )
    expert = lax.broadcasted_iota(jnp.int32, logits.shape, 0)
    hits = [expert == routes[k : k + 1, :] for k in range(2)]
    chosen = [jnp.sum(jnp.where(hit, logits, 0.0), axis=0, keepdims=True) for hit in hits]
    highest = jnp.maximum(chosen[0], chosen[1])
    raised = [jnp.exp(value - highest) for value in chosen]
    total = raised[0] + raised[1]
    return [value / total for value in raised], hits


def slot_table(slots, n_slots):
    index = lax.broadcasted_iota(jnp.int32, (n_slots, slots.shape[1]), 0)
    return jnp.concatenate(
        [wide(index == slots[e : e + 1, :]) for e in range(slots.shape[0])], axis=0
    )


def dispatch_kernel(
    n_slots, n_gate, token_ref, grad_ref, router_ref, route_ref, slot_ref, first_ref, *refs
):
    in_ref, up_ref, kept_ref, gate_ref = refs[n_gate:]
    tokens = token_ref[0]
    gates, _ = token_gates(router_ref[...], tokens, route_ref[0])
    slots = slot_ref[0]
    table = slot_table(slots, n_slots)
    table_low = low(table)
    local = slots.shape[0]
    picked = jnp.dot(table_low, tokens, preferred_element_type=jnp.float32)
    grads = jnp.dot(table_low, grad_ref[0], preferred_element_type=jnp.float32)
    first = first_ref[0]
    gate_ref[0] = jnp.concatenate(gates, axis=0)
    for e in range(local):
        rows = slice(e * n_slots, (e + 1) * n_slots)
        gate = jnp.where(
            route_ref[0, 0:1, :] == first + e,
            gates[0],
            jnp.where(route_ref[0, 1:2, :] == first + e, gates[1], 0.0),
        )
        slot_gate = jnp.sum(table[rows] * gate, axis=1, keepdims=True)
        in_ref[e] = low(picked[rows])
        kept_ref[e] = low(grads[rows])
        up_ref[e] = low(grads[rows] * slot_gate)


def dispatch(tokens, grads, router_t, routes, slots, first, n_slots, gate=()):
    n_block, span, width = tokens.shape
    local = slots.shape[1]
    block = pl.BlockSpec((1, span, width), lambda b: (b, 0, 0))
    per_device = n_block // grads.shape[0]
    grad_block = pl.BlockSpec((1, span, width), lambda b: (b // per_device, b % per_device, 0))
    rows = pl.BlockSpec((local, n_slots, width), lambda b: (0, b, 0))
    return pl.pallas_call(
        functools.partial(dispatch_kernel, n_slots, len(gate)),
        grid=(n_block,),
        in_specs=[
            block,
            grad_block,
            pl.BlockSpec(router_t.shape, lambda b: (0, 0)),
            pl.BlockSpec((1, 2, span), lambda b: (b, 0, 0)),
            pl.BlockSpec((1, local, span), lambda b: (b, 0, 0)),
            pl.BlockSpec(memory_space=pltpu.SMEM),
        ]
        + gate_specs(gate),
        out_specs=[rows, rows, rows, pl.BlockSpec((1, 2, span), lambda b: (b, 0, 0))],
        out_shape=[jax.ShapeDtypeStruct((local, n_block * n_slots, width), jnp.bfloat16)] * 3
        + [jax.ShapeDtypeStruct((n_block, 2, span), jnp.float32)],
        compiler_params=pltpu.CompilerParams(vmem_limit_bytes=VMEM_LIMIT),
        cost_estimate=SHORT,
        name="dispatch",
    )(tokens, grads, router_t, routes, slots, first, *gate)


def combine_kernel(
    n_slots,
    n_gate,
    in_ref,
    kept_ref,
    gate_ref,
    router_ref,
    route_ref,
    slot_ref,
    first_ref,
    out_ref,
    back_ref,
    *refs,
):
    mixed_refs, sum_refs, router_grad_ref = refs[n_gate:][:2], refs[n_gate:][2:4], refs[-1]
    half = pl.num_programs(0) // 2

    @pl.when(pl.program_id(0) == 0)
    def clear():
        router_grad_ref[...] = jnp.zeros_like(router_grad_ref)

    slots = slot_ref[0]
    local, span = slots.shape
    gates = [gate_ref[0, k : k + 1, :] for k in range(2)]
    expert = lax.broadcasted_iota(jnp.int32, (router_ref.shape[1], span), 0)
    hits = [expert == route_ref[0, k : k + 1, :] for k in range(2)]
    table = slot_table(slots, n_slots)
    table_low = low(table)
    first = first_ref[0]

    def rows_of(ref):
        return jnp.concatenate([ref[e] for e in range(local)], axis=0)

    produced = wide(rows_of(out_ref))
    gate_grad = jnp.sum(wide(rows_of(kept_ref)) * produced, axis=1, keepdims=True)
    spread = (wide(hits[0]) - wide(hits[1])) * (gates[0] * gates[1])
    spread_hi = low(spread)
    spread_lo = low(spread - wide(spread_hi))
    factor = lax.dot_general(
        table_low, spread_hi, ROWS_BY_ROWS, preferred_element_type=jnp.float32
    ) + lax.dot_general(table_low, spread_lo, ROWS_BY_ROWS, preferred_element_type=jnp.float32)
    signs, slot_gates = [], []
    for e in range(local):
        rows = slice(e * n_slots, (e + 1) * n_slots)
        is_first = route_ref[0, 0:1, :] == first + e
        is_second = route_ref[0, 1:2, :] == first + e
        sign = jnp.where(is_first, 1.0, jnp.where(is_second, -1.0, 0.0))
        gate = jnp.where(is_first, gates[0], jnp.where(is_second, gates[1], 0.0))
        signs.append(jnp.sum(table[rows] * sign, axis=1, keepdims=True))
        slot_gates.append(jnp.sum(table[rows] * gate, axis=1, keepdims=True))
    sign, slot_gate = jnp.concatenate(signs, axis=0), jnp.concatenate(slot_gates, axis=0)
    logit_grad = factor * (sign * gate_grad)
    logit_hi = low(logit_grad)
    logit_lo = low(logit_grad - wide(logit_hi))
    back = wide(rows_of(back_ref))
    for part in (logit_hi, logit_lo):
        back = back + lax.dot_general(
            part, router_ref[...], ROWS_BY_ROWS, preferred_element_type=jnp.float32
        )
    mixed = low(
        lax.dot_general(
            table_low,
            low(produced * slot_gate),
            COLS_BY_COLS,
            preferred_element_type=jnp.float32,
        )
    )
    back_sum = low(
        lax.dot_general(table_low, low(back), COLS_BY_COLS, preferred_element_type=jnp.float32)
    )
    for part in range(2):

        @pl.when((pl.program_id(0) >= half) == (part == 1))
        def store(part=part):
            mixed_refs[part][0] = mixed
            sum_refs[part][0] = back_sum

    picked = rows_of(in_ref)
    for part in (logit_hi, logit_lo):
        router_grad_ref[...] += lax.dot_general(
            part, picked, COLS_BY_COLS, preferred_element_type=jnp.float32
        )


def combine(inputs, kept, gates, router, routes, slots, first, out, back, n_slots, gate=()):
    n_block, local, span = slots.shape
    width, experts = router.shape
    rows = pl.BlockSpec((local, n_slots, width), lambda b: (0, b, 0))
    half = n_block // 2
    halves = [
        pl.BlockSpec((1, span, width), lambda b: (jnp.minimum(b, half - 1), 0, 0)),
        pl.BlockSpec((1, span, width), lambda b: (jnp.maximum(b - half, 0), 0, 0)),
    ]
    return pl.pallas_call(
        functools.partial(combine_kernel, n_slots, len(gate)),
        grid=(n_block,),
        in_specs=[
            rows,
            rows,
            pl.BlockSpec((1, 2, span), lambda b: (b, 0, 0)),
            pl.BlockSpec(router.shape, lambda b: (0, 0)),
            pl.BlockSpec((1, 2, span), lambda b: (b, 0, 0)),
            pl.BlockSpec((1, local, span), lambda b: (b, 0, 0)),
            pl.BlockSpec(memory_space=pltpu.SMEM),
            rows,
            rows,
        ]
        + gate_specs(gate),
        out_specs=halves + halves + [pl.BlockSpec((experts, width), lambda b: (0, 0))],
        out_shape=[
            *[jax.ShapeDtypeStruct((half, span, width), jnp.bfloat16)] * 4,
            jax.ShapeDtypeStruct((experts, width), jnp.float32),
        ],
        compiler_params=pltpu.CompilerParams(vmem_limit_bytes=VMEM_LIMIT),
        cost_estimate=SHORT,
        name="combine",
    )(inputs, kept, gates, router, routes, slots, first, out, back, *gate)


def expert_kernel(tile, started, *refs):
    if started:
        x_ref, g_ref, in_ref, down_ref, out_so_far, back_so_far = refs[:6]
        refs = refs[6:]
    else:
        x_ref, g_ref, in_ref, down_ref = refs[:4]
        refs = refs[4:]
    out_ref, back_ref, in_grad_ref, down_grad_ref, x_t, hidden_t, pre_grads = refs
    step = pl.program_id(1)
    rows = pl.ds(pl.multiple_of(step * tile, tile), tile)
    x = x_ref[0, rows, :]
    g = g_ref[0, rows, :]
    pre = jnp.dot(x, in_ref[0], preferred_element_type=jnp.float32)
    hidden_grad = lax.dot_general(
        g, down_ref[0], ROWS_BY_ROWS, preferred_element_type=jnp.float32
    )
    root = 0.7978845608028654
    square = pre * pre
    bent = jnp.tanh(pre * (root + root * 0.044715 * square))
    half = 0.5 + 0.5 * bent
    hidden = low(pre * half)
    slope = half + pre * (half * (1.0 - bent)) * (root + 3.0 * root * 0.044715 * square)
    pre_grad = low(hidden_grad * slope)
    out = jnp.dot(hidden, down_ref[0], preferred_element_type=jnp.float32)
    back = lax.dot_general(
        pre_grad, in_ref[0], ROWS_BY_ROWS, preferred_element_type=jnp.float32
    )
    if started:
        out = out + out_so_far[0]
        back = back + back_so_far[0]
    out_ref[0] = out.astype(out_ref.dtype)
    back_ref[0] = back.astype(back_ref.dtype)
    x_t[:, rows] = x.T
    hidden_t[:, rows] = hidden.T
    pre_grads[rows, :] = pre_grad

    @pl.when(step == pl.num_programs(1) - 1)
    def weight_grads():
        part = 256
        for at in range(0, hidden_t.shape[0], part):
            some = slice(at, min(at + part, hidden_t.shape[0]))
            down_grad_ref[0, some, :] = low(
                jnp.dot(hidden_t[some, :], g_ref[0], preferred_element_type=jnp.float32)
            )
        for at in range(0, x_t.shape[0], part):
            some = slice(at, min(at + part, x_t.shape[0]))
            in_grad_ref[0, some, :] = low(
                jnp.dot(x_t[some, :], pre_grads[...], preferred_element_type=jnp.float32)
            )


def expert_slice(x, g, w_in, w_out, so_far, is_last):
    local, n_rows, width = x.shape
    inner = w_in.shape[2]
    tile = min(n_rows, 1024)
    whole = pl.BlockSpec((1, n_rows, width), lambda e, i: (e, 0, 0))
    up = pl.BlockSpec((1, width, inner), lambda e, i: (e, 0, 0))
    down = pl.BlockSpec((1, inner, width), lambda e, i: (e, 0, 0))
    some = pl.BlockSpec((1, tile, width), lambda e, i: (e, i, 0))
    started = so_far is not None
    kind = jnp.bfloat16 if is_last else jnp.float32
    totals = tuple(so_far) if started else ()
    return pl.pallas_call(
        functools.partial(expert_kernel, tile, started),
        grid=(local, n_rows // tile),
        in_specs=[whole, whole, up, down] + [some] * len(totals),
        out_specs=[some, some, up, down],
        out_shape=[
            jax.ShapeDtypeStruct(x.shape, kind),
            jax.ShapeDtypeStruct(x.shape, kind),
            jax.ShapeDtypeStruct(w_in.shape, jnp.bfloat16),
            jax.ShapeDtypeStruct(w_out.shape, jnp.bfloat16),
        ],
        input_output_aliases={4: 0, 5: 1} if started and not is_last else {},
        scratch_shapes=[
            pltpu.VMEM((width, n_rows), jnp.bfloat16),
            pltpu.VMEM((inner, n_rows), jnp.bfloat16),
            pltpu.VMEM((n_rows, inner), jnp.bfloat16),
        ],
        compiler_params=pltpu.CompilerParams(vmem_limit_bytes=VMEM_LIMIT),
        cost_estimate=SHORT,
        name="expert_slice",
    )(x, g, w_in, w_out, *totals)


def body(
    tokens,
    cotangent,
    qkv_weight,
    out_weight,
    norm_gains,
    rel_bias,
    router_weight,
    w_in,
    w_out,
    doc_lengths,
    bucket_ids,
    routes,
):
    n_batch, n_span, n_width = tokens.shape
    n_rows = n_batch * n_span
    n_buckets, n_heads = rel_bias.shape
    n_inner = qkv_weight.shape[2]
    groups = lax.axis_size("expert")
    local_experts = w_in.shape[0]
    experts_all = local_experts * groups
    n_slots = max(2, 2 * n_span * 2 // experts_all)
    dp_places = dp_order()
    place = lax.axis_index("dp")
    n_dp = len(dp_places)
    offsets = [(place - piece) * n_span for piece in dp_places]
    extra = experts_all + 2
    lanes = -(-extra // 128) * 128
    route_rows = -(-2 * n_rows // n_width // 16) * 16
    packed = jnp.concatenate(
        [qkv_weight[0], qkv_weight[1], qkv_weight[2], out_weight]
        + [router_weight, norm_gains.T, jnp.zeros((out_weight.shape[0], lanes - extra), jnp.bfloat16)],
        axis=1,
    )
    token_pieces = dp_gather(tokens)
    full, full_plane, full_last = gather_all(packed)
    ahead = (*token_pieces[1:3], *full_plane) if by_steps() else ()
    in_pieces, down_pieces, near_in, near_down = dp_gather_pair(w_in, w_out, ahead)
    weights = [full[:, c * n_inner : (c + 1) * n_inner] for c in range(4)]
    router = full[:, 4 * n_inner : 4 * n_inner + experts_all]
    router_t = router.T
    gains = wide(full[:, 4 * n_inner + experts_all : 4 * n_inner + extra].T)
    route_values = low(routes.reshape(n_batch, n_span, 2).transpose(0, 2, 1)).reshape(-1)
    route_values = jnp.pad(route_values, (0, route_rows * n_width - 2 * n_rows))
    grad_rows = jnp.concatenate(
        [cotangent.reshape(n_rows, n_width), route_values.reshape(route_rows, n_width)]
    )
    grad_all, grad_steps = expert_gather(after(grad_rows, *full_last))
    routes_all = grad_all[:, n_rows:].reshape(groups, -1)[:, : 2 * n_rows]
    routes_all = routes_all.astype(jnp.int32).reshape(groups * n_batch, 2, n_span)
    first = lax.axis_index("expert").astype(jnp.int32) * local_experts
    mine = first + jnp.arange(local_experts, dtype=jnp.int32)
    member = jnp.any(routes_all[:, None] == mine[None, :, None, None], axis=2)
    before = wide(jnp.arange(n_span)[:, None] < jnp.arange(n_span)[None, :])
    ranks = jnp.einsum(
        "bet,tu->beu", low(member), low(before), preferred_element_type=jnp.float32
    ).astype(jnp.int32)
    slots = jnp.where(member, ranks, -1)
    first = first[None]

    base = bias_base(rel_bias, bucket_ids, offsets, n_span)
    begin = document_starts(doc_lengths, place * n_span, n_span)
    starts = jnp.stack([begin - piece * n_span for piece in dp_places], axis=1)

    normed1_all = jnp.stack(
        [low(norm_forward(wide(piece), gains[0])[0]) for piece in token_pieces], axis=1
    )
    normed1_all = normed1_all.reshape(n_batch, n_dp * n_span, n_width)
    flat_normed1 = normed1_all.reshape(-1, n_width)
    normed1 = normed1_all[:, :n_span] if by_steps() else lax.dynamic_slice_in_dim(
        normed1_all, place * n_span, n_span, 1
    )
    normed1 = normed1.reshape(n_rows, n_width)
    queries = low(low(jnp.dot(normed1, weights[0], preferred_element_type=jnp.float32)) * SCALE)
    queries = queries.reshape(n_batch, n_span, n_inner)
    keys, values = (
        low(jnp.dot(flat_normed1, weights[c], preferred_element_type=jnp.float32)).reshape(
            n_batch, -1, n_inner
        )
        for c in (1, 2)
    )
    attended_rows, log_total = attention_forward(
        queries, keys, values, base, starts, n_heads, (*near_in, *grad_steps[1:3])
    )
    attended = attended_rows.reshape(n_rows, n_inner)
    inputs = wide(tokens.reshape(n_rows, n_width))
    resid = inputs + jnp.dot(attended, weights[3], preferred_element_type=jnp.float32)
    normed2, inverse2 = norm_forward(resid, gains[1])
    normed2_low = low(normed2).reshape(n_batch, n_span, n_width)
    normed2_low = after(normed2_low, *grad_steps[3:])
    far_pieces = (in_pieces[3], down_pieces[3]) if by_steps() else ()
    token_all = expert_gather(normed2_low, near_down, far_pieces)[0]
    token_all = token_all.reshape(groups * n_batch, n_span, n_width)
    expert_in, expert_up, expert_kept, gates = dispatch(
        token_all,
        grad_all,
        router_t,
        routes_all,
        slots,
        first,
        n_slots,
        (*in_pieces[1:], *down_pieces[1:]),
    )
    so_far = None
    in_grads, down_grads = {}, {}
    for r in (*range(n_dp - 1, 3, -1), 3, 1, 2, 0):
        *so_far, in_grads[r], down_grads[r] = expert_slice(
            expert_in, expert_up, in_pieces[r], down_pieces[r], so_far, r == 0
        )
    in_grads, down_grads = ([grads[r] for r in range(n_dp)] for grads in (in_grads, down_grads))
    piece_shape = (groups // 2, n_batch, n_span, n_width)
    received = dp_scatter_pair(in_grads, down_grads)
    in_share, down_share, last = dp_scatter_pair_end(in_grads, down_grads, received)
    mixed_kept, mixed_given, back_kept, back_given, router_grad = combine(
        expert_in,
        expert_kept,
        gates,
        router,
        routes_all,
        slots,
        first,
        *so_far,
        n_slots,
        received[:2] if last else (),
    )
    back_other = swap_cores(back_given.reshape(piece_shape), received[2:] if last else ())
    normed2_grad, back_corner, _ = expert_scatter(back_kept.reshape(piece_shape), back_other)
    normed2_grad = normed2_grad.reshape(n_rows, n_width)
    mixed_other = swap_cores(mixed_given.reshape(piece_shape), (back_corner,))
    gain2_grad = jnp.sum(normed2_grad * resid * inverse2, axis=0)
    grad_out = wide(cotangent.reshape(n_rows, n_width))
    resid_grad = grad_out + norm_backward(resid, inverse2, gains[1], normed2_grad)
    branch_low = low(resid_grad)
    attended_grad = low(
        lax.dot_general(branch_low, weights[3], ROWS_BY_ROWS, preferred_element_type=jnp.float32)
    )
    query_grad, key_grad, value_grad, dist_grad = attention_backward(
        queries,
        keys,
        values,
        attended_rows,
        attended_grad.reshape(n_batch, n_span, n_inner),
        base,
        starts,
        log_total,
        n_heads,
        (*last, mixed_other),
    )
    bias_grad = bias_fold(dist_grad, bucket_ids, offsets, n_buckets)
    mixed, mixed_corner, mixed_last = expert_scatter(
        mixed_kept.reshape(piece_shape), mixed_other, (dist_grad,), (dist_grad,)
    )
    block_out = low(resid + mixed.reshape(n_rows, n_width)).reshape(n_batch, n_span, n_width)
    query_grad = query_grad.reshape(n_rows, n_inner)
    key_grad = key_grad.reshape(-1, n_inner)
    value_grad = value_grad.reshape(-1, n_inner)
    own_part = lax.dot_general(
        query_grad, weights[0], ROWS_BY_ROWS, preferred_element_type=jnp.float32
    )
    all_part = lax.dot_general(
        key_grad, weights[1], ROWS_BY_ROWS, preferred_element_type=jnp.float32
    ) + lax.dot_general(value_grad, weights[2], ROWS_BY_ROWS, preferred_element_type=jnp.float32)
    all_part = all_part.reshape(n_batch, n_dp, n_span, n_width)
    sent = low(all_part)
    shared = dp_scatter([sent[:, r] for r in range(n_dp)])
    normed1_grad = own_part + shared.reshape(n_rows, n_width)
    inverse1 = lax.rsqrt(jnp.mean(inputs * inputs, axis=-1, keepdims=True) + EPS)
    tokens_grad = resid_grad + norm_backward(inputs, inverse1, gains[0], normed1_grad)
    def rows_grad(rows, grads):
        return low(
            lax.dot_general(rows, grads, COLS_BY_COLS, preferred_element_type=jnp.float32)
        )

    weight_grads = jnp.stack(
        [
            rows_grad(normed1, query_grad),
            rows_grad(flat_normed1, key_grad),
            rows_grad(flat_normed1, value_grad),
            rows_grad(attended, branch_low),
        ]
    )
    weight_grads = after(weight_grads, mixed_corner)
    gain1_grad = (
        sum(jnp.sum(wide(weight_grads[c]) * wide(weights[c]), axis=1) for c in range(3)) / gains[0]
    )
    shares = scatter_all(weight_grads, mixed_last)
    small_rows = experts_all + 2
    bias_flat = jnp.pad(bias_grad.reshape(1, -1), ((0, 0), (0, n_width - bias_grad.size)))
    small = sum_all(
        jnp.concatenate([router_grad, gain1_grad[None], gain2_grad[None], bias_flat])
    )
    rel_bias_grad = small[small_rows, : bias_grad.size].reshape(bias_grad.shape)
    n_own = router_weight.shape[0]
    own = lax.dynamic_slice_in_dim(
        small, (place * groups + lax.axis_index("expert")) * n_own, n_own, 1
    )
    router_share = own[:experts_all].T
    gains_share = own[experts_all:small_rows]
    qkv_share, out_share = shares[:3], shares[3]
    return (
        block_out,
        tokens_grad.reshape(n_batch, n_span, n_width),
        qkv_share,
        out_share,
        gains_share,
        rel_bias_grad,
        router_share,
        in_share,
        down_share,
    )


def solution(mesh):
    return jax.shard_map(
        body,
        mesh=mesh,
        in_specs=(
            P("expert", "dp", None),
            P("expert", "dp", None),
            P(None, ("dp", "expert"), None),
            P(("dp", "expert"), None),
            P(None, ("dp", "expert")),
            P(),
            P(("dp", "expert"), None),
            P("expert", None, "dp"),
            P("expert", "dp", None),
            P("expert", None),
            P(),
            P("expert", "dp", None),
        ),
        out_specs=(
            P("expert", "dp", None),
            P("expert", "dp", None),
            P(None, ("dp", "expert"), None),
            P(("dp", "expert"), None),
            P(None, ("dp", "expert")),
            P(),
            P(("dp", "expert"), None),
            P("expert", None, "dp"),
            P("expert", "dp", None),
        ),
        check_vma=False,
    )
```

```python
import functools

import jax
import jax.numpy as jnp
from jax import lax
from jax.experimental import pallas as pl
from jax.experimental.pallas import tpu as pltpu
from jax.sharding import PartitionSpec as P

EPS = 1e-06
SCALE = 0.125
NEG = -1e30
VMEM_LIMIT = 48 * 1024 * 1024
SHORT = pl.CostEstimate(flops=1, bytes_accessed=1, transcendentals=0)
ROWS_BY_ROWS = (((1,), (1,)), ((), ()))
COLS_BY_COLS = (((0,), (0,)), ((), ()))
FIRST_BIT = ((0, 1), (1, 0), (2, 3), (3, 2))
SECOND_BIT = ((0, 2), (2, 0), (1, 3), (3, 1))
PARTNER = tuple((i, i ^ 1) for i in range(8))
NEXT_CHIP = tuple((i, i ^ 2) for i in range(8))
SECOND_CHIP = tuple((i, i ^ 4) for i in range(8))


def norm_forward(values, gain):
    inverse = lax.rsqrt(jnp.mean(values * values, axis=-1, keepdims=True) + EPS)
    return (values * inverse * gain, inverse)


def norm_backward(values, inverse, gain, grad_in):
    scaled = grad_in * gain
    cubed = inverse * inverse * inverse
    return inverse * scaled - values * cubed * jnp.mean(scaled * values, axis=-1, keepdims=True)


def low(values):
    return values.astype(jnp.bfloat16)


def wide(values):
    return values.astype(jnp.float32)


def pass_kernel(*refs):
    pass


def after(value, *others):
    if not others:
        return value
    return pl.pallas_call(
        pass_kernel,
        in_specs=[pl.BlockSpec(memory_space=pl.ANY)] * (1 + len(others)),
        out_specs=pl.BlockSpec(memory_space=pl.ANY),
        out_shape=jax.ShapeDtypeStruct(value.shape, value.dtype),
        input_output_aliases={0: 0},
        cost_estimate=SHORT,
        name="after",
    )(value, *others)


def by_steps():
    return lax.axis_size("dp") == 4 and lax.axis_size("expert") == 8


def dp_order():
    n_dp = lax.axis_size("dp")
    if by_steps():
        me = lax.axis_index("dp")
        return [jnp.bitwise_xor(me, r) for r in range(n_dp)]
    return [jnp.int32(r) for r in range(n_dp)]


def expert_order():
    groups = lax.axis_size("expert")
    if by_steps():
        me = lax.axis_index("expert")
        return [jnp.bitwise_xor(me, 2 * r + p) for p in range(2) for r in range(4)]
    return [jnp.int32(r) for r in range(groups)]


def dp_gather(block):
    if not by_steps():
        full = lax.all_gather(block, "dp")
        return [full[r] for r in range(full.shape[0])]
    along = lax.ppermute(block, "dp", FIRST_BIT)
    across = lax.ppermute(block, "dp", SECOND_BIT)
    return [block, along, across, lax.ppermute(along, "dp", SECOND_BIT)]


def dp_gather_pair(first, second, gate=()):
    if not by_steps():
        return dp_gather(first), dp_gather(second), (), ()
    sent = (after(first, *gate), second)
    along = [lax.ppermute(block, "dp", FIRST_BIT) for block in sent]
    across = [lax.ppermute(block, "dp", SECOND_BIT) for block in sent]
    far_first = lax.ppermute(across[0], "dp", FIRST_BIT)
    far_second = lax.ppermute(along[1], "dp", SECOND_BIT)
    return (
        [first, along[0], across[0], far_first],
        [second, along[1], across[1], far_second],
        (along[0], across[0]),
        (along[1], across[1]),
    )


def dp_scatter_pair(first, second):
    if not by_steps():
        return [
            wide(lax.psum_scatter(jnp.stack(parts), "dp", scatter_dimension=0))
            for parts in (first, second)
        ]
    first_far = lax.ppermute(first[3], "dp", FIRST_BIT)
    second_far = lax.ppermute(second[3], "dp", SECOND_BIT)
    first_along = lax.ppermute(first[1], "dp", FIRST_BIT)
    second_across = lax.ppermute(second[2], "dp", SECOND_BIT)
    return first_far, second_far, first_along, second_across


def dp_scatter_pair_end(first, second, received, gate=()):
    if not by_steps():
        return (*received, ())
    first_far, second_far, first_along, second_across = received
    first_sum = after(low(wide(first[2]) + wide(first_far)), *gate)
    first_last = lax.ppermute(first_sum, "dp", SECOND_BIT)
    second_last = lax.ppermute(low(wide(second[1]) + wide(second_far)), "dp", FIRST_BIT)
    return (
        wide(first[0]) + wide(first_along) + wide(first_last),
        wide(second[0]) + wide(second_across) + wide(second_last),
        (first_last, second_last),
    )


def dp_scatter(parts, gate=()):
    if not by_steps():
        return wide(lax.psum_scatter(jnp.stack(parts), "dp", scatter_dimension=0))
    half = parts[0].shape[0] // 2
    low_half, high_half = ([part[rows] for part in parts] for rows in (slice(0, half), slice(half, None)))
    received = dp_scatter_pair(low_half, high_half)
    ends = dp_scatter_pair_end(low_half, high_half, received, gate)
    return jnp.concatenate(ends[:2], axis=0)


def line_gather(block, gates=()):
    near = lax.ppermute(block, "expert", NEXT_CHIP)
    far = lax.ppermute(block, "expert", SECOND_CHIP)
    corner = lax.ppermute(after(far, *gates), "expert", NEXT_CHIP)
    return [block, near, far, corner]


def line_scatter(parts, first_gate=(), second_gate=(), near_gate=()):
    corner = lax.ppermute(after(parts[3], *first_gate), "expert", NEXT_CHIP)
    passed = after(low(wide(parts[2]) + wide(corner)), *second_gate)
    near = lax.ppermute(after(parts[1], *near_gate), "expert", NEXT_CHIP)
    far = lax.ppermute(passed, "expert", SECOND_CHIP)
    return wide(parts[0]) + wide(near) + wide(far), corner, (near, far)


def expert_gather(block, gates=(), last_gates=()):
    if not by_steps():
        return lax.all_gather(block, "expert"), ()
    mine = line_gather(block, gates)
    mine[3] = after(mine[3], *last_gates)
    return jnp.stack(mine + [lax.ppermute(piece, "expert", PARTNER) for piece in mine]), mine


def swap_cores(given, gate=()):
    if not by_steps():
        return given
    return lax.ppermute(after(given, *gate), "expert", PARTNER)


def expert_scatter(kept, other, second_gate=(), near_gate=()):
    if not by_steps():
        parts = jnp.concatenate([kept, other])
        total = wide(lax.psum_scatter(parts, "expert", scatter_dimension=0))
        return total, total, ()
    merged = [low(wide(kept[r]) + wide(other[r])) for r in range(4)]
    return line_scatter(merged, (), second_gate, near_gate)


def gather_all(shard):
    rows, columns = shard.shape
    if not by_steps():
        return lax.all_gather(shard, ("dp", "expert"), axis=0, tiled=True), (), ()
    place = lax.axis_index("dp")
    odd_first, odd_second = place % 2 == 1, place // 2 == 1
    along = lax.ppermute(shard, "dp", FIRST_BIT)
    near = jnp.where(odd_first, jnp.stack([along, shard]), jnp.stack([shard, along]))
    far = lax.ppermute(near, "dp", SECOND_BIT)
    plane = jnp.where(odd_second, jnp.concatenate([far, near]), jnp.concatenate([near, far]))
    mine = line_gather(plane)
    pieces = mine + [lax.ppermute(piece, "expert", PARTNER) for piece in mine]
    owners = expert_order()
    full = jnp.zeros((4, 8, rows, columns), shard.dtype)
    for index, piece in enumerate(pieces):
        full = lax.dynamic_update_slice_in_dim(full, piece[:, None], owners[index], 1)
    return full.reshape(32 * rows, columns), (far,), mine[3:]


def scatter_all(parts, gates=()):
    if not by_steps():
        return wide(lax.psum_scatter(parts, ("dp", "expert"), scatter_dimension=1, tiled=True))
    count, rows, columns = parts.shape
    blocks = parts.reshape(count, 4, 4, 2, rows // 32, columns)
    me = lax.axis_index("expert")
    chip, core = me // 2, me % 2
    kept, given = (
        lax.dynamic_index_in_dim(blocks, index, 3, keepdims=False) for index in (core, 1 - core)
    )
    merged = low(wide(kept) + wide(lax.ppermute(given, "expert", PARTNER)))
    plane = low(
        dp_scatter(
            [lax.dynamic_index_in_dim(merged, place, 1, keepdims=False) for place in dp_order()],
            gates,
        )
    )
    pieces = [
        lax.dynamic_index_in_dim(plane, jnp.bitwise_xor(chip, r), 1, keepdims=False)
        for r in range(4)
    ]
    return line_scatter(pieces)[0]


def sum_all(values):
    if not by_steps():
        return lax.psum(values, ("dp", "expert"))
    for bit in (1, 2, 4):
        values = values + lax.ppermute(values, "expert", [(i, i ^ bit) for i in range(8)])
    for pairs in (FIRST_BIT, SECOND_BIT):
        values = values + lax.ppermute(values, "dp", pairs)
    return values


def spread_rows(base, span):
    grown = base
    while grown.shape[0] < span:
        grown = jnp.concatenate([grown, pltpu.roll(grown, grown.shape[0], 1)], axis=0)
    return grown[:, span:]


def fold_rows(block, span):
    wide = jnp.concatenate([jnp.zeros_like(block), block], axis=1)
    while wide.shape[0] > 1:
        half = wide.shape[0] // 2
        wide = wide[:half] + pltpu.roll(wide[half:], 2 * span - half, 1)
    return wide


def attention_forward_kernel(
    n_piece, span, head_dim, n_gate, q_ref, k_ref, v_ref, base_ref, start_ref, *refs
):
    out_ref, lse_ref, bias_ref = refs[n_gate:]

    @pl.when(pl.program_id(1) == 0)
    def fill_bias():
        for head in range(2):
            for piece in range(n_piece):
                bias_ref[head, piece] = spread_rows(
                    base_ref[0, head, piece : piece + 1, :], span
                )

    queries = q_ref[0]
    lane_head = lax.broadcasted_iota(jnp.int32, queries.shape, 1) // head_dim
    key_row = lax.broadcasted_iota(jnp.int32, (span, span), 0)
    values_t = [v_ref[0, pl.ds(piece * span, span), :].T for piece in range(n_piece)]
    outs = []
    for head in range(2):
        masked = jnp.where(lane_head == head, queries, jnp.zeros_like(queries))
        scores = []
        highest = None
        for piece in range(n_piece):
            keys = k_ref[0, pl.ds(piece * span, span), :]
            block = lax.dot_general(
                keys, masked, (((1,), (1,)), ((), ())), preferred_element_type=jnp.float32
            )
            block = block + bias_ref[head, piece]
            block = jnp.where(key_row >= start_ref[0, piece : piece + 1, :], block, NEG)
            scores.append(block)
            top = jnp.max(block, axis=0, keepdims=True)
            highest = top if highest is None else jnp.maximum(highest, top)
        total = jnp.zeros_like(highest)
        result = jnp.zeros((head_dim, span), jnp.float32)
        for piece in range(n_piece):
            weights = jnp.exp(scores[piece] - highest)
            total = total + jnp.sum(weights, axis=0, keepdims=True)
            result = result + jnp.dot(
                values_t[piece][head * head_dim : (head + 1) * head_dim],
                weights.astype(jnp.bfloat16),
                preferred_element_type=jnp.float32,
            )
        outs.append(result / total)
        lse_ref[0, 0, head : head + 1, :] = highest + jnp.log(total)
    out_ref[0] = jnp.concatenate(outs, axis=0).T.astype(out_ref.dtype)


def attention_backward_kernel(
    n_piece,
    span,
    head_dim,
    n_gate,
    q_ref,
    k_ref,
    v_ref,
    out_ref,
    grad_ref,
    base_ref,
    start_ref,
    lse_ref,
    *refs,
):
    dq_ref, dk_ref, dv_ref, dist_ref, bias_ref, sum_ref = refs[n_gate:]
    batch = pl.program_id(1)

    @pl.when(batch == 0)
    def fill_bias():
        for head in range(2):
            for piece in range(n_piece):
                bias_ref[head, piece] = spread_rows(
                    base_ref[0, head, piece : piece + 1, :], span
                )
                sum_ref[head, piece] = jnp.zeros((span, span), jnp.float32)

    queries = q_ref[0]
    grads = grad_ref[0]
    product = grads.astype(jnp.float32) * out_ref[0].astype(jnp.float32)
    product_hi = product.astype(jnp.bfloat16)
    product_lo = (product - product_hi.astype(jnp.float32)).astype(jnp.bfloat16)
    lane_head = lax.broadcasted_iota(jnp.int32, queries.shape, 1) // head_dim
    key_row = lax.broadcasted_iota(jnp.int32, (span, span), 0)
    picker = (
        lax.broadcasted_iota(jnp.int32, (8, 2 * head_dim), 1) // head_dim
        == lax.broadcasted_iota(jnp.int32, (8, 2 * head_dim), 0)
    ).astype(jnp.bfloat16)
    rows_by_rows = (((1,), (1,)), ((), ()))
    correction = lax.dot_general(
        picker, product_hi, rows_by_rows, preferred_element_type=jnp.float32
    ) + lax.dot_general(picker, product_lo, rows_by_rows, preferred_element_type=jnp.float32)
    zero = jnp.zeros_like(queries)
    head_queries = [jnp.where(lane_head == head, queries, zero) for head in range(2)]
    head_grads = [jnp.where(lane_head == head, grads, zero) for head in range(2)]
    query_grads = [jnp.zeros((head_dim, span), jnp.float32) for _ in range(2)]
    for piece in range(n_piece):
        rows = pl.ds(piece * span, span)
        keys = k_ref[0, rows, :]
        values = v_ref[0, rows, :]
        keys_t = keys.T
        allowed = key_row >= start_ref[0, piece : piece + 1, :]
        key_grad = jnp.zeros((span, 2 * head_dim), jnp.float32)
        value_grad = jnp.zeros((span, 2 * head_dim), jnp.float32)
        for head in range(2):
            scores = lax.dot_general(
                keys, head_queries[head], rows_by_rows, preferred_element_type=jnp.float32
            )
            scores = jnp.where(allowed, scores + bias_ref[head, piece], NEG)
            probs = jnp.exp(scores - lse_ref[0, 0, head : head + 1, :])
            prob_grad = lax.dot_general(
                values, head_grads[head], rows_by_rows, preferred_element_type=jnp.float32
            )
            score_grad = (probs * (prob_grad - correction[head : head + 1, :])).astype(jnp.bfloat16)
            sum_ref[head, piece] += score_grad.astype(jnp.float32)
            value_grad = value_grad + jnp.dot(
                probs.astype(jnp.bfloat16), head_grads[head], preferred_element_type=jnp.float32
            )
            key_grad = key_grad + jnp.dot(
                score_grad, head_queries[head], preferred_element_type=jnp.float32
            )
            query_grads[head] = query_grads[head] + jnp.dot(
                keys_t[head * head_dim : (head + 1) * head_dim],
                score_grad,
                preferred_element_type=jnp.float32,
            )
        dk_ref[0, rows, :] = key_grad.astype(jnp.bfloat16)
        dv_ref[0, rows, :] = value_grad.astype(jnp.bfloat16)
    dq_ref[0] = (jnp.concatenate(query_grads, axis=0) * SCALE).T.astype(jnp.bfloat16)

    @pl.when(batch == pl.num_programs(1) - 1)
    def fold_distances():
        for head in range(2):
            for piece in range(n_piece):
                dist_ref[0, head, piece : piece + 1, :] = fold_rows(sum_ref[head, piece], span)


def gate_specs(gate):
    return [pl.BlockSpec(memory_space=pl.ANY) for _ in gate]


def attention_specs(n_piece, span, pair):
    n_keys = n_piece * span
    rows = pl.BlockSpec((1, span, pair), lambda h, b: (b, 0, h))
    keys = pl.BlockSpec((1, n_keys, pair), lambda h, b: (b, 0, h))
    base = pl.BlockSpec((1, 2, n_piece, 2 * span), lambda h, b: (h, 0, 0, 0))
    start = pl.BlockSpec((1, n_piece, span), lambda h, b: (b, 0, 0))
    lse = pl.BlockSpec((1, 1, 2, span), lambda h, b: (h, b, 0, 0))
    return rows, keys, base, start, lse


def attention_forward(queries, keys, values, base, start, n_heads, gate=()):
    n_batch, span, inner = queries.shape
    n_piece = keys.shape[1] // span
    head_dim = inner // n_heads
    n_pairs = n_heads // 2
    rows, key_rows, base_spec, start_spec, lse_spec = attention_specs(n_piece, span, 2 * head_dim)
    return pl.pallas_call(
        functools.partial(attention_forward_kernel, n_piece, span, head_dim, len(gate)),
        grid=(n_pairs, n_batch),
        in_specs=[rows, key_rows, key_rows, base_spec, start_spec] + gate_specs(gate),
        out_specs=[rows, lse_spec],
        out_shape=[
            jax.ShapeDtypeStruct(queries.shape, jnp.bfloat16),
            jax.ShapeDtypeStruct((n_pairs, n_batch, 2, span), jnp.float32),
        ],
        scratch_shapes=[pltpu.VMEM((2, n_piece, span, span), jnp.float32)],
        compiler_params=pltpu.CompilerParams(vmem_limit_bytes=VMEM_LIMIT),
        cost_estimate=SHORT,
        name="attention_forward",
    )(queries, keys, values, base, start, *gate)


def attention_backward(
    queries, keys, values, attended, grads, base, start, lse, n_heads, gate=()
):
    n_batch, span, inner = queries.shape
    n_piece = keys.shape[1] // span
    head_dim = inner // n_heads
    n_pairs = n_heads // 2
    rows, key_rows, base_spec, start_spec, lse_spec = attention_specs(n_piece, span, 2 * head_dim)
    return pl.pallas_call(
        functools.partial(attention_backward_kernel, n_piece, span, head_dim, len(gate)),
        grid=(n_pairs, n_batch),
        in_specs=[rows, key_rows, key_rows, rows, rows, base_spec, start_spec, lse_spec]
        + gate_specs(gate),
        out_specs=[rows, key_rows, key_rows, base_spec],
        out_shape=[
            jax.ShapeDtypeStruct(queries.shape, jnp.bfloat16),
            jax.ShapeDtypeStruct(keys.shape, jnp.bfloat16),
            jax.ShapeDtypeStruct(keys.shape, jnp.bfloat16),
            jax.ShapeDtypeStruct((n_pairs, 2, n_piece, 2 * span), jnp.float32),
        ],
        scratch_shapes=[
            pltpu.VMEM((2, n_piece, span, span), jnp.float32),
            pltpu.VMEM((2, n_piece, span, span), jnp.float32),
        ],
        compiler_params=pltpu.CompilerParams(vmem_limit_bytes=VMEM_LIMIT),
        cost_estimate=pl.CostEstimate(
            flops=40 * n_batch * n_heads * span * n_piece * span * head_dim,
            bytes_accessed=12 * keys.size,
            transcendentals=0,
        ),
        name="attention_backward",
    )(queries, keys, values, attended, grads, base, start, lse, *gate)


def bias_base(rel_bias, bucket_ids, offsets, span):
    length = bucket_ids.shape[0]
    hits = wide(bucket_ids[None, :] == jnp.arange(rel_bias.shape[0], dtype=jnp.int32)[:, None])
    table = jnp.dot(rel_bias.T, hits, precision=lax.Precision.HIGHEST)
    padded = jnp.pad(table, ((0, 0), (length, 0)), constant_values=NEG)
    windows = [
        lax.dynamic_slice_in_dim(padded, offset + length - span, 2 * span, 1) for offset in offsets
    ]
    base = jnp.stack(windows, axis=1)
    return base.reshape(base.shape[0] // 2, 2, len(offsets), 2 * span)


def bias_fold(dist, bucket_ids, offsets, n_buckets):
    n_heads, n_piece, span = dist.shape[0] * 2, dist.shape[2], dist.shape[3] // 2
    length = bucket_ids.shape[0]
    sums = dist.reshape(n_heads, n_piece, 2 * span)
    hits = wide(bucket_ids[:, None] == jnp.arange(n_buckets, dtype=jnp.int32)[None, :])
    padded = jnp.pad(hits, ((length, 0), (0, 0)))
    windows = jnp.stack(
        [lax.dynamic_slice_in_dim(padded, offset + length - span, 2 * span, 0) for offset in offsets]
    )
    return jnp.einsum("hpu,pun->nh", sums, windows, precision=lax.Precision.HIGHEST)


def document_starts(doc_lengths, offset, span):
    ends = jnp.cumsum(doc_lengths, axis=-1)
    places = offset + jnp.arange(span, dtype=jnp.int32)
    begun = ends[:, None, :] <= places[None, :, None]
    return jnp.max(jnp.where(begun, ends[:, None, :], 0), axis=-1)


def token_gates(router_t, tokens, routes):
    logits = lax.dot_general(
        router_t, tokens, ROWS_BY_ROWS, preferred_element_type=jnp.float32
    )
    expert = lax.broadcasted_iota(jnp.int32, logits.shape, 0)
    hits = [expert == routes[k : k + 1, :] for k in range(2)]
    chosen = [jnp.sum(jnp.where(hit, logits, 0.0), axis=0, keepdims=True) for hit in hits]
    highest = jnp.maximum(chosen[0], chosen[1])
    raised = [jnp.exp(value - highest) for value in chosen]
    total = raised[0] + raised[1]
    return [value / total for value in raised], hits


def slot_table(slots, n_slots):
    index = lax.broadcasted_iota(jnp.int32, (n_slots, slots.shape[1]), 0)
    return jnp.concatenate(
        [wide(index == slots[e : e + 1, :]) for e in range(slots.shape[0])], axis=0
    )


def dispatch_kernel(
    n_slots, n_gate, token_ref, grad_ref, router_ref, route_ref, slot_ref, first_ref, *refs
):
    in_ref, up_ref, kept_ref, gate_ref = refs[n_gate:]
    tokens = token_ref[0]
    gates, _ = token_gates(router_ref[...], tokens, route_ref[0])
    slots = slot_ref[0]
    table = slot_table(slots, n_slots)
    table_low = low(table)
    local = slots.shape[0]
    picked = jnp.dot(table_low, tokens, preferred_element_type=jnp.float32)
    grads = jnp.dot(table_low, grad_ref[0], preferred_element_type=jnp.float32)
    first = first_ref[0]
    gate_ref[0] = jnp.concatenate(gates, axis=0)
    for e in range(local):
        rows = slice(e * n_slots, (e + 1) * n_slots)
        gate = jnp.where(
            route_ref[0, 0:1, :] == first + e,
            gates[0],
            jnp.where(route_ref[0, 1:2, :] == first + e, gates[1], 0.0),
        )
        slot_gate = jnp.sum(table[rows] * gate, axis=1, keepdims=True)
        in_ref[e] = low(picked[rows])
        kept_ref[e] = low(grads[rows])
        up_ref[e] = low(grads[rows] * slot_gate)


def dispatch(tokens, grads, router_t, routes, slots, first, n_slots, gate=()):
    n_block, span, width = tokens.shape
    local = slots.shape[1]
    block = pl.BlockSpec((1, span, width), lambda b: (b, 0, 0))
    per_device = n_block // grads.shape[0]
    grad_block = pl.BlockSpec((1, span, width), lambda b: (b // per_device, b % per_device, 0))
    rows = pl.BlockSpec((local, n_slots, width), lambda b: (0, b, 0))
    return pl.pallas_call(
        functools.partial(dispatch_kernel, n_slots, len(gate)),
        grid=(n_block,),
        in_specs=[
            block,
            grad_block,
            pl.BlockSpec(router_t.shape, lambda b: (0, 0)),
            pl.BlockSpec((1, 2, span), lambda b: (b, 0, 0)),
            pl.BlockSpec((1, local, span), lambda b: (b, 0, 0)),
            pl.BlockSpec(memory_space=pltpu.SMEM),
        ]
        + gate_specs(gate),
        out_specs=[rows, rows, rows, pl.BlockSpec((1, 2, span), lambda b: (b, 0, 0))],
        out_shape=[jax.ShapeDtypeStruct((local, n_block * n_slots, width), jnp.bfloat16)] * 3
        + [jax.ShapeDtypeStruct((n_block, 2, span), jnp.float32)],
        compiler_params=pltpu.CompilerParams(vmem_limit_bytes=VMEM_LIMIT),
        cost_estimate=SHORT,
        name="dispatch",
    )(tokens, grads, router_t, routes, slots, first, *gate)


def combine_kernel(
    n_slots,
    n_gate,
    in_ref,
    kept_ref,
    gate_ref,
    router_ref,
    route_ref,
    slot_ref,
    first_ref,
    out_ref,
    back_ref,
    *refs,
):
    mixed_refs, sum_refs, router_grad_ref = refs[n_gate:][:2], refs[n_gate:][2:4], refs[-1]
    half = pl.num_programs(0) // 2

    @pl.when(pl.program_id(0) == 0)
    def clear():
        router_grad_ref[...] = jnp.zeros_like(router_grad_ref)

    slots = slot_ref[0]
    local, span = slots.shape
    gates = [gate_ref[0, k : k + 1, :] for k in range(2)]
    expert = lax.broadcasted_iota(jnp.int32, (router_ref.shape[1], span), 0)
    hits = [expert == route_ref[0, k : k + 1, :] for k in range(2)]
    table = slot_table(slots, n_slots)
    table_low = low(table)
    first = first_ref[0]

    def rows_of(ref):
        return jnp.concatenate([ref[e] for e in range(local)], axis=0)

    produced = wide(rows_of(out_ref))
    gate_grad = jnp.sum(wide(rows_of(kept_ref)) * produced, axis=1, keepdims=True)
    spread = (wide(hits[0]) - wide(hits[1])) * (gates[0] * gates[1])
    spread_hi = low(spread)
    spread_lo = low(spread - wide(spread_hi))
    factor = lax.dot_general(
        table_low, spread_hi, ROWS_BY_ROWS, preferred_element_type=jnp.float32
    ) + lax.dot_general(table_low, spread_lo, ROWS_BY_ROWS, preferred_element_type=jnp.float32)
    signs, slot_gates = [], []
    for e in range(local):
        rows = slice(e * n_slots, (e + 1) * n_slots)
        is_first = route_ref[0, 0:1, :] == first + e
        is_second = route_ref[0, 1:2, :] == first + e
        sign = jnp.where(is_first, 1.0, jnp.where(is_second, -1.0, 0.0))
        gate = jnp.where(is_first, gates[0], jnp.where(is_second, gates[1], 0.0))
        signs.append(jnp.sum(table[rows] * sign, axis=1, keepdims=True))
        slot_gates.append(jnp.sum(table[rows] * gate, axis=1, keepdims=True))
    sign, slot_gate = jnp.concatenate(signs, axis=0), jnp.concatenate(slot_gates, axis=0)
    logit_grad = factor * (sign * gate_grad)
    logit_hi = low(logit_grad)
    logit_lo = low(logit_grad - wide(logit_hi))
    back = wide(rows_of(back_ref))
    for part in (logit_hi, logit_lo):
        back = back + lax.dot_general(
            part, router_ref[...], ROWS_BY_ROWS, preferred_element_type=jnp.float32
        )
    mixed = low(
        lax.dot_general(
            table_low,
            low(produced * slot_gate),
            COLS_BY_COLS,
            preferred_element_type=jnp.float32,
        )
    )
    back_sum = low(
        lax.dot_general(table_low, low(back), COLS_BY_COLS, preferred_element_type=jnp.float32)
    )
    for part in range(2):

        @pl.when((pl.program_id(0) >= half) == (part == 1))
        def store(part=part):
            mixed_refs[part][0] = mixed
            sum_refs[part][0] = back_sum

    picked = rows_of(in_ref)
    for part in (logit_hi, logit_lo):
        router_grad_ref[...] += lax.dot_general(
            part, picked, COLS_BY_COLS, preferred_element_type=jnp.float32
        )


def combine(inputs, kept, gates, router, routes, slots, first, out, back, n_slots, gate=()):
    n_block, local, span = slots.shape
    width, experts = router.shape
    rows = pl.BlockSpec((local, n_slots, width), lambda b: (0, b, 0))
    half = n_block // 2
    halves = [
        pl.BlockSpec((1, span, width), lambda b: (jnp.minimum(b, half - 1), 0, 0)),
        pl.BlockSpec((1, span, width), lambda b: (jnp.maximum(b - half, 0), 0, 0)),
    ]
    return pl.pallas_call(
        functools.partial(combine_kernel, n_slots, len(gate)),
        grid=(n_block,),
        in_specs=[
            rows,
            rows,
            pl.BlockSpec((1, 2, span), lambda b: (b, 0, 0)),
            pl.BlockSpec(router.shape, lambda b: (0, 0)),
            pl.BlockSpec((1, 2, span), lambda b: (b, 0, 0)),
            pl.BlockSpec((1, local, span), lambda b: (b, 0, 0)),
            pl.BlockSpec(memory_space=pltpu.SMEM),
            rows,
            rows,
        ]
        + gate_specs(gate),
        out_specs=halves + halves + [pl.BlockSpec((experts, width), lambda b: (0, 0))],
        out_shape=[
            *[jax.ShapeDtypeStruct((half, span, width), jnp.bfloat16)] * 4,
            jax.ShapeDtypeStruct((experts, width), jnp.float32),
        ],
        compiler_params=pltpu.CompilerParams(vmem_limit_bytes=VMEM_LIMIT),
        cost_estimate=SHORT,
        name="combine",
    )(inputs, kept, gates, router, routes, slots, first, out, back, *gate)


def expert_kernel(tile, started, *refs):
    if started:
        x_ref, g_ref, in_ref, down_ref, out_so_far, back_so_far = refs[:6]
        refs = refs[6:]
    else:
        x_ref, g_ref, in_ref, down_ref = refs[:4]
        refs = refs[4:]
    out_ref, back_ref, in_grad_ref, down_grad_ref, x_t, hidden_t, pre_grads = refs
    step = pl.program_id(1)
    rows = pl.ds(pl.multiple_of(step * tile, tile), tile)
    x = x_ref[0, rows, :]
    g = g_ref[0, rows, :]
    pre = jnp.dot(x, in_ref[0], preferred_element_type=jnp.float32)
    hidden_grad = lax.dot_general(
        g, down_ref[0], ROWS_BY_ROWS, preferred_element_type=jnp.float32
    )
    root = 0.7978845608028654
    square = pre * pre
    bent = jnp.tanh(pre * (root + root * 0.044715 * square))
    half = 0.5 + 0.5 * bent
    hidden = low(pre * half)
    slope = half + pre * (half * (1.0 - bent)) * (root + 3.0 * root * 0.044715 * square)
    pre_grad = low(hidden_grad * slope)
    out = jnp.dot(hidden, down_ref[0], preferred_element_type=jnp.float32)
    back = lax.dot_general(
        pre_grad, in_ref[0], ROWS_BY_ROWS, preferred_element_type=jnp.float32
    )
    if started:
        out = out + out_so_far[0]
        back = back + back_so_far[0]
    out_ref[0] = out.astype(out_ref.dtype)
    back_ref[0] = back.astype(back_ref.dtype)
    x_t[:, rows] = x.T
    hidden_t[:, rows] = hidden.T
    pre_grads[rows, :] = pre_grad

    @pl.when(step == pl.num_programs(1) - 1)
    def weight_grads():
        part = 256
        for at in range(0, hidden_t.shape[0], part):
            some = slice(at, min(at + part, hidden_t.shape[0]))
            down_grad_ref[0, some, :] = low(
                jnp.dot(hidden_t[some, :], g_ref[0], preferred_element_type=jnp.float32)
            )
        for at in range(0, x_t.shape[0], part):
            some = slice(at, min(at + part, x_t.shape[0]))
            in_grad_ref[0, some, :] = low(
                jnp.dot(x_t[some, :], pre_grads[...], preferred_element_type=jnp.float32)
            )


def expert_slice(x, g, w_in, w_out, so_far, is_last):
    local, n_rows, width = x.shape
    inner = w_in.shape[2]
    tile = min(n_rows, 1024)
    whole = pl.BlockSpec((1, n_rows, width), lambda e, i: (e, 0, 0))
    up = pl.BlockSpec((1, width, inner), lambda e, i: (e, 0, 0))
    down = pl.BlockSpec((1, inner, width), lambda e, i: (e, 0, 0))
    some = pl.BlockSpec((1, tile, width), lambda e, i: (e, i, 0))
    started = so_far is not None
    kind = jnp.bfloat16 if is_last else jnp.float32
    totals = tuple(so_far) if started else ()
    return pl.pallas_call(
        functools.partial(expert_kernel, tile, started),
        grid=(local, n_rows // tile),
        in_specs=[whole, whole, up, down] + [some] * len(totals),
        out_specs=[some, some, up, down],
        out_shape=[
            jax.ShapeDtypeStruct(x.shape, kind),
            jax.ShapeDtypeStruct(x.shape, kind),
            jax.ShapeDtypeStruct(w_in.shape, jnp.bfloat16),
            jax.ShapeDtypeStruct(w_out.shape, jnp.bfloat16),
        ],
        input_output_aliases={4: 0, 5: 1} if started and not is_last else {},
        scratch_shapes=[
            pltpu.VMEM((width, n_rows), jnp.bfloat16),
            pltpu.VMEM((inner, n_rows), jnp.bfloat16),
            pltpu.VMEM((n_rows, inner), jnp.bfloat16),
        ],
        compiler_params=pltpu.CompilerParams(vmem_limit_bytes=VMEM_LIMIT),
        cost_estimate=SHORT,
        name="expert_slice",
    )(x, g, w_in, w_out, *totals)


def body(
    tokens,
    cotangent,
    qkv_weight,
    out_weight,
    norm_gains,
    rel_bias,
    router_weight,
    w_in,
    w_out,
    doc_lengths,
    bucket_ids,
    routes,
):
    n_batch, n_span, n_width = tokens.shape
    n_rows = n_batch * n_span
    n_buckets, n_heads = rel_bias.shape
    n_inner = qkv_weight.shape[2]
    groups = lax.axis_size("expert")
    local_experts = w_in.shape[0]
    experts_all = local_experts * groups
    n_slots = max(2, 2 * n_span * 2 // experts_all)
    dp_places = dp_order()
    place = lax.axis_index("dp")
    n_dp = len(dp_places)
    offsets = [(place - piece) * n_span for piece in dp_places]
    extra = experts_all + 2
    lanes = -(-extra // 128) * 128
    route_rows = -(-2 * n_rows // n_width // 16) * 16
    packed = jnp.concatenate(
        [qkv_weight[0], qkv_weight[1], qkv_weight[2], out_weight]
        + [router_weight, norm_gains.T, jnp.zeros((out_weight.shape[0], lanes - extra), jnp.bfloat16)],
        axis=1,
    )
    token_pieces = dp_gather(tokens)
    full, full_plane, full_last = gather_all(packed)
    ahead = (*token_pieces[1:3], *full_plane) if by_steps() else ()
    in_pieces, down_pieces, near_in, near_down = dp_gather_pair(w_in, w_out, ahead)
    weights = [full[:, c * n_inner : (c + 1) * n_inner] for c in range(4)]
    router = full[:, 4 * n_inner : 4 * n_inner + experts_all]
    router_t = router.T
    gains = wide(full[:, 4 * n_inner + experts_all : 4 * n_inner + extra].T)
    route_values = low(routes.reshape(n_batch, n_span, 2).transpose(0, 2, 1)).reshape(-1)
    route_values = jnp.pad(route_values, (0, route_rows * n_width - 2 * n_rows))
    grad_rows = jnp.concatenate(
        [cotangent.reshape(n_rows, n_width), route_values.reshape(route_rows, n_width)]
    )
    grad_all, grad_steps = expert_gather(after(grad_rows, *full_last))
    routes_all = grad_all[:, n_rows:].reshape(groups, -1)[:, : 2 * n_rows]
    routes_all = routes_all.astype(jnp.int32).reshape(groups * n_batch, 2, n_span)
    first = lax.axis_index("expert").astype(jnp.int32) * local_experts
    mine = first + jnp.arange(local_experts, dtype=jnp.int32)
    member = jnp.any(routes_all[:, None] == mine[None, :, None, None], axis=2)
    before = wide(jnp.arange(n_span)[:, None] < jnp.arange(n_span)[None, :])
    ranks = jnp.einsum(
        "bet,tu->beu", low(member), low(before), preferred_element_type=jnp.float32
    ).astype(jnp.int32)
    slots = jnp.where(member, ranks, -1)
    first = first[None]

    base = bias_base(rel_bias, bucket_ids, offsets, n_span)
    begin = document_starts(doc_lengths, place * n_span, n_span)
    starts = jnp.stack([begin - piece * n_span for piece in dp_places], axis=1)

    normed1_all = jnp.stack(
        [low(norm_forward(wide(piece), gains[0])[0]) for piece in token_pieces], axis=1
    )
    normed1_all = normed1_all.reshape(n_batch, n_dp * n_span, n_width)
    flat_normed1 = normed1_all.reshape(-1, n_width)
    normed1 = normed1_all[:, :n_span] if by_steps() else lax.dynamic_slice_in_dim(
        normed1_all, place * n_span, n_span, 1
    )
    normed1 = normed1.reshape(n_rows, n_width)
    queries = low(low(jnp.dot(normed1, weights[0], preferred_element_type=jnp.float32)) * SCALE)
    queries = queries.reshape(n_batch, n_span, n_inner)
    keys, values = (
        low(jnp.dot(flat_normed1, weights[c], preferred_element_type=jnp.float32)).reshape(
            n_batch, -1, n_inner
        )
        for c in (1, 2)
    )
    attended_rows, log_total = attention_forward(
        queries, keys, values, base, starts, n_heads, (*near_in, *grad_steps[1:3])
    )
    attended = attended_rows.reshape(n_rows, n_inner)
    inputs = wide(tokens.reshape(n_rows, n_width))
    resid = inputs + jnp.dot(attended, weights[3], preferred_element_type=jnp.float32)
    normed2, inverse2 = norm_forward(resid, gains[1])
    normed2_low = low(normed2).reshape(n_batch, n_span, n_width)
    normed2_low = after(normed2_low, *grad_steps[3:])
    far_pieces = (in_pieces[3], down_pieces[3]) if by_steps() else ()
    token_all = expert_gather(normed2_low, near_down, far_pieces)[0]
    token_all = token_all.reshape(groups * n_batch, n_span, n_width)
    expert_in, expert_up, expert_kept, gates = dispatch(
        token_all,
        grad_all,
        router_t,
        routes_all,
        slots,
        first,
        n_slots,
        (*in_pieces[1:], *down_pieces[1:]),
    )
    so_far = None
    in_grads, down_grads = {}, {}
    for r in (*range(n_dp - 1, 3, -1), 3, 1, 2, 0):
        *so_far, in_grads[r], down_grads[r] = expert_slice(
            expert_in, expert_up, in_pieces[r], down_pieces[r], so_far, r == 0
        )
    in_grads, down_grads = ([grads[r] for r in range(n_dp)] for grads in (in_grads, down_grads))
    piece_shape = (groups // 2, n_batch, n_span, n_width)
    received = dp_scatter_pair(in_grads, down_grads)
    in_share, down_share, last = dp_scatter_pair_end(in_grads, down_grads, received)
    mixed_kept, mixed_given, back_kept, back_given, router_grad = combine(
        expert_in,
        expert_kept,
        gates,
        router,
        routes_all,
        slots,
        first,
        *so_far,
        n_slots,
        received[:2] if last else (),
    )
    back_other = swap_cores(back_given.reshape(piece_shape), received[2:] if last else ())
    normed2_grad, back_corner, _ = expert_scatter(back_kept.reshape(piece_shape), back_other)
    normed2_grad = normed2_grad.reshape(n_rows, n_width)
    mixed_other = swap_cores(mixed_given.reshape(piece_shape), (back_corner,))
    gain2_grad = jnp.sum(normed2_grad * resid * inverse2, axis=0)
    grad_out = wide(cotangent.reshape(n_rows, n_width))
    resid_grad = grad_out + norm_backward(resid, inverse2, gains[1], normed2_grad)
    branch_low = low(resid_grad)
    attended_grad = low(
        lax.dot_general(branch_low, weights[3], ROWS_BY_ROWS, preferred_element_type=jnp.float32)
    )
    query_grad, key_grad, value_grad, dist_grad = attention_backward(
        queries,
        keys,
        values,
        attended_rows,
        attended_grad.reshape(n_batch, n_span, n_inner),
        base,
        starts,
        log_total,
        n_heads,
        (*last, mixed_other),
    )
    bias_grad = bias_fold(dist_grad, bucket_ids, offsets, n_buckets)
    mixed, mixed_corner, mixed_last = expert_scatter(
        mixed_kept.reshape(piece_shape), mixed_other, (dist_grad,), (dist_grad,)
    )
    block_out = low(resid + mixed.reshape(n_rows, n_width)).reshape(n_batch, n_span, n_width)
    query_grad = query_grad.reshape(n_rows, n_inner)
    key_grad = key_grad.reshape(-1, n_inner)
    value_grad = value_grad.reshape(-1, n_inner)
    own_part = lax.dot_general(
        query_grad, weights[0], ROWS_BY_ROWS, preferred_element_type=jnp.float32
    )
    all_part = lax.dot_general(
        key_grad, weights[1], ROWS_BY_ROWS, preferred_element_type=jnp.float32
    ) + lax.dot_general(value_grad, weights[2], ROWS_BY_ROWS, preferred_element_type=jnp.float32)
    all_part = all_part.reshape(n_batch, n_dp, n_span, n_width)
    sent = low(all_part)
    shared = dp_scatter([sent[:, r] for r in range(n_dp)])
    normed1_grad = own_part + shared.reshape(n_rows, n_width)
    inverse1 = lax.rsqrt(jnp.mean(inputs * inputs, axis=-1, keepdims=True) + EPS)
    tokens_grad = resid_grad + norm_backward(inputs, inverse1, gains[0], normed1_grad)
    def rows_grad(rows, grads):
        return low(
            lax.dot_general(rows, grads, COLS_BY_COLS, preferred_element_type=jnp.float32)
        )

    weight_grads = jnp.stack(
        [
            rows_grad(normed1, query_grad),
            rows_grad(flat_normed1, key_grad),
            rows_grad(flat_normed1, value_grad),
            rows_grad(attended, branch_low),
        ]
    )
    weight_grads = after(weight_grads, mixed_corner)
    gain1_grad = (
        sum(jnp.sum(wide(weight_grads[c]) * wide(weights[c]), axis=1) for c in range(3)) / gains[0]
    )
    shares = scatter_all(weight_grads, mixed_last)
    small_rows = experts_all + 2
    bias_flat = jnp.pad(bias_grad.reshape(1, -1), ((0, 0), (0, n_width - bias_grad.size)))
    small = sum_all(
        jnp.concatenate([router_grad, gain1_grad[None], gain2_grad[None], bias_flat])
    )
    rel_bias_grad = small[small_rows, : bias_grad.size].reshape(bias_grad.shape)
    n_own = router_weight.shape[0]
    own = lax.dynamic_slice_in_dim(
        small, (place * groups + lax.axis_index("expert")) * n_own, n_own, 1
    )
    router_share = own[:experts_all].T
    gains_share = own[experts_all:small_rows]
    qkv_share, out_share = shares[:3], shares[3]
    return (
        block_out,
        tokens_grad.reshape(n_batch, n_span, n_width),
        qkv_share,
        out_share,
        gains_share,
        rel_bias_grad,
        router_share,
        in_share,
        down_share,
    )


def solution(mesh):
    return jax.shard_map(
        body,
        mesh=mesh,
        in_specs=(
            P("expert", "dp", None),
            P("expert", "dp", None),
            P(None, ("dp", "expert"), None),
            P(("dp", "expert"), None),
            P(None, ("dp", "expert")),
            P(),
            P(("dp", "expert"), None),
            P("expert", None, "dp"),
            P("expert", "dp", None),
            P("expert", None),
            P(),
            P("expert", "dp", None),
        ),
        out_specs=(
            P("expert", "dp", None),
            P("expert", "dp", None),
            P(None, ("dp", "expert"), None),
            P(("dp", "expert"), None),
            P(None, ("dp", "expert")),
            P(),
            P(("dp", "expert"), None),
            P("expert", None, "dp"),
            P("expert", "dp", None),
        ),
        check_vma=False,
    )
```
